32 devices in a mesh: tile: 16 (over z, y, core), depth: 2 (over x).
Axes of the slice: x: 2, y: 2, z: 4, core: 2. Of those that a mesh axis runs over, the one named last changes fastest.
Arguments:
- objects: float32 [2, 4, 2048, 256], P('depth', None, 'tile'), may hold values from 0.25 to 30, as said below
- observed: float32 [2, 4, 2048, 256], P('depth', None, 'tile'), may hold values from 0.25 to 30, as said below
- pupil_phase: float32 [2, 128, 128], P('depth'), may hold values from -319 to 319
- pupil_amplitude: float32 [2, 128, 128], P('depth'), may hold values from 0.25 to 1.75
Outputs:
- new_objects: float32 [2, 4, 2048, 256], P('depth', None, 'tile')
- new_phase: float32 [2, 128, 128], P('depth')
The draws below stay inside these ranges and needn't reach their ends.
Inputs may be any that keep to these rules, and one draw needn't show every extreme that they name: `objects`: strictly positive intensities. `observed`: strictly positive intensities.
All inputs are finite; a program needn't handle non-finite values.
Results may differ from the reference program's by a relative error of at most 0.0001.
Values sent between devices are 32-bit elements; how exact they have to be, the bound alone decides.
No kernel may reach another device: no remote copies, remote signals or barrier semaphores. Data moves between devices by JAX's collectives and lax.ppermute only.
A program may use at most 64 MiB of HBM per device.

```python
import math
import jax
import jax.numpy as jnp
from jax import lax

COLS = 256
PLANES = 4
HALF = 64
PUP = 128
KER = 129
NROWS = 2048
STRATA = 2


def spread_box(field, width):
    reach = width // 2
    rows_summed = field
    for offset in range(1, reach + 1):
        rows_summed = rows_summed + jnp.roll(field, offset, 2) + jnp.roll(field, -offset, 2)
    both_summed = rows_summed
    for offset in range(1, reach + 1):
        both_summed = both_summed + jnp.roll(rows_summed, offset, 3) + jnp.roll(rows_summed, -offset, 3)
    return both_summed


def bright_cells(key):
    full_shape = (STRATA, PLANES, NROWS, COLS)
    place_key, level_key = jax.random.split(jax.random.fold_in(key, 11))
    placed = jax.random.uniform(place_key, full_shape, jnp.float32, 0.0, 1.0) < 0.01
    levels = jnp.exp(jax.random.uniform(level_key, full_shape, jnp.float32, math.log(3.0), math.log(12.0)))
    return jnp.where(placed, levels, 0.0)


def draw_background(key, salt_value):
    base_key = jax.random.fold_in(jax.random.fold_in(key, salt_value), 0)
    full_shape = (STRATA, PLANES, NROWS, COLS)
    position = jnp.arange(NROWS, dtype=jnp.float32) / max(NROWS - 1, 1)
    depth_fraction = jnp.arange(STRATA, dtype=jnp.float32) / max(STRATA - 1, 1)
    depth_ramp = (1.0 + 2.0 * depth_fraction)[:, None, None, None]
    base_level = jnp.exp(jax.random.uniform(base_key, full_shape, jnp.float32, math.log(0.5), math.log(2.0)))
    row_ramp = (1.0 + 2.0 * position)[None, None, :, None]
    return base_level * row_ramp * depth_ramp


def draw_objects(key, part):
    cells = spread_box(bright_cells(key), 3)
    return jnp.minimum(draw_background(key, 3) + cells, 30.0)


def draw_observed(key, part):
    cells = spread_box(bright_cells(key), 5)
    return jnp.minimum(draw_background(key, 7) + 0.5 * cells, 30.0)


def draw_pupil_phase(key, part):
    keys = jax.random.split(jax.random.fold_in(key, 5), 5)
    positions = (jnp.arange(PUP, dtype=jnp.float32) - (PUP - 1) / 2.0) / (PUP / 2.0)
    across = positions[None, :, None]
    along = positions[None, None, :]
    tilt_most = 0.5 * math.pi * HALF * PUP / KER
    focus_most = math.pi * HALF * PUP / (8.0 * KER)
    coeff_shape = (STRATA, 1, 1)
    tilts = tilt_most * jax.random.uniform(keys[0], (2, STRATA, 1, 1), jnp.float32, -1.0, 1.0)
    rough = jnp.clip(0.3 * jax.random.normal(keys[4], (STRATA, PUP, PUP), jnp.float32), -1.2, 1.2)
    focus = focus_most * jax.random.uniform(keys[2], coeff_shape, jnp.float32, -1.0, 1.0) ** 3
    astig = 0.5 * focus_most * jax.random.uniform(keys[3], coeff_shape, jnp.float32, -1.0, 1.0) ** 3
    smooth = tilts[0] * across + tilts[1] * along
    smooth = smooth + focus * (across ** 2 + along ** 2) + astig * (across ** 2 - along ** 2)
    return smooth + rough


def setup_inputs(seed: int = 0) -> dict:
    streams_of = jax.random.split(jax.random.key(seed), 5)
    return {
        "objects": draw_objects(jax.random.fold_in(streams_of[4], 71), 0),
        "observed": draw_observed(jax.random.fold_in(streams_of[4], 71), 0),
        "pupil_phase": draw_pupil_phase(jax.random.fold_in(streams_of[4], 71), 0),
        "pupil_amplitude": jnp.clip(1.0 + 0.15 * jax.random.normal(streams_of[3], (STRATA, PUP, PUP), jnp.float32), 0.25, 1.75),
    }


HIGHEST_PRECISION = lax.Precision.HIGHEST
BACKGROUND = 0.1
STEP_SIZE = 0.3
EPSILON = 1e-06

def twiddle(out_index, in_index, length, flip_sign):
    product = out_index[:, None] * in_index[None, :] % length
    radians = product.astype(jnp.float32) * (2.0 * math.pi / length)
    return (jnp.cos(radians), flip_sign * jnp.sin(radians))

def matmul(left, right):
    return jnp.dot(left, right, precision=HIGHEST_PRECISION)

def point_spread(pupil_angle, amplitude_map):
    pupil_size = pupil_angle.shape[0]
    kernel_size = 2 * HALF + 1
    positions = jnp.arange(pupil_size, dtype=jnp.int32)
    centre = (pupil_size - 1) / 2.0
    offsets = positions.astype(jnp.float32) - centre
    distance = offsets[:, None] ** 2 + offsets[None, :] ** 2
    aperture = (distance <= (pupil_size / 2.0) ** 2).astype(jnp.float32)
    field_real = amplitude_map * aperture * jnp.cos(pupil_angle)
    field_imag = amplitude_map * aperture * jnp.sin(pupil_angle)
    lags = (jnp.arange(kernel_size, dtype=jnp.int32) - HALF) % kernel_size
    fourier_real, fourier_imag = twiddle(lags, positions, kernel_size, -1.0)
    left_real = matmul(fourier_real, field_real) - matmul(fourier_imag, field_imag)
    left_imag = matmul(fourier_real, field_imag) + matmul(fourier_imag, field_real)
    outer_real = matmul(left_real, fourier_real.T) - matmul(left_imag, fourier_imag.T)
    outer_imag = matmul(left_real, fourier_imag.T) + matmul(left_imag, fourier_real.T)
    intensity = outer_real ** 2 + outer_imag ** 2
    return intensity / jnp.sum(intensity)

def full_kernel(kernel):
    padded = jnp.zeros((NROWS, COLS), kernel.dtype).at[:KER, :KER].set(kernel)
    return jnp.fft.fft2(jnp.roll(padded, (-HALF, -HALF), (0, 1)))

def reference(objects, observed, pupil_phase, pupil_amplitude):
    gradients = []
    for stratum in range(STRATA):
        picture = objects[stratum]
        measured = observed[stratum]
        amplitude_map = pupil_amplitude[stratum]
        first_kernel, pullback = jax.vjp(lambda trial: point_spread(trial, amplitude_map), pupil_phase[stratum])
        object_spectrum = jnp.fft.fft2(picture)
        first_blur = jnp.real(jnp.fft.ifft2(object_spectrum * full_kernel(first_kernel))) + BACKGROUND
        misfit = 1.0 - measured / first_blur
        lagged = lax.optimization_barrier(jnp.sum(jnp.real(jnp.fft.ifft2(jnp.fft.fft2(misfit) * jnp.conj(object_spectrum))), axis=0))
        psf_grad = jnp.roll(lagged, (HALF, HALF), (0, 1))[:KER, :KER]
        gradients.append(pullback(psf_grad)[0])
    grand_total = jnp.float32(0.0)
    for stratum in range(STRATA):
        grand_total = grand_total + jnp.sum(gradients[stratum] * gradients[stratum])
    mean_square = grand_total / (STRATA * PUP * PUP)
    new_objects = []
    new_phases = []
    for stratum in range(STRATA):
        picture = objects[stratum]
        measured = observed[stratum]
        updated = pupil_phase[stratum] - STEP_SIZE * gradients[stratum] / jnp.sqrt(mean_square + EPSILON)
        second_kernel = point_spread(updated, pupil_amplitude[stratum])
        kernel_spec = full_kernel(second_kernel)
        second_blur = jnp.real(jnp.fft.ifft2(jnp.fft.fft2(picture) * kernel_spec)) + BACKGROUND
        ratio_field = measured / second_blur
        correction = jnp.real(jnp.fft.ifft2(jnp.fft.fft2(ratio_field) * jnp.conj(kernel_spec)))
        new_objects.append(picture * correction)
        new_phases.append(updated)
    return (jnp.stack(new_objects), jnp.stack(new_phases))
```

```python
import functools
import math

import jax
import jax.numpy as jnp
import ml_dtypes
import numpy as np
from jax import lax
from jax.experimental import pallas as pl
from jax.experimental.pallas import tpu as pltpu
from jax.sharding import PartitionSpec as P

HALF = 64
BACKGROUND = 0.1
STEP_SIZE = 0.3
EPSILON = 1e-06
VMEM_LIMIT = 32 * 1024 * 1024


def round_up(value, step):
    return -(-value // step) * step


def angles(left, right, length):
    return (2.0 * math.pi / length) * np.outer(left, right)


def halves(matrix):
    high = matrix.astype(np.float32).astype(ml_dtypes.bfloat16)
    low = (matrix - high.astype(np.float64)).astype(np.float32).astype(ml_dtypes.bfloat16)
    return np.stack([high, low])


def row_constants(rows, length):
    freqs = np.arange(length // 2) + 0.5
    theta = angles(freqs, np.arange(length), length)
    forward = np.concatenate([np.cos(theta), -np.sin(theta)], 0)
    inner = theta[:, HALF : HALF + rows]
    inverse = np.concatenate([np.cos(inner).T, -np.sin(inner).T], 1) * (2.0 / length)
    return forward, inverse


def col_constants(cols):
    half = cols // 2
    forward, inverse = [], []
    for parity in range(2):
        theta = angles(np.arange(half), 2 * np.arange(half) + parity, cols)
        c, s = np.cos(theta), np.sin(theta)
        forward.append(np.block([[c, -s], [s, c]]))
        inverse.append(np.block([[c.T, s.T], [-s.T, c.T]]) / cols)
    return np.stack(forward), np.stack(inverse)


def kernel_constants(length, cols, ker, pad_rows, pad_cols):
    lags = np.arange(ker) - HALF
    theta = angles(np.arange(length // 2) + 0.5, lags, length)
    rows = np.zeros((length, pad_rows))
    rows[: length // 2, :ker] = np.cos(theta)
    rows[length // 2 :, :ker] = -np.sin(theta)
    half = cols // 2
    right = np.zeros((2 * pad_cols, 2 * cols))
    for parity in range(2):
        theta = angles(lags, 2 * np.arange(half) + parity, cols)
        c, s = np.cos(theta), np.sin(theta)
        at = parity * cols
        right[:ker, at : at + half] = c
        right[:ker, at + half : at + cols] = -s
        right[pad_cols : pad_cols + ker, at : at + half] = s
        right[pad_cols : pad_cols + ker, at + half : at + cols] = c
    return rows, right


def pupil_constants(pup, ker, pad_rows, pad_cols):
    theta = angles(np.arange(ker) - HALF, np.arange(pup), ker)
    real, imag = np.cos(theta), -np.sin(theta)
    right = np.zeros((2 * pup, 2 * pad_cols))
    right[:pup, :ker] = real.T
    right[:pup, pad_cols : pad_cols + ker] = imag.T
    right[pup:, :ker] = -imag.T
    right[pup:, pad_cols : pad_cols + ker] = real.T
    left = np.zeros((2 * pad_rows, 2 * pup))
    left[:ker, :pup] = real
    left[:ker, pup:] = -imag
    left[pad_rows : pad_rows + ker, :pup] = imag
    left[pad_rows : pad_rows + ker, pup:] = real
    return left, right


def aperture_of(pup):
    offsets = np.arange(pup) - (pup - 1) / 2.0
    distance = offsets[:, None] ** 2 + offsets[None, :] ** 2
    return (distance <= (pup / 2.0) ** 2).astype(np.float32)


def dot(left, right):
    return jnp.dot(left, right, preferred_element_type=jnp.float32)


def split(value):
    high = value.astype(jnp.bfloat16)
    low = (value - high.astype(jnp.float32)).astype(jnp.bfloat16)
    return high, low


def left_by(const, value):
    high, low = split(value)
    return dot(const[0], high) + (dot(const[1], high) + dot(const[0], low))


def right_by(value, const):
    high, low = split(value)
    return dot(high, const[0]) + (dot(low, const[0]) + dot(high, const[1]))


def sine_cosine(angle):
    turns = jnp.floor(angle * (2.0 / math.pi) + 0.5)
    rest = angle - turns * 1.5703125
    rest = rest - turns * 4.837512969970703e-4
    rest = rest - turns * 7.54978995489e-8
    square = rest * rest
    sine = rest + rest * square * (
        -1.6666654611e-1 + square * (8.3321608736e-3 + square * -1.9515295891e-4)
    )
    cosine = 1.0 - 0.5 * square + square * square * (
        4.166664568298827e-2 + square * (-1.388731625493765e-3 + square * 2.443315711809948e-5)
    )
    quadrant = turns.astype(jnp.int32) & 3
    swap = (quadrant & 1) == 1
    sine_out = jnp.where(swap, cosine, sine)
    cosine_out = jnp.where(swap, sine, cosine)
    sine_out = jnp.where(quadrant >= 2, -sine_out, sine_out)
    cosine_out = jnp.where((quadrant == 1) | (quadrant == 2), -cosine_out, cosine_out)
    return sine_out, cosine_out


def total(value):
    return jnp.sum(jnp.sum(value, axis=0, keepdims=True), axis=1, keepdims=True)


def point_spread(phase, weight, pupil_left, pupil_right):
    sine, cosine = sine_cosine(phase)
    pupil = jnp.concatenate([weight * cosine, weight * sine], 1)
    across = right_by(pupil, pupil_right)
    cols = across.shape[1] // 2
    field = left_by(pupil_left, jnp.concatenate([across[:, :cols], across[:, cols:]], 0))
    rows = field.shape[0] // 2
    intensity = field[:rows] * field[:rows] + field[rows:] * field[rows:]
    norm = 1.0 / total(intensity)
    root = jnp.sqrt(norm)
    return pupil * root, field * root, intensity * norm


def kernel_spectrum(psf, kernel_rows, kernel_right):
    left = left_by(kernel_rows, psf)
    freqs = left.shape[0] // 2
    return right_by(jnp.concatenate([left[:freqs], left[freqs:]], 1), kernel_right)


def forward(strips, row_matrix, col_matrix):
    sums, differences = [], []
    for strip in strips:
        half = strip.shape[1] // 2
        first, second = strip[:, :half], strip[:, half:]
        mixed = left_by(row_matrix, jnp.concatenate([first + second, first - second], 1))
        freqs = mixed.shape[0] // 2
        sums.append(jnp.concatenate([mixed[:freqs, :half], mixed[freqs:, :half]], 1))
        differences.append(jnp.concatenate([mixed[:freqs, half:], mixed[freqs:, half:]], 1))
    return (
        right_by(jnp.concatenate(sums, 0), col_matrix[0]),
        right_by(jnp.concatenate(differences, 0), col_matrix[1]),
    )


def inverse(spectrum, planes, row_matrix, col_matrix):
    even = right_by(spectrum[0], col_matrix[0])
    odd = right_by(spectrum[1], col_matrix[1])
    freqs = even.shape[0] // planes
    half = even.shape[1] // 2
    strips = []
    for plane in range(planes):
        rows = slice(plane * freqs, (plane + 1) * freqs)
        stacked = jnp.concatenate(
            [
                jnp.concatenate([even[rows, :half], odd[rows, :half]], 1),
                jnp.concatenate([even[rows, half:], odd[rows, half:]], 1),
            ],
            0,
        )
        mixed = left_by(row_matrix, stacked)
        first, second = mixed[:, :half], mixed[:, half:]
        strips.append(jnp.concatenate([first + second, first - second], 1))
    return strips


def times(spectrum, other, planes, conjugate):
    half = other.shape[1] // 2
    real = jnp.concatenate([other[:, :half]] * planes, 0)
    imag = jnp.concatenate([other[:, half:]] * planes, 0)
    left, right = spectrum[:, :half], spectrum[:, half:]
    if conjugate:
        return jnp.concatenate([left * real + right * imag, right * real - left * imag], 1)
    return jnp.concatenate([left * real - right * imag, left * imag + right * real], 1)


def cross(first, second, planes):
    half = first.shape[1] // 2
    freqs = first.shape[0] // planes
    left, right = first[:, :half], first[:, half:]
    real, imag = second[:, :half], second[:, half:]
    both = jnp.concatenate([left * real + right * imag, right * real - left * imag], 1)
    summed = both[:freqs]
    for plane in range(1, planes):
        summed = summed + both[plane * freqs : (plane + 1) * freqs]
    return summed


def first_kernel(phase, weight, pupil_left, pupil_right, kernel_rows, kernel_right, pupil_out, field_out, spec_out):
    pupil, field, psf = point_spread(phase[...], weight[...], pupil_left, pupil_right)
    pupil_out[...] = pupil
    field_out[...] = field
    spec_out[...] = kernel_spectrum(psf, kernel_rows, kernel_right)


def gradient_kernel(
    before, own, after, observed, spec, pupil, field,
    row_forward, row_own, row_inverse, col_forward, col_inverse,
    lag_right, lag_left, adjoint_left, adjoint_right, gradient_out,
):
    planes = own.shape[0]
    cols = own.shape[2]
    strips = [jnp.concatenate([before[p], own[p], after[p]], 0) for p in range(planes)]
    even, odd = forward(strips, row_forward, col_forward)
    blurred = inverse(
        (times(even, spec[:, :cols], planes, False), times(odd, spec[:, cols:], planes, False)),
        planes, row_inverse, col_inverse,
    )
    misfit = [1.0 - observed[p] / (blurred[p] + BACKGROUND) for p in range(planes)]
    misfit_even, misfit_odd = forward(misfit, row_own, col_forward)
    shared = jnp.concatenate([cross(misfit_even, even, planes), cross(misfit_odd, odd, planes)], 1)
    across = right_by(shared, lag_right)
    pad_cols = across.shape[1] // 2
    psf_grad = left_by(lag_left, jnp.concatenate([across[:, :pad_cols], across[:, pad_cols:]], 0))
    far = field[...]
    pad_rows = far.shape[0] // 2
    real, imag = far[:pad_rows], far[pad_rows:]
    centred = 2.0 * (psf_grad - total(psf_grad * (real * real + imag * imag)))
    back = left_by(adjoint_left, jnp.concatenate([centred * real, centred * imag], 0))
    pup = back.shape[0] // 2
    back = right_by(jnp.concatenate([back[:pup], back[pup:]], 1), adjoint_right)
    near = pupil[...]
    gradient_out[...] = back[:, pup:] * near[:, :pup] - back[:, :pup] * near[:, pup:]


def blocks_kernel(before, own, after, row_forward, col_forward, even_out, odd_out):
    planes = own.shape[0]
    strips = [jnp.concatenate([before[p], own[p]], 0) for p in range(planes)]
    strips += [jnp.concatenate([own[p], after[p]], 0) for p in range(planes)]
    even, odd = forward(strips, row_forward, col_forward)
    even_out[...] = even
    odd_out[...] = odd


def second_kernel(
    phase, weight, gradient, squares, even, odd, own, before, observed, after,
    pupil_left, pupil_right, kernel_rows, kernel_right,
    row_forward, row_inverse, col_forward, col_inverse, objects_out, phase_out, *, cells,
):
    planes, rows, cols = own.shape
    slope = gradient[...]
    mean_square = squares[...] * (1.0 / cells)
    updated = phase[...] - STEP_SIZE * slope / jnp.sqrt(mean_square + EPSILON)
    phase_out[...] = updated
    _, _, psf = point_spread(updated, weight[...], pupil_left, pupil_right)
    spec = kernel_spectrum(psf, kernel_rows, kernel_right)
    spec_even, spec_odd = spec[:, :cols], spec[:, cols:]
    blurred = inverse(
        (times(even[...], spec_even, 2 * planes, False), times(odd[...], spec_odd, 2 * planes, False)),
        2 * planes, row_inverse, col_inverse,
    )
    ratios = []
    for p in range(planes):
        light = jnp.concatenate([blurred[p], blurred[planes + p]], 0) + BACKGROUND
        ratios.append(jnp.concatenate([before[p], observed[p], after[p]], 0) / light)
    ratio_even, ratio_odd = forward(ratios, row_forward, col_forward)
    correction = inverse(
        (times(ratio_even, spec_even, planes, True), times(ratio_odd, spec_odd, planes, True)),
        planes, row_inverse, col_inverse,
    )
    for p in range(planes):
        objects_out[p] = own[p] * correction[p]


def call(kernel, out_shapes, args):
    outs = [jax.ShapeDtypeStruct(shape, jnp.float32) for shape in out_shapes]
    return pl.pallas_call(
        kernel,
        out_shape=outs,
        in_specs=[pl.BlockSpec(memory_space=pltpu.VMEM)] * len(args),
        out_specs=[pl.BlockSpec(memory_space=pltpu.VMEM)] * len(outs),
        compiler_params=pltpu.CompilerParams(vmem_limit_bytes=VMEM_LIMIT),
        cost_estimate=pl.CostEstimate(flops=4 * 10**9, bytes_accessed=4 * 10**6, transcendentals=0),
    )(*args)


def from_neighbours(last, first):
    count = lax.axis_size("tile")
    up = [(i, (i + 1) % count) for i in range(count)]
    down = [(j, i) for i, j in up]
    return lax.ppermute(last, "tile", up), lax.ppermute(first, "tile", down)


def sum_over(value, axis):
    count = lax.axis_size(axis)
    if count & (count - 1):
        return lax.psum(value, axis)
    step = 1
    while step < count:
        value = value + lax.ppermute(value, axis, [(i, i ^ step) for i in range(count)])
        step *= 2
    return value


def on_device(objects, observed, pupil_phase, pupil_amplitude):
    picture, measured, phase = objects[0], observed[0], pupil_phase[0]
    planes, rows, cols = picture.shape
    pup = phase.shape[0]
    ker = 2 * HALF + 1
    length = rows + 2 * HALF
    pad_rows, pad_cols = round_up(ker, 16), round_up(ker, 128)
    row_forward, row_inverse = row_constants(rows, length)
    col_forward, col_inverse = col_constants(cols)
    kernel_rows, kernel_right = kernel_constants(length, cols, ker, pad_rows, pad_cols)
    pupil_left, pupil_right = pupil_constants(pup, ker, pad_rows, pad_cols)
    row_own = row_forward[:, HALF : HALF + rows]
    lag_right = kernel_right.T / cols
    lag_left = kernel_rows.T * (2.0 / length)
    adjoint_left, adjoint_right = pupil_left.T, pupil_right.T

    def pair(matrix):
        return jnp.asarray(halves(matrix))

    def pairs(matrices):
        return jnp.asarray(np.stack([halves(matrix) for matrix in matrices]))

    weight = pupil_amplitude[0] * jnp.asarray(aperture_of(pup))
    before, after = from_neighbours(picture[:, rows - HALF :], picture[:, :HALF])
    far_before, far_after = from_neighbours(
        jnp.concatenate([picture[:, rows - 2 * HALF : rows - HALF], measured[:, rows - HALF :]], 0),
        jnp.concatenate([picture[:, HALF : 2 * HALF], measured[:, :HALF]], 0),
    )
    psf_constants = (pair(pupil_left), pair(pupil_right), pair(kernel_rows), pair(kernel_right))
    pupil, field, spec = call(
        first_kernel,
        [(pup, 2 * pup), (2 * pad_rows, pad_cols), (length // 2, 2 * cols)],
        (phase, weight, *psf_constants),
    )
    (gradient,) = call(
        gradient_kernel,
        [(pup, pup)],
        (
            before, picture, after, measured, spec, pupil, field,
            pair(row_forward), pair(row_own), pair(row_inverse), pairs(col_forward), pairs(col_inverse),
            pair(lag_right), pair(lag_left), pair(adjoint_left), pair(adjoint_right),
        ),
    )
    even, odd = call(
        blocks_kernel,
        [(planes * length, cols)] * 2,
        (
            jnp.concatenate([far_before[:planes], before], 1),
            picture,
            jnp.concatenate([after, far_after[:planes]], 1),
            pair(row_forward), pairs(col_forward),
        ),
    )
    gradient = sum_over(gradient, "tile")
    squares = sum_over(jnp.sum(gradient * gradient).reshape(1, 1), "depth")
    new_objects, new_phase = call(
        functools.partial(second_kernel, cells=lax.axis_size("depth") * pup * pup),
        [picture.shape, phase.shape],
        (
            phase, weight, gradient, squares, even, odd, picture,
            far_before[planes:], measured, far_after[planes:], *psf_constants,
            pair(row_forward), pair(row_inverse), pairs(col_forward), pairs(col_inverse),
        ),
    )
    return new_objects[None], new_phase[None]


def solution(mesh):
    return jax.shard_map(
        on_device,
        mesh=mesh,
        in_specs=(
            P("depth", None, "tile", None),
            P("depth", None, "tile", None),
            P("depth", None, None),
            P("depth", None, None),
        ),
        out_specs=(P("depth", None, "tile", None), P("depth", None, None)),
        check_vma=False,
    )
```

```python
import functools
import math

import jax
import jax.numpy as jnp
import ml_dtypes
import numpy as np
from jax import lax
from jax.experimental import pallas as pl
from jax.experimental.pallas import tpu as pltpu
from jax.sharding import PartitionSpec as P

HALF = 64
BACKGROUND = 0.1
STEP_SIZE = 0.3
EPSILON = 1e-06
VMEM_LIMIT = 32 * 1024 * 1024


def round_up(value, step):
    return -(-value // step) * step


def angles(left, right, length):
    return (2.0 * math.pi / length) * np.outer(left, right)


def halves(matrix):
    high = matrix.astype(np.float32).astype(ml_dtypes.bfloat16)
    low = (matrix - high.astype(np.float64)).astype(np.float32).astype(ml_dtypes.bfloat16)
    return high, low


def row_constants(rows, length):
    freqs = np.arange(length // 2) + 0.5
    theta = angles(freqs, np.arange(length), length)
    forward = np.concatenate([np.cos(theta), -np.sin(theta)], 0)
    inner = theta[:, HALF : HALF + rows]
    inverse = np.concatenate([np.cos(inner).T, -np.sin(inner).T], 1) * (2.0 / length)
    return forward, inverse


def col_constants(cols):
    half = cols // 2
    forward, inverse = [], []
    for parity in range(2):
        theta = angles(np.arange(half), 2 * np.arange(half) + parity, cols)
        c, s = np.cos(theta), np.sin(theta)
        forward.append(np.block([[c, -s], [s, c]]))
        inverse.append(np.block([[c.T, s.T], [-s.T, c.T]]) / cols)
    return forward, inverse


def kernel_constants(length, cols, ker, pad_rows, pad_cols):
    lags = np.arange(ker) - HALF
    theta = angles(np.arange(length // 2) + 0.5, lags, length)
    rows = np.zeros((length, pad_rows))
    rows[: length // 2, :ker] = np.cos(theta)
    rows[length // 2 :, :ker] = -np.sin(theta)
    half = cols // 2
    right = np.zeros((2 * pad_cols, 2 * cols))
    for parity in range(2):
        theta = angles(lags, 2 * np.arange(half) + parity, cols)
        c, s = np.cos(theta), np.sin(theta)
        at = parity * cols
        right[:ker, at : at + half] = c
        right[:ker, at + half : at + cols] = -s
        right[pad_cols : pad_cols + ker, at : at + half] = s
        right[pad_cols : pad_cols + ker, at + half : at + cols] = c
    return rows, right


def pupil_constants(pup, ker, pad_rows, pad_cols):
    theta = angles(np.arange(ker) - HALF, np.arange(pup), ker)
    real, imag = np.cos(theta), -np.sin(theta)
    right = np.zeros((2 * pup, 2 * pad_cols))
    right[:pup, :ker] = real.T
    right[:pup, pad_cols : pad_cols + ker] = imag.T
    right[pup:, :ker] = -imag.T
    right[pup:, pad_cols : pad_cols + ker] = real.T
    left = np.zeros((2 * pad_rows, 2 * pup))
    left[:ker, :pup] = real
    left[:ker, pup:] = -imag
    left[pad_rows : pad_rows + ker, :pup] = imag
    left[pad_rows : pad_rows + ker, pup:] = real
    return left, right


class Packed:
    def __init__(self, matrices, width):
        self.places, blocks, row = {}, [], 0
        for name, matrix in matrices.items():
            high, low = halves(matrix)
            rows, cols = matrix.shape
            beside = 2 * round_up(cols, 128) <= width
            block = np.zeros((round_up(rows, 16) * (1 if beside else 2), width), high.dtype)
            block[:rows, :cols] = high
            down, right = (0, width // 2) if beside else (round_up(rows, 16), 0)
            block[down : down + rows, right : right + cols] = low
            self.places[name] = (row, row + down, right, rows, cols)
            blocks.append(block)
            row += block.shape[0]
        self.array = np.concatenate(blocks)

    def at(self, ref):
        return {
            name: (ref.at[top : top + rows, :cols], ref.at[bottom : bottom + rows, right : right + cols])
            for name, (top, bottom, right, rows, cols) in self.places.items()
        }


def dot(left, right):
    return jnp.dot(left, right, preferred_element_type=jnp.float32)


def split(value):
    high = value.astype(jnp.bfloat16)
    low = (value - high.astype(jnp.float32)).astype(jnp.bfloat16)
    return high, low


def left_by(const, value):
    high, low = split(value)
    return dot(const[0][...], high) + (dot(const[1][...], high) + dot(const[0][...], low))


def right_by(value, const):
    high, low = split(value)
    return dot(high, const[0][...]) + (dot(low, const[0][...]) + dot(high, const[1][...]))


def sine_cosine(angle):
    turns = jnp.floor(angle * (2.0 / math.pi) + 0.5)
    rest = angle - turns * 1.5703125
    rest = rest - turns * 4.837512969970703e-4
    rest = rest - turns * 7.54978995489e-8
    square = rest * rest
    sine = rest + rest * square * (
        -1.6666654611e-1 + square * (8.3321608736e-3 + square * -1.9515295891e-4)
    )
    cosine = 1.0 - 0.5 * square + square * square * (
        4.166664568298827e-2 + square * (-1.388731625493765e-3 + square * 2.443315711809948e-5)
    )
    quadrant = turns.astype(jnp.int32) & 3
    swap = (quadrant & 1) == 1
    sine_out = jnp.where(swap, cosine, sine)
    cosine_out = jnp.where(swap, sine, cosine)
    sine_out = jnp.where(quadrant >= 2, -sine_out, sine_out)
    cosine_out = jnp.where((quadrant == 1) | (quadrant == 2), -cosine_out, cosine_out)
    return sine_out, cosine_out


def total(value):
    return jnp.sum(jnp.sum(value, axis=0, keepdims=True), axis=1, keepdims=True)


def weights(amplitude):
    pup = amplitude.shape[0]
    rows = lax.broadcasted_iota(jnp.int32, amplitude.shape, 0).astype(jnp.float32) - (pup - 1) / 2.0
    cols = lax.broadcasted_iota(jnp.int32, amplitude.shape, 1).astype(jnp.float32) - (pup - 1) / 2.0
    return jnp.where(rows * rows + cols * cols <= (pup / 2.0) ** 2, amplitude, 0.0)


def point_spread(phase, amplitude, const):
    weight = weights(amplitude)
    sine, cosine = sine_cosine(phase)
    pupil = jnp.concatenate([weight * cosine, weight * sine], 1)
    across = right_by(pupil, const["pupil_right"])
    cols = across.shape[1] // 2
    field = left_by(const["pupil_left"], jnp.concatenate([across[:, :cols], across[:, cols:]], 0))
    rows = field.shape[0] // 2
    intensity = field[:rows] * field[:rows] + field[rows:] * field[rows:]
    norm = 1.0 / total(intensity)
    root = jnp.sqrt(norm)
    return pupil * root, field * root, intensity * norm


def kernel_spectrum(psf, const):
    left = left_by(const["kernel_rows"], psf)
    freqs = left.shape[0] // 2
    return right_by(jnp.concatenate([left[:freqs], left[freqs:]], 1), const["kernel_right"])


def forward(strips, row_matrix, const):
    sums, differences = [], []
    for strip in strips:
        half = strip.shape[1] // 2
        first, second = strip[:, :half], strip[:, half:]
        mixed = left_by(row_matrix, jnp.concatenate([first + second, first - second], 1))
        freqs = mixed.shape[0] // 2
        sums.append(jnp.concatenate([mixed[:freqs, :half], mixed[freqs:, :half]], 1))
        differences.append(jnp.concatenate([mixed[:freqs, half:], mixed[freqs:, half:]], 1))
    return (
        right_by(jnp.concatenate(sums, 0), const["forward_even"]),
        right_by(jnp.concatenate(differences, 0), const["forward_odd"]),
    )


def inverse(spectrum, planes, const):
    even = right_by(spectrum[0], const["inverse_even"])
    odd = right_by(spectrum[1], const["inverse_odd"])
    freqs = even.shape[0] // planes
    half = even.shape[1] // 2
    strips = []
    for plane in range(planes):
        rows = slice(plane * freqs, (plane + 1) * freqs)
        stacked = jnp.concatenate(
            [
                jnp.concatenate([even[rows, :half], odd[rows, :half]], 1),
                jnp.concatenate([even[rows, half:], odd[rows, half:]], 1),
            ],
            0,
        )
        mixed = left_by(const["row_inverse"], stacked)
        first, second = mixed[:, :half], mixed[:, half:]
        strips.append(jnp.concatenate([first + second, first - second], 1))
    return strips


def times(spectrum, other, planes, conjugate):
    half = other.shape[1] // 2
    real = jnp.concatenate([other[:, :half]] * planes, 0)
    imag = jnp.concatenate([other[:, half:]] * planes, 0)
    left, right = spectrum[:, :half], spectrum[:, half:]
    if conjugate:
        return jnp.concatenate([left * real + right * imag, right * real - left * imag], 1)
    return jnp.concatenate([left * real - right * imag, left * imag + right * real], 1)


def cross(first, second, planes):
    half = first.shape[1] // 2
    freqs = first.shape[0] // planes
    left, right = first[:, :half], first[:, half:]
    real, imag = second[:, :half], second[:, half:]
    both = jnp.concatenate([left * real + right * imag, right * real - left * imag], 1)
    summed = both[:freqs]
    for plane in range(1, planes):
        summed = summed + both[plane * freqs : (plane + 1) * freqs]
    return summed


def near_kernel(own, last_out, first_out, wrap_out, sems):
    rows = own.shape[1]
    wrap_row = pl.multiple_of(jnp.where(lax.axis_index("tile") == 0, 0, rows - HALF), 8)
    copies = [
        pltpu.make_async_copy(own.at[:, pl.ds(rows - HALF, HALF), :], last_out, sems.at[0]),
        pltpu.make_async_copy(own.at[:, pl.ds(0, HALF), :], first_out, sems.at[1]),
        pltpu.make_async_copy(own.at[:, pl.ds(wrap_row, HALF), :], wrap_out, sems.at[2]),
    ]
    for copy in copies:
        copy.start()
    for copy in copies:
        copy.wait()


def first_kernel(phase, amplitude, own, observed, packed, pupil_out, field_out, spec_out, last_out, first_out, *, at):
    planes, rows, _ = own.shape
    last_out[:planes] = own[:, rows - 2 * HALF : rows - HALF]
    last_out[planes:] = observed[:, rows - HALF :]
    first_out[:planes] = own[:, HALF : 2 * HALF]
    first_out[planes:] = observed[:, :HALF]
    const = at(packed)
    pupil, field, psf = point_spread(phase[...], amplitude[...], const)
    pupil_out[...] = pupil
    field_out[...] = field
    spec_out[...] = kernel_spectrum(psf, const)


def halo_rows(before, after, wrap, plane):
    tile = lax.axis_index("tile")
    wrapped = wrap[plane]
    return (
        jnp.where(tile == 0, wrapped, before[plane]),
        jnp.where(tile == lax.axis_size("tile") - 1, wrapped, after[plane]),
    )


def gradient_kernel(before, own, after, wrap, observed, spec, pupil, field, packed, keep_out, give_out, *, at):
    planes, rows, cols = own.shape
    const = at(packed)
    strips = []
    for p in range(planes):
        above, below = halo_rows(before, after, wrap, p)
        strips.append(jnp.concatenate([above, own[p], below], 0))
    even, odd = forward(strips, const["row_forward"], const)
    blurred = inverse(
        (times(even, spec[:, :cols], planes, False), times(odd, spec[:, cols:], planes, False)), planes, const
    )
    misfit = [1.0 - observed[p] / (blurred[p] + BACKGROUND) for p in range(planes)]
    misfit_even, misfit_odd = forward(misfit, const["row_own"], const)
    shared = jnp.concatenate([cross(misfit_even, even, planes), cross(misfit_odd, odd, planes)], 1)
    across = right_by(shared, const["lag_right"])
    pad_cols = across.shape[1] // 2
    psf_grad = left_by(const["lag_left"], jnp.concatenate([across[:, :pad_cols], across[:, pad_cols:]], 0))
    far = field[...]
    pad_rows = far.shape[0] // 2
    real, imag = far[:pad_rows], far[pad_rows:]
    centred = 2.0 * (psf_grad - total(psf_grad * (real * real + imag * imag)))
    back = left_by(const["adjoint_left"], jnp.concatenate([centred * real, centred * imag], 0))
    pup = back.shape[0] // 2
    back = right_by(jnp.concatenate([back[:pup], back[pup:]], 1), const["adjoint_right"])
    near = pupil[...]
    slope = back[:, pup:] * near[:, :pup] - back[:, :pup] * near[:, pup:]
    even_core = lax.axis_index("tile") % 2 == 0
    keep_out[...] = jnp.where(even_core, slope[: pup // 2], slope[pup // 2 :])
    give_out[...] = jnp.where(even_core, slope[pup // 2 :], slope[: pup // 2])


def square_sums(value):
    rows = value.shape[0]
    squared = value * value
    summed = squared[:8]
    for top in range(8, rows, 8):
        summed = summed + squared[top : top + 8]
    return summed


def squares_kernel(mine, received, half_out, squares_out):
    half = mine[...] + received[...]
    half_out[...] = half
    squares_out[...] = square_sums(half)


def blocks_kernel(before, own, after, wrap, far_before, far_after, squares, packed, even_out, odd_out, *, at):
    planes = own.shape[0]
    const = at(packed)
    upper, lower = [], []
    for p in range(planes):
        above, below = halo_rows(before, after, wrap, p)
        upper.append(jnp.concatenate([far_before[p], above, own[p]], 0))
        lower.append(jnp.concatenate([own[p], below, far_after[p]], 0))
    even, odd = forward(upper + lower, const["row_forward"], const)
    even_out[...] = even
    odd_out[...] = odd


def second_kernel(
    phase, amplitude, half, other, squares, even, odd, own, far_before, observed, far_after,
    psf_packed, packed, objects_out, phase_out, *, psf_at, at, cells, others,
):
    planes, rows, cols = own.shape
    const = at(packed)
    psf_const = psf_at(psf_packed)
    mine, theirs = half[...], other[...]
    even_core = lax.axis_index("tile") % 2 == 0
    slope = jnp.concatenate([jnp.where(even_core, mine, theirs), jnp.where(even_core, theirs, mine)], 0)
    summed = square_sums(slope)
    for ref in (squares,) + others:
        summed = summed + ref[...]
    mean_square = total(summed) * (1.0 / cells)
    updated = phase[...] - STEP_SIZE * slope / jnp.sqrt(mean_square + EPSILON)
    phase_out[...] = updated
    _, _, psf = point_spread(updated, amplitude[...], psf_const)
    spec = kernel_spectrum(psf, psf_const)
    spec_even, spec_odd = spec[:, :cols], spec[:, cols:]
    blurred = inverse(
        (times(even[...], spec_even, 2 * planes, False), times(odd[...], spec_odd, 2 * planes, False)),
        2 * planes, const,
    )
    ratios = []
    for p in range(planes):
        light = jnp.concatenate([blurred[p], blurred[planes + p]], 0) + BACKGROUND
        ratios.append(jnp.concatenate([far_before[planes + p], observed[p], far_after[planes + p]], 0) / light)
    ratio_even, ratio_odd = forward(ratios, const["row_forward"], const)
    correction = inverse(
        (times(ratio_even, spec_even, planes, True), times(ratio_odd, spec_odd, planes, True)), planes, const
    )
    for p in range(planes):
        objects_out[p] = own[p] * correction[p]


def call(kernel, out_shapes, args, flops=10**6, anywhere=(), scratch=()):
    outs = [jax.ShapeDtypeStruct(shape, jnp.float32) for shape in out_shapes]
    return pl.pallas_call(
        kernel,
        out_shape=outs,
        in_specs=[
            pl.BlockSpec(memory_space=pl.ANY if i in anywhere else pltpu.VMEM) for i in range(len(args))
        ],
        out_specs=[pl.BlockSpec(memory_space=pltpu.VMEM)] * len(outs),
        scratch_shapes=scratch,
        compiler_params=pltpu.CompilerParams(vmem_limit_bytes=VMEM_LIMIT),
        cost_estimate=pl.CostEstimate(flops=flops, bytes_accessed=10**5, transcendentals=0),
    )(*args)


def ring(count):
    up = [(i, (i + 1) % count) for i in range(count)]
    return up, [(j, i) for i, j in up]


def exchange(value, step):
    return lax.ppermute(value, "tile", [(i, i ^ step) for i in range(lax.axis_size("tile"))])


def from_other_depths(value, flip):
    tiles, depths = lax.axis_size("tile"), lax.axis_size("depth")
    received = []
    for turn in range(1, depths):
        pairs = [
            (t * depths + d, (t ^ flip) * depths + (d + turn) % depths)
            for t in range(tiles)
            for d in range(depths)
        ]
        received.append(lax.ppermute(value, ("tile", "depth"), pairs))
    return received


def on_device(objects, observed, pupil_phase, pupil_amplitude):
    picture, measured, phase, amplitude = objects[0], observed[0], pupil_phase[0], pupil_amplitude[0]
    planes, rows, cols = picture.shape
    pup = phase.shape[0]
    count = lax.axis_size("tile")
    ker = 2 * HALF + 1
    length = rows + 2 * HALF
    pad_rows, pad_cols = round_up(ker, 16), round_up(ker, 128)
    row_forward, row_inverse = row_constants(rows, length)
    col_forward, col_inverse = col_constants(cols)
    kernel_rows, kernel_right = kernel_constants(length, cols, ker, pad_rows, pad_cols)
    pupil_left, pupil_right = pupil_constants(pup, ker, pad_rows, pad_cols)
    psf_const = Packed(
        {"pupil_left": pupil_left, "pupil_right": pupil_right, "kernel_rows": kernel_rows, "kernel_right": kernel_right},
        2 * cols,
    )
    const = Packed(
        {
            "row_forward": row_forward,
            "row_inverse": row_inverse,
            "forward_even": col_forward[0],
            "forward_odd": col_forward[1],
            "inverse_even": col_inverse[0],
            "inverse_odd": col_inverse[1],
            "row_own": row_forward[:, HALF : HALF + rows],
            "lag_right": kernel_right.T / cols,
            "lag_left": kernel_rows.T * (2.0 / length),
            "adjoint_left": pupil_left.T,
            "adjoint_right": pupil_right.T,
        },
        2 * cols,
    )
    psf_packed, packed = jnp.asarray(psf_const.array), jnp.asarray(const.array)

    edge = (planes, HALF, cols)
    last, first, wrap = call(near_kernel, [edge] * 3, (picture,), anywhere=(0,), scratch=[pltpu.SemaphoreType.DMA((3,))])
    up, down = ring(count)
    before = lax.ppermute(last, "tile", up[:-1])
    after = lax.ppermute(first, "tile", down[:-1])
    wrap = lax.ppermute(wrap, "tile", [(0, count - 1), (count - 1, 0)])
    pupil, field, spec, far_last, far_first = call(
        functools.partial(first_kernel, at=psf_const.at),
        [(pup, 2 * pup), (2 * pad_rows, pad_cols), (length // 2, 2 * cols)] + [(2 * planes, HALF, cols)] * 2,
        (phase, amplitude, picture, measured, psf_packed),
        flops=4 * 10**9,
    )
    far_before = lax.ppermute(far_last, "tile", up)
    far_after = lax.ppermute(far_first, "tile", down)
    keep, give = call(
        functools.partial(gradient_kernel, at=const.at),
        [(pup // 2, pup)] * 2,
        (before, picture, after, wrap, measured, spec, pupil, field, packed),
    )
    half = keep + exchange(give, 1)
    steps = [1 << bit for bit in range(2, count.bit_length() - 1)] + [2]
    for step in steps[:-1]:
        half = half + exchange(half, step)
    half, squares = call(squares_kernel, [(pup // 2, pup), (8, pup)], (half, exchange(half, steps[-1])))
    other = exchange(half, 1)
    squares_of = from_other_depths(squares, 0) + from_other_depths(squares, 1)
    even, odd = call(
        functools.partial(blocks_kernel, at=const.at),
        [(planes * length, cols)] * 2,
        (before, picture, after, wrap, far_before, far_after, squares, packed),
        flops=3 * 10**9,
        anywhere=(6,),
    )
    depth_count = len(squares_of)

    def last_kernel(*refs):
        second_kernel(
            *refs[:4], refs[4], *refs[4 + depth_count :],
            psf_at=psf_const.at, at=const.at, cells=lax.axis_size("depth") * pup * pup, others=refs[5 : 4 + depth_count],
        )

    new_objects, new_phase = call(
        last_kernel,
        [picture.shape, phase.shape],
        (
            phase, amplitude, half, other, *squares_of, even, odd, picture,
            far_before, measured, far_after, psf_packed, packed,
        ),
    )
    return new_objects[None], new_phase[None]


def solution(mesh):
    return jax.shard_map(
        on_device,
        mesh=mesh,
        in_specs=(
            P("depth", None, "tile", None),
            P("depth", None, "tile", None),
            P("depth", None, None),
            P("depth", None, None),
        ),
        out_specs=(P("depth", None, "tile", None), P("depth", None, None)),
        check_vma=False,
    )
```

```python
import functools
import math

import jax
import jax.numpy as jnp
import ml_dtypes
import numpy as np
from jax import lax
from jax.experimental import pallas as pl
from jax.experimental.pallas import tpu as pltpu
from jax.sharding import PartitionSpec as P

HALF = 64
BACKGROUND = 0.1
STEP_SIZE = 0.3
EPSILON = 1e-06
VMEM_LIMIT = 32 * 1024 * 1024


def round_up(value, step):
    return -(-value // step) * step


def angles(left, right, length):
    return (2.0 * math.pi / length) * np.outer(left, right)


def halves(matrix):
    high = matrix.astype(np.float32).astype(ml_dtypes.bfloat16)
    low = (matrix - high.astype(np.float64)).astype(np.float32).astype(ml_dtypes.bfloat16)
    return high, low


def row_constants(rows, length):
    freqs = np.arange(length // 2) + 0.5
    theta = angles(freqs, np.arange(length), length)
    forward = np.concatenate([np.cos(theta), -np.sin(theta)], 0)
    inner = theta[:, HALF : HALF + rows]
    inverse = np.concatenate([np.cos(inner).T, -np.sin(inner).T], 1) * (2.0 / length)
    return forward, inverse


def col_constants(cols):
    half = cols // 2
    forward, inverse = [], []
    for parity in range(2):
        theta = angles(np.arange(half), 2 * np.arange(half) + parity, cols)
        c, s = np.cos(theta), np.sin(theta)
        forward.append(np.block([[c, -s], [s, c]]))
        inverse.append(np.block([[c.T, s.T], [-s.T, c.T]]) / cols)
    return forward, inverse


def kernel_constants(length, cols, ker, pad_rows, pad_cols):
    lags = np.arange(ker) - HALF
    theta = angles(np.arange(length // 2) + 0.5, lags, length)
    rows = np.zeros((length, pad_rows))
    rows[: length // 2, :ker] = np.cos(theta)
    rows[length // 2 :, :ker] = -np.sin(theta)
    half = cols // 2
    right = np.zeros((2 * pad_cols, 2 * cols))
    for parity in range(2):
        theta = angles(lags, 2 * np.arange(half) + parity, cols)
        c, s = np.cos(theta), np.sin(theta)
        at = parity * cols
        right[:ker, at : at + half] = c
        right[:ker, at + half : at + cols] = -s
        right[pad_cols : pad_cols + ker, at : at + half] = s
        right[pad_cols : pad_cols + ker, at + half : at + cols] = c
    return rows, right


def pupil_constants(pup, ker, pad_rows, pad_cols):
    theta = angles(np.arange(ker) - HALF, np.arange(pup), ker)
    real, imag = np.cos(theta), -np.sin(theta)
    right = np.zeros((2 * pup, 2 * pad_cols))
    right[:pup, :ker] = real.T
    right[:pup, pad_cols : pad_cols + ker] = imag.T
    right[pup:, :ker] = -imag.T
    right[pup:, pad_cols : pad_cols + ker] = real.T
    left = np.zeros((2 * pad_rows, 2 * pup))
    left[:ker, :pup] = real
    left[:ker, pup:] = -imag
    left[pad_rows : pad_rows + ker, :pup] = imag
    left[pad_rows : pad_rows + ker, pup:] = real
    return left, right


class Packed:
    def __init__(self, matrices, width):
        self.places, blocks, row = {}, [], 0
        for name, matrix in matrices.items():
            high, low = halves(matrix)
            rows, cols = matrix.shape
            beside = 2 * round_up(cols, 128) <= width
            block = np.zeros((round_up(rows, 16) * (1 if beside else 2), width), high.dtype)
            block[:rows, :cols] = high
            down, right = (0, width // 2) if beside else (round_up(rows, 16), 0)
            block[down : down + rows, right : right + cols] = low
            self.places[name] = (row, row + down, right, rows, cols)
            blocks.append(block)
            row += block.shape[0]
        self.array = np.concatenate(blocks)

    def at(self, ref):
        return {
            name: (ref.at[top : top + rows, :cols], ref.at[bottom : bottom + rows, right : right + cols])
            for name, (top, bottom, right, rows, cols) in self.places.items()
        }


def dot(left, right):
    return jnp.dot(left, right, preferred_element_type=jnp.float32)


def split(value):
    high = value.astype(jnp.bfloat16)
    low = (value - high.astype(jnp.float32)).astype(jnp.bfloat16)
    return high, low


def left_by(const, value):
    high, low = split(value)
    return dot(const[0][...], high) + (dot(const[1][...], high) + dot(const[0][...], low))


def right_by(value, const):
    high, low = split(value)
    return dot(high, const[0][...]) + (dot(low, const[0][...]) + dot(high, const[1][...]))


def sine_cosine(angle):
    turns = jnp.floor(angle * (2.0 / math.pi) + 0.5)
    rest = angle - turns * 1.5703125
    rest = rest - turns * 4.837512969970703e-4
    rest = rest - turns * 7.54978995489e-8
    square = rest * rest
    sine = rest + rest * square * (
        -1.6666654611e-1 + square * (8.3321608736e-3 + square * -1.9515295891e-4)
    )
    cosine = 1.0 - 0.5 * square + square * square * (
        4.166664568298827e-2 + square * (-1.388731625493765e-3 + square * 2.443315711809948e-5)
    )
    quadrant = turns.astype(jnp.int32) & 3
    swap = (quadrant & 1) == 1
    sine_out = jnp.where(swap, cosine, sine)
    cosine_out = jnp.where(swap, sine, cosine)
    sine_out = jnp.where(quadrant >= 2, -sine_out, sine_out)
    cosine_out = jnp.where((quadrant == 1) | (quadrant == 2), -cosine_out, cosine_out)
    return sine_out, cosine_out


def total(value):
    return jnp.sum(jnp.sum(value, axis=0, keepdims=True), axis=1, keepdims=True)


def weights(amplitude):
    pup = amplitude.shape[0]
    rows = lax.broadcasted_iota(jnp.int32, amplitude.shape, 0).astype(jnp.float32) - (pup - 1) / 2.0
    cols = lax.broadcasted_iota(jnp.int32, amplitude.shape, 1).astype(jnp.float32) - (pup - 1) / 2.0
    return jnp.where(rows * rows + cols * cols <= (pup / 2.0) ** 2, amplitude, 0.0)


def point_spread(phase, amplitude, const, ready=lambda: None):
    weight = weights(amplitude)
    sine, cosine = sine_cosine(phase)
    pupil = jnp.concatenate([weight * cosine, weight * sine], 1)
    ready()
    across = right_by(pupil, const["pupil_right"])
    cols = across.shape[1] // 2
    field = left_by(const["pupil_left"], jnp.concatenate([across[:, :cols], across[:, cols:]], 0))
    rows = field.shape[0] // 2
    intensity = field[:rows] * field[:rows] + field[rows:] * field[rows:]
    norm = 1.0 / total(intensity)
    left = left_by(const["kernel_rows"], intensity)
    freqs = left.shape[0] // 2
    spectrum = right_by(jnp.concatenate([left[:freqs], left[freqs:]], 1), const["kernel_right"])
    return pupil, field, spectrum * norm, norm


def forward(strips, row_matrix, const):
    sums, differences = [], []
    for strip in strips:
        half = strip.shape[1] // 2
        first, second = strip[:, :half], strip[:, half:]
        mixed = left_by(row_matrix, jnp.concatenate([first + second, first - second], 1))
        freqs = mixed.shape[0] // 2
        sums.append(jnp.concatenate([mixed[:freqs, :half], mixed[freqs:, :half]], 1))
        differences.append(jnp.concatenate([mixed[:freqs, half:], mixed[freqs:, half:]], 1))
    even = [right_by(jnp.concatenate(sums[p : p + 2], 0), const["forward_even"]) for p in range(0, len(sums), 2)]
    odd = [right_by(jnp.concatenate(differences[p : p + 2], 0), const["forward_odd"]) for p in range(0, len(sums), 2)]
    return even, odd


def inverse(even, odd, freqs, const):
    even = [right_by(spectrum, const["inverse_even"]) for spectrum in even]
    odd = [right_by(spectrum, const["inverse_odd"]) for spectrum in odd]
    strips = []
    for sums, differences in zip(even, odd):
        half = sums.shape[1] // 2
        for top in range(0, sums.shape[0], freqs):
            rows = slice(top, top + freqs)
            stacked = jnp.concatenate(
                [
                    jnp.concatenate([sums[rows, :half], differences[rows, :half]], 1),
                    jnp.concatenate([sums[rows, half:], differences[rows, half:]], 1),
                ],
                0,
            )
            mixed = left_by(const["row_inverse"], stacked)
            first, second = mixed[:, :half], mixed[:, half:]
            strips.append(jnp.concatenate([first + second, first - second], 1))
    return strips


def times(spectra, other, conjugate):
    half = other.shape[1] // 2
    products = []
    for spectrum in spectra:
        planes = spectrum.shape[0] // other.shape[0]
        real = jnp.concatenate([other[:, :half]] * planes, 0)
        imag = jnp.concatenate([other[:, half:]] * planes, 0)
        left, right = spectrum[:, :half], spectrum[:, half:]
        if conjugate:
            product = [left * real + right * imag, right * real - left * imag]
        else:
            product = [left * real - right * imag, left * imag + right * real]
        products.append(jnp.concatenate(product, 1))
    return products


def cross(firsts, seconds, freqs):
    summed = None
    for first, second in zip(firsts, seconds):
        half = first.shape[1] // 2
        left, right = first[:, :half], first[:, half:]
        real, imag = second[:, :half], second[:, half:]
        both = jnp.concatenate([left * real + right * imag, right * real - left * imag], 1)
        for top in range(0, both.shape[0], freqs):
            summed = both[top : top + freqs] if summed is None else summed + both[top : top + freqs]
    return summed


def is_even():
    return lax.axis_index("tile") % 2 == 0


def edge_rows(top, bottom):
    even = is_even()
    return [pl.multiple_of(jnp.where(even, *choice), 8) for choice in ((top, bottom), (bottom, top))]


def run_all(copies):
    for copy in copies:
        copy.start()
    for copy in copies:
        copy.wait()


def near_kernel(own, chip_out, core_out, sems):
    chip, core = edge_rows(0, own.shape[1] - HALF)
    run_all([
        pltpu.make_async_copy(own.at[:, pl.ds(chip, HALF), :], chip_out, sems.at[0]),
        pltpu.make_async_copy(own.at[:, pl.ds(core, HALF), :], core_out, sems.at[1]),
    ])


def first_kernel(
    phase, amplitude, own, observed, psf_packed, _, pupil_out, field_out, spec_out, chip_out, core_out, psf_out,
    phase_in, amplitude_in, sems, *, at,
):
    planes, rows, _ = own.shape
    objects_chip, objects_core = edge_rows(HALF, rows - 2 * HALF)
    observed_chip, observed_core = edge_rows(0, rows - HALF)
    pairs = [
        (phase, phase_in),
        (amplitude, amplitude_in),
        (psf_packed, psf_out),
        (own.at[:, pl.ds(objects_chip, HALF), :], chip_out.at[:planes]),
        (observed.at[:, pl.ds(observed_chip, HALF), :], chip_out.at[planes:]),
        (own.at[:, pl.ds(objects_core, HALF), :], core_out.at[:planes]),
        (observed.at[:, pl.ds(observed_core, HALF), :], core_out.at[planes:]),
    ]
    copies = [pltpu.make_async_copy(source, target, sems.at[i]) for i, (source, target) in enumerate(pairs)]
    for copy in copies:
        copy.start()
    for copy in copies[:2]:
        copy.wait()
    const = at(psf_out)
    pupil, field, spectrum, norm = point_spread(phase_in[...], amplitude_in[...], const, copies[2].wait)
    root = jnp.sqrt(norm)
    pupil_out[...] = pupil * root
    field_out[...] = field * root
    spec_out[...] = spectrum
    for copy in copies[3:]:
        copy.wait()


def halo_rows(chip, core):
    even = is_even()
    return jnp.where(even, chip, core), jnp.where(even, core, chip)


def gradient_kernel(from_chip, from_core, own, observed, spec, pupil, field, packed, keep_out, give_out, *, at):
    planes, rows, cols = own.shape
    const = at(packed)
    freqs = spec.shape[0]
    strips = []
    for p in range(planes):
        above, below = halo_rows(from_chip[p], from_core[p])
        strips.append(jnp.concatenate([above, own[p], below], 0))
    even, odd = forward(strips, const["row_forward"], const)
    blurred = inverse(times(even, spec[:, :cols], False), times(odd, spec[:, cols:], False), freqs, const)
    misfit = [1.0 - observed[p] / (blurred[p] + BACKGROUND) for p in range(planes)]
    misfit_even, misfit_odd = forward(misfit, const["row_own"], const)
    shared = jnp.concatenate([cross(misfit_even, even, freqs), cross(misfit_odd, odd, freqs)], 1)
    across = right_by(shared, const["lag_right"])
    pad_cols = across.shape[1] // 2
    psf_grad = left_by(const["lag_left"], jnp.concatenate([across[:, :pad_cols], across[:, pad_cols:]], 0))
    far = field[...]
    pad_rows = far.shape[0] // 2
    real, imag = far[:pad_rows], far[pad_rows:]
    centred = 2.0 * (psf_grad - total(psf_grad * (real * real + imag * imag)))
    back = left_by(const["adjoint_left"], jnp.concatenate([centred * real, centred * imag], 0))
    pup = back.shape[0] // 2
    back = right_by(jnp.concatenate([back[:pup], back[pup:]], 1), const["adjoint_right"])
    near = pupil[...]
    slope = back[:, pup:] * near[:, :pup] - back[:, :pup] * near[:, pup:]
    even_core = is_even()
    keep_out[...] = jnp.where(even_core, slope[: pup // 2], slope[pup // 2 :])
    give_out[...] = jnp.where(even_core, slope[pup // 2 :], slope[: pup // 2])


def square_sums(value):
    rows = value.shape[0]
    squared = value * value
    summed = squared[:8]
    for top in range(8, rows, 8):
        summed = summed + squared[top : top + 8]
    return summed


def squares_kernel(mine, received, joined_out):
    half = mine[...] + received[...]
    joined_out[: half.shape[0]] = half
    joined_out[half.shape[0] :] = square_sums(half)


def blocks_kernel(from_chip, from_core, own, far_chip, far_core, _, packed, even_out, odd_out, *, at):
    planes = own.shape[0]
    const = at(packed)
    strips = []
    for p in range(planes):
        above, below = halo_rows(from_chip[p], from_core[p])
        far_above, far_below = halo_rows(far_chip[p], far_core[p])
        strips.append(jnp.concatenate([far_above, above, own[p]], 0))
        strips.append(jnp.concatenate([own[p], below, far_below], 0))
    even, odd = forward(strips, const["row_forward"], const)
    even_out[...] = jnp.concatenate(even, 0)
    odd_out[...] = jnp.concatenate(odd, 0)


def second_kernel(
    phase, amplitude, mine, theirs, squares, even, odd, own, observed, far_chip, far_core,
    psf_packed, packed, objects_out, phase_out, *, psf_at, at, cells,
):
    planes, rows, cols = own.shape
    const = at(packed)
    half = phase.shape[0] // 2
    first, second = halo_rows(mine[:half], theirs[:half])
    slope = jnp.concatenate([first, second], 0)
    summed = squares[...]
    mean_square = total(summed) * (1.0 / cells)
    updated = phase[...] - STEP_SIZE * slope / jnp.sqrt(mean_square + EPSILON)
    phase_out[...] = updated
    _, _, spec, _ = point_spread(updated, amplitude[...], psf_at(psf_packed))
    spec_even, spec_odd = spec[:, :cols], spec[:, cols:]
    freqs = spec.shape[0]
    pairs = range(0, even.shape[0], 2 * freqs)
    light = inverse(
        times([even[top : top + 2 * freqs] for top in pairs], spec_even, False),
        times([odd[top : top + 2 * freqs] for top in pairs], spec_odd, False),
        freqs, const,
    )
    ratios = []
    for p in range(planes):
        above, below = halo_rows(far_chip[planes + p], far_core[planes + p])
        blurred = jnp.concatenate(light[2 * p : 2 * p + 2], 0) + BACKGROUND
        ratios.append(jnp.concatenate([above, observed[p], below], 0) / blurred)
    ratio_even, ratio_odd = forward(ratios, const["row_forward"], const)
    correction = inverse(times(ratio_even, spec_even, True), times(ratio_odd, spec_odd, True), freqs, const)
    for p in range(planes):
        objects_out[p] = own[p] * correction[p]


def call(kernel, out_shapes, args, flops=10**6, spaces=None, scratch=()):
    outs = [
        jax.ShapeDtypeStruct(shape, jnp.float32) if isinstance(shape, tuple) else shape for shape in out_shapes
    ]
    spaces = spaces or {}
    return pl.pallas_call(
        kernel,
        out_shape=outs,
        in_specs=[pl.BlockSpec(memory_space=spaces.get(i, pltpu.VMEM)) for i in range(len(args))],
        out_specs=[pl.BlockSpec(memory_space=pltpu.VMEM)] * len(outs),
        scratch_shapes=scratch,
        compiler_params=pltpu.CompilerParams(vmem_limit_bytes=VMEM_LIMIT),
        cost_estimate=pl.CostEstimate(flops=flops, bytes_accessed=10**5, transcendentals=0),
    )(*args)


def swap(chip_rows, core_rows):
    count = lax.axis_size("tile")
    chip_pairs = [(i, (i + 1 if i % 2 else i - 1) % count) for i in range(count)]
    return lax.ppermute(chip_rows, "tile", chip_pairs), exchange(core_rows, 1)


def exchange(value, step):
    return lax.ppermute(value, "tile", [(i, i ^ step) for i in range(lax.axis_size("tile"))])


def sum_over_depth(value):
    count = lax.axis_size("depth")
    if count & (count - 1):
        return lax.psum(value, "depth")
    for bit in range(count.bit_length() - 1):
        value = value + lax.ppermute(value, "depth", [(i, i ^ (1 << bit)) for i in range(count)])
    return value


def on_device(objects, observed, pupil_phase, pupil_amplitude):
    picture, measured, phase, amplitude = objects[0], observed[0], pupil_phase[0], pupil_amplitude[0]
    planes, rows, cols = picture.shape
    pup = phase.shape[0]
    count = lax.axis_size("tile")
    ker = 2 * HALF + 1
    length = rows + 2 * HALF
    pad_rows, pad_cols = round_up(ker, 16), round_up(ker, 128)
    row_forward, row_inverse = row_constants(rows, length)
    col_forward, col_inverse = col_constants(cols)
    kernel_rows, kernel_right = kernel_constants(length, cols, ker, pad_rows, pad_cols)
    pupil_left, pupil_right = pupil_constants(pup, ker, pad_rows, pad_cols)
    psf_const = Packed(
        {"pupil_left": pupil_left, "pupil_right": pupil_right, "kernel_rows": kernel_rows, "kernel_right": kernel_right},
        2 * cols,
    )
    const = Packed(
        {
            "row_forward": row_forward,
            "row_inverse": row_inverse,
            "forward_even": col_forward[0],
            "forward_odd": col_forward[1],
            "inverse_even": col_inverse[0],
            "inverse_odd": col_inverse[1],
            "row_own": row_forward[:, HALF : HALF + rows],
            "lag_right": kernel_right.T / cols,
            "lag_left": kernel_rows.T * (2.0 / length),
            "adjoint_left": pupil_left.T,
            "adjoint_right": pupil_right.T,
        },
        2 * cols,
    )
    psf_packed, packed = jnp.asarray(psf_const.array), jnp.asarray(const.array)

    in_hbm = [
        pltpu.with_memory_space_constraint(value, pltpu.HBM)
        for value in (phase, amplitude, picture, measured, psf_packed)
    ]
    edge = (planes, HALF, cols)
    chip_rows, core_rows = call(near_kernel, [edge] * 2, in_hbm[2:3], scratch=[pltpu.SemaphoreType.DMA((2,))], spaces={0: pltpu.HBM})
    from_chip, from_core = swap(chip_rows, core_rows)
    pupil, field, spec, far_chip, far_core, psf_packed = call(
        functools.partial(first_kernel, at=psf_const.at),
        [(pup, 2 * pup), (2 * pad_rows, pad_cols), (length // 2, 2 * cols)]
        + [(2 * planes, HALF, cols)] * 2
        + [psf_packed],
        (*in_hbm, chip_rows),
        flops=3 * 10**9,
        spaces={0: pltpu.HBM, 1: pltpu.HBM, 2: pltpu.HBM, 3: pltpu.HBM, 4: pltpu.HBM, 5: pl.ANY},
        scratch=[pltpu.VMEM(phase.shape, jnp.float32)] * 2 + [pltpu.SemaphoreType.DMA((7,))],
    )
    far_chip, far_core, from_chip, from_core = lax.optimization_barrier((far_chip, far_core, from_chip, from_core))
    far_chip, far_core = swap(far_chip, far_core)
    keep, give = call(
        functools.partial(gradient_kernel, at=const.at),
        [(pup // 2, pup)] * 2,
        (from_chip, from_core, picture, measured, spec, pupil, field, packed),
        flops=4 * 10**10,
    )
    half = keep + exchange(give, 1)
    bits = list(range(2, count.bit_length() - 1))
    for low, high in zip(bits[::2], bits[1::2]):
        half = half + ((exchange(half, 1 << low) + exchange(half, 1 << high)) + exchange(half, (1 << low) | (1 << high)))
    if len(bits) % 2:
        half = half + exchange(half, 1 << bits[-1])
    received = exchange(half, 2)
    even, odd = call(
        functools.partial(blocks_kernel, at=const.at),
        [(planes * length, cols)] * 2,
        (from_chip, from_core, picture, far_chip, far_core, half, packed),
        spaces={5: pl.ANY},
    )
    received, even = lax.optimization_barrier((received, even))
    (joined,) = call(squares_kernel, [(pup // 2 + 8, pup)], (half, received))
    other = exchange(joined, 1)
    squares = sum_over_depth(joined[pup // 2 :] + other[pup // 2 :])
    new_objects, new_phase = call(
        functools.partial(
            second_kernel, psf_at=psf_const.at, at=const.at, cells=lax.axis_size("depth") * pup * pup
        ),
        [picture.shape, phase.shape],
        (
            phase, amplitude, joined, other, squares, even, odd, picture, measured,
            far_chip, far_core, psf_packed, packed,
        ),
    )
    return new_objects[None], new_phase[None]


def solution(mesh):
    return jax.shard_map(
        on_device,
        mesh=mesh,
        in_specs=(
            P("depth", None, "tile", None),
            P("depth", None, "tile", None),
            P("depth", None, None),
            P("depth", None, None),
        ),
        out_specs=(P("depth", None, "tile", None), P("depth", None, None)),
        check_vma=False,
    )
```

```python
import functools
import math

import jax
import jax.numpy as jnp
import ml_dtypes
import numpy as np
from jax import lax
from jax.experimental import pallas as pl
from jax.experimental.pallas import tpu as pltpu
from jax.sharding import PartitionSpec as P

HALF = 64
BACKGROUND = 0.1
STEP_SIZE = 0.3
EPSILON = 1e-06
VMEM_LIMIT = 32 * 1024 * 1024


def round_up(value, step):
    return -(-value // step) * step


def angles(left, right, length):
    return (2.0 * math.pi / length) * np.outer(left, right)


def halves(matrix):
    high = matrix.astype(np.float32).astype(ml_dtypes.bfloat16)
    low = (matrix - high.astype(np.float64)).astype(np.float32).astype(ml_dtypes.bfloat16)
    return high, low


def row_constants(rows, length):
    freqs = np.arange(length // 2) + 0.5
    theta = angles(freqs, np.arange(length), length)
    forward = np.concatenate([np.cos(theta), -np.sin(theta)], 0)
    inner = theta[:, HALF : HALF + rows]
    inverse = np.concatenate([np.cos(inner).T, -np.sin(inner).T], 1) * (2.0 / length)
    return forward, inverse


def col_constants(cols):
    half = cols // 2
    forward, inverse = [], []
    for parity in range(2):
        theta = angles(np.arange(half), 2 * np.arange(half) + parity, cols)
        c, s = np.cos(theta), np.sin(theta)
        forward.append(np.block([[c, -s], [s, c]]))
        inverse.append(np.block([[c.T, s.T], [-s.T, c.T]]) / cols)
    return forward, inverse


def kernel_constants(length, cols, ker, pad_rows, pad_cols):
    lags = np.arange(ker) - HALF
    theta = angles(np.arange(length // 2) + 0.5, lags, length)
    rows = np.zeros((length, pad_rows))
    rows[: length // 2, :ker] = np.cos(theta)
    rows[length // 2 :, :ker] = -np.sin(theta)
    half = cols // 2
    right = np.zeros((2 * pad_cols, 2 * cols))
    for parity in range(2):
        theta = angles(lags, 2 * np.arange(half) + parity, cols)
        c, s = np.cos(theta), np.sin(theta)
        at = parity * cols
        right[:ker, at : at + half] = c
        right[:ker, at + half : at + cols] = -s
        right[pad_cols : pad_cols + ker, at : at + half] = s
        right[pad_cols : pad_cols + ker, at + half : at + cols] = c
    return rows, right


def pupil_constants(pup, ker, pad_rows, pad_cols):
    theta = angles(np.arange(ker) - HALF, np.arange(pup), ker)
    real, imag = np.cos(theta), -np.sin(theta)
    right = np.zeros((2 * pup, 2 * pad_cols))
    right[:pup, :ker] = real.T
    right[:pup, pad_cols : pad_cols + ker] = imag.T
    right[pup:, :ker] = -imag.T
    right[pup:, pad_cols : pad_cols + ker] = real.T
    left = np.zeros((2 * pad_rows, 2 * pup))
    left[:ker, :pup] = real
    left[:ker, pup:] = -imag
    left[pad_rows : pad_rows + ker, :pup] = imag
    left[pad_rows : pad_rows + ker, pup:] = real
    return left, right


class Joined:
    def __init__(self, left, right):
        self.places, groups = {}, {}
        for name, matrix in left.items():
            high, low = halves(matrix)
            groups.setdefault("left", []).append((name, np.concatenate([high, low, high], 1)))
        for name, matrix in right.items():
            high, low = halves(matrix)
            groups.setdefault(matrix.shape[0], []).append((name, np.concatenate([high, high, low], 0)))
        self.arrays = []
        for kind, members in groups.items():
            at = 0
            for name, block in members:
                rows, cols = block.shape
                start = (at, 0) if kind == "left" else (0, at)
                self.places[name] = (len(self.arrays), *start, rows, cols)
                at += rows if kind == "left" else cols
            blocks = [block for _, block in members]
            if kind == "left":
                width = max(block.shape[1] for block in blocks)
                blocks = [np.pad(block, ((0, 0), (0, width - block.shape[1]))) for block in blocks]
            self.arrays.append(np.concatenate(blocks, 0 if kind == "left" else 1))

    def at(self, *refs):
        return {
            name: refs[which].at[top : top + rows, first : first + cols]
            for name, (which, top, first, rows, cols) in self.places.items()
        }


def dot(left, right):
    return jnp.dot(left, right, preferred_element_type=jnp.float32)


def split(value):
    high = value.astype(jnp.bfloat16)
    low = (value - high.astype(jnp.float32)).astype(jnp.bfloat16)
    return high, low


def left_by(const, value):
    high, low = split(value)
    return dot(const[...], jnp.concatenate([high, high, low], 0))


def right_by(value, const):
    high, low = split(value)
    return dot(jnp.concatenate([high, low, high], 1), const[...])


def sine_cosine(angle):
    turns = jnp.floor(angle * (2.0 / math.pi) + 0.5)
    rest = angle - turns * 1.5703125
    rest = rest - turns * 4.837512969970703e-4
    rest = rest - turns * 7.54978995489e-8
    square = rest * rest
    sine = rest + rest * square * (
        -1.6666654611e-1 + square * (8.3321608736e-3 + square * -1.9515295891e-4)
    )
    cosine = 1.0 - 0.5 * square + square * square * (
        4.166664568298827e-2 + square * (-1.388731625493765e-3 + square * 2.443315711809948e-5)
    )
    quadrant = turns.astype(jnp.int32) & 3
    swap = (quadrant & 1) == 1
    sine_out = jnp.where(swap, cosine, sine)
    cosine_out = jnp.where(swap, sine, cosine)
    sine_out = jnp.where(quadrant >= 2, -sine_out, sine_out)
    cosine_out = jnp.where((quadrant == 1) | (quadrant == 2), -cosine_out, cosine_out)
    return sine_out, cosine_out


def total(value):
    return jnp.sum(jnp.sum(value, axis=0, keepdims=True), axis=1, keepdims=True)


def weights(amplitude):
    pup = amplitude.shape[0]
    rows = lax.broadcasted_iota(jnp.int32, amplitude.shape, 0).astype(jnp.float32) - (pup - 1) / 2.0
    cols = lax.broadcasted_iota(jnp.int32, amplitude.shape, 1).astype(jnp.float32) - (pup - 1) / 2.0
    return jnp.where(rows * rows + cols * cols <= (pup / 2.0) ** 2, amplitude, 0.0)


def point_spread(phase, amplitude, const, ready=lambda: None):
    weight = weights(amplitude)
    sine, cosine = sine_cosine(phase)
    pupil = jnp.concatenate([weight * cosine, weight * sine], 1)
    ready()
    across = right_by(pupil, const["pupil_right"])
    cols = across.shape[1] // 2
    field = left_by(const["pupil_left"], jnp.concatenate([across[:, :cols], across[:, cols:]], 0))
    rows = field.shape[0] // 2
    intensity = field[:rows] * field[:rows] + field[rows:] * field[rows:]
    norm = 1.0 / total(intensity)
    left = left_by(const["kernel_rows"], intensity)
    freqs = left.shape[0] // 2
    spectrum = right_by(jnp.concatenate([left[:freqs], left[freqs:]], 1), const["kernel_right"])
    return pupil, field, spectrum * norm, norm


def forward(strips, row_matrix, const):
    sums, differences = [], []
    for strip in strips:
        half = strip.shape[1] // 2
        first, second = strip[:, :half], strip[:, half:]
        mixed = left_by(row_matrix, jnp.concatenate([first + second, first - second], 1))
        freqs = mixed.shape[0] // 2
        sums.append(jnp.concatenate([mixed[:freqs, :half], mixed[freqs:, :half]], 1))
        differences.append(jnp.concatenate([mixed[:freqs, half:], mixed[freqs:, half:]], 1))
    even = [right_by(jnp.concatenate(sums[p : p + 2], 0), const["forward_even"]) for p in range(0, len(sums), 2)]
    odd = [right_by(jnp.concatenate(differences[p : p + 2], 0), const["forward_odd"]) for p in range(0, len(sums), 2)]
    return even, odd


def inverse(even, odd, freqs, const):
    even = [right_by(spectrum, const["inverse_even"]) for spectrum in even]
    odd = [right_by(spectrum, const["inverse_odd"]) for spectrum in odd]
    strips = []
    for sums, differences in zip(even, odd):
        half = sums.shape[1] // 2
        for top in range(0, sums.shape[0], freqs):
            rows = slice(top, top + freqs)
            stacked = jnp.concatenate(
                [
                    jnp.concatenate([sums[rows, :half], differences[rows, :half]], 1),
                    jnp.concatenate([sums[rows, half:], differences[rows, half:]], 1),
                ],
                0,
            )
            mixed = left_by(const["row_inverse"], stacked)
            first, second = mixed[:, :half], mixed[:, half:]
            strips.append(jnp.concatenate([first + second, first - second], 1))
    return strips


def times(spectra, other, conjugate):
    half = other.shape[1] // 2
    products = []
    for spectrum in spectra:
        planes = spectrum.shape[0] // other.shape[0]
        real = jnp.concatenate([other[:, :half]] * planes, 0)
        imag = jnp.concatenate([other[:, half:]] * planes, 0)
        left, right = spectrum[:, :half], spectrum[:, half:]
        if conjugate:
            product = [left * real + right * imag, right * real - left * imag]
        else:
            product = [left * real - right * imag, left * imag + right * real]
        products.append(jnp.concatenate(product, 1))
    return products


def cross(firsts, seconds, freqs):
    summed = None
    for first, second in zip(firsts, seconds):
        half = first.shape[1] // 2
        left, right = first[:, :half], first[:, half:]
        real, imag = second[:, :half], second[:, half:]
        both = jnp.concatenate([left * real + right * imag, right * real - left * imag], 1)
        for top in range(0, both.shape[0], freqs):
            summed = both[top : top + freqs] if summed is None else summed + both[top : top + freqs]
    return summed


def is_even():
    return lax.axis_index("tile") % 2 == 0


def edge_rows(top, bottom):
    even = is_even()
    return [pl.multiple_of(jnp.where(even, *choice), 8) for choice in ((top, bottom), (bottom, top))]


def run_all(copies):
    for copy in copies:
        copy.start()
    for copy in copies:
        copy.wait()


def near_kernel(own, chip_out, core_out, sems):
    chip, core = edge_rows(0, own.shape[1] - HALF)
    run_all([
        pltpu.make_async_copy(own.at[:, pl.ds(chip, HALF), :], chip_out, sems.at[0]),
        pltpu.make_async_copy(own.at[:, pl.ds(core, HALF), :], core_out, sems.at[1]),
    ])


def first_kernel(
    phase, amplitude, own, observed, *refs, at, arrays,
):
    psf_refs, (_, pupil_out, field_out, spec_out, chip_out, core_out) = refs[:arrays], refs[arrays : arrays + 6]
    psf_outs, (phase_in, amplitude_in, sems) = refs[arrays + 6 : -3], refs[-3:]
    planes, rows, _ = own.shape
    objects_chip, objects_core = edge_rows(HALF, rows - 2 * HALF)
    observed_chip, observed_core = edge_rows(0, rows - HALF)
    pairs = [
        (phase, phase_in),
        (amplitude, amplitude_in),
        *zip(psf_refs, psf_outs),
        (own.at[:, pl.ds(objects_chip, HALF), :], chip_out.at[:planes]),
        (observed.at[:, pl.ds(observed_chip, HALF), :], chip_out.at[planes:]),
        (own.at[:, pl.ds(objects_core, HALF), :], core_out.at[:planes]),
        (observed.at[:, pl.ds(observed_core, HALF), :], core_out.at[planes:]),
    ]
    copies = [pltpu.make_async_copy(source, target, sems.at[i]) for i, (source, target) in enumerate(pairs)]
    for copy in copies:
        copy.start()
    for copy in copies[:2]:
        copy.wait()

    def matrices_are_here():
        for copy in copies[2 : 2 + arrays]:
            copy.wait()

    pupil, field, spectrum, norm = point_spread(phase_in[...], amplitude_in[...], at(*psf_outs), matrices_are_here)
    root = jnp.sqrt(norm)
    pupil_out[...] = pupil * root
    field_out[...] = field * root
    spec_out[...] = spectrum
    for copy in copies[2 + arrays :]:
        copy.wait()


def halo_rows(chip, core):
    even = is_even()
    return jnp.where(even, chip, core), jnp.where(even, core, chip)


def gradient_kernel(
    from_chip, from_core, own, observed, spec, pupil, field, *refs, at,
):
    planes, rows, cols = own.shape
    const = at(*refs[:-2])
    keep_out, give_out = refs[-2:]
    freqs = spec.shape[0]
    strips = []
    for p in range(planes):
        above, below = halo_rows(from_chip[p], from_core[p])
        strips.append(jnp.concatenate([above, own[p], below], 0))
    even, odd = forward(strips, const["row_forward"], const)
    blurred = inverse(times(even, spec[:, :cols], False), times(odd, spec[:, cols:], False), freqs, const)
    misfit = [1.0 - observed[p] / (blurred[p] + BACKGROUND) for p in range(planes)]
    misfit_even, misfit_odd = forward(misfit, const["row_own"], const)
    shared = jnp.concatenate([cross(misfit_even, even, freqs), cross(misfit_odd, odd, freqs)], 1)
    across = right_by(shared, const["lag_right"])
    pad_cols = across.shape[1] // 2
    psf_grad = left_by(const["lag_left"], jnp.concatenate([across[:, :pad_cols], across[:, pad_cols:]], 0))
    far = field[...]
    pad_rows = far.shape[0] // 2
    real, imag = far[:pad_rows], far[pad_rows:]
    centred = 2.0 * (psf_grad - total(psf_grad * (real * real + imag * imag)))
    back = left_by(const["adjoint_left"], jnp.concatenate([centred * real, centred * imag], 0))
    pup = back.shape[0] // 2
    back = right_by(jnp.concatenate([back[:pup], back[pup:]], 1), const["adjoint_right"])
    near = pupil[...]
    slope = back[:, pup:] * near[:, :pup] - back[:, :pup] * near[:, pup:]
    even_core = is_even()
    keep_out[...] = jnp.where(even_core, slope[: pup // 2], slope[pup // 2 :])
    give_out[...] = jnp.where(even_core, slope[pup // 2 :], slope[: pup // 2])


def square_sums(value):
    rows = value.shape[0]
    squared = value * value
    summed = squared[:8]
    for top in range(8, rows, 8):
        summed = summed + squared[top : top + 8]
    return summed


def squares_kernel(mine, received, *others):
    joined_out = others[-1]
    half = mine[...] + received[...]
    squares = square_sums(half)
    for first, second in zip(others[:-1:2], others[1:-1:2]):
        squares = squares + square_sums(first[...] + second[...])
    joined_out[: half.shape[0]] = half
    joined_out[half.shape[0] :] = squares


def blocks_kernel(from_chip, from_core, own, far_chip, far_core, _, *refs, at):
    planes = own.shape[0]
    const = at(*refs[:-2])
    even_out, odd_out = refs[-2:]
    strips = []
    for p in range(planes):
        above, below = halo_rows(from_chip[p], from_core[p])
        far_above, far_below = halo_rows(far_chip[p], far_core[p])
        strips.append(jnp.concatenate([far_above, above, own[p]], 0))
        strips.append(jnp.concatenate([own[p], below, far_below], 0))
    even, odd = forward(strips, const["row_forward"], const)
    even_out[...] = jnp.concatenate(even, 0)
    odd_out[...] = jnp.concatenate(odd, 0)


def second_kernel(
    phase, amplitude, mine, theirs, squares, even, odd, own, observed, far_chip, far_core,
    *refs, at, psf_at, arrays, cells,
):
    planes, rows, cols = own.shape
    const = at(*refs[:arrays])
    psf_const = psf_at(*refs[arrays:-2])
    objects_out, phase_out = refs[-2:]
    half = phase.shape[0] // 2
    first, second = halo_rows(mine[:half], theirs[:half])
    slope = jnp.concatenate([first, second], 0)
    summed = squares[...]
    mean_square = total(summed) * (1.0 / cells)
    updated = phase[...] - STEP_SIZE * slope / jnp.sqrt(mean_square + EPSILON)
    phase_out[...] = updated
    _, _, spec, _ = point_spread(updated, amplitude[...], psf_const)
    spec_even, spec_odd = spec[:, :cols], spec[:, cols:]
    freqs = spec.shape[0]
    pairs = range(0, even.shape[0], 2 * freqs)
    light = inverse(
        times([even[top : top + 2 * freqs] for top in pairs], spec_even, False),
        times([odd[top : top + 2 * freqs] for top in pairs], spec_odd, False),
        freqs, const,
    )
    ratios = []
    for p in range(planes):
        above, below = halo_rows(far_chip[planes + p], far_core[planes + p])
        blurred = jnp.concatenate(light[2 * p : 2 * p + 2], 0) + BACKGROUND
        ratios.append(jnp.concatenate([above, observed[p], below], 0) / blurred)
    ratio_even, ratio_odd = forward(ratios, const["row_forward"], const)
    correction = inverse(times(ratio_even, spec_even, True), times(ratio_odd, spec_odd, True), freqs, const)
    for p in range(planes):
        objects_out[p] = own[p] * correction[p]


def call(kernel, out_shapes, args, flops=10**6, spaces=None, scratch=()):
    outs = [
        jax.ShapeDtypeStruct(shape, jnp.float32) if isinstance(shape, tuple) else shape for shape in out_shapes
    ]
    spaces = spaces or {}
    return pl.pallas_call(
        kernel,
        out_shape=outs,
        in_specs=[pl.BlockSpec(memory_space=spaces.get(i, pltpu.VMEM)) for i in range(len(args))],
        out_specs=[pl.BlockSpec(memory_space=pltpu.VMEM)] * len(outs),
        scratch_shapes=scratch,
        compiler_params=pltpu.CompilerParams(vmem_limit_bytes=VMEM_LIMIT),
        cost_estimate=pl.CostEstimate(flops=flops, bytes_accessed=10**5, transcendentals=0),
    )(*args)


def swap(chip_rows, core_rows):
    count = lax.axis_size("tile")
    chip_pairs = [(i, (i + 1 if i % 2 else i - 1) % count) for i in range(count)]
    return lax.ppermute(chip_rows, "tile", chip_pairs), exchange(core_rows, 1)


def exchange(value, step):
    return lax.ppermute(value, "tile", [(i, i ^ step) for i in range(lax.axis_size("tile"))])


def across_depth_and_chip(value):
    pairs = [(2 * t + d, 2 * (t ^ 2) + 1 - d) for t in range(lax.axis_size("tile")) for d in range(2)]
    return lax.ppermute(value, ("tile", "depth"), pairs)


def sum_over_depth(value):
    count = lax.axis_size("depth")
    if count & (count - 1):
        return lax.psum(value, "depth")
    for bit in range(count.bit_length() - 1):
        value = value + lax.ppermute(value, "depth", [(i, i ^ (1 << bit)) for i in range(count)])
    return value


def on_device(objects, observed, pupil_phase, pupil_amplitude):
    picture, measured, phase, amplitude = objects[0], observed[0], pupil_phase[0], pupil_amplitude[0]
    planes, rows, cols = picture.shape
    pup = phase.shape[0]
    count = lax.axis_size("tile")
    ker = 2 * HALF + 1
    length = rows + 2 * HALF
    pad_rows, pad_cols = round_up(ker, 16), round_up(ker, 128)
    row_forward, row_inverse = row_constants(rows, length)
    col_forward, col_inverse = col_constants(cols)
    kernel_rows, kernel_right = kernel_constants(length, cols, ker, pad_rows, pad_cols)
    pupil_left, pupil_right = pupil_constants(pup, ker, pad_rows, pad_cols)
    psf_const = Joined(
        {"pupil_left": pupil_left, "kernel_rows": kernel_rows},
        {"pupil_right": pupil_right, "kernel_right": kernel_right},
    )
    block_left = {"row_forward": row_forward, "row_inverse": row_inverse}
    block_right = {
        "forward_even": col_forward[0],
        "forward_odd": col_forward[1],
        "inverse_even": col_inverse[0],
        "inverse_odd": col_inverse[1],
    }
    block_const = Joined(block_left, block_right)
    lag_const = Joined(
        {
            "row_own": row_forward[:, HALF : HALF + rows],
            "lag_left": kernel_rows.T * (2.0 / length),
            "adjoint_left": pupil_left.T,
        },
        {"lag_right": kernel_right.T / cols, "adjoint_right": pupil_right.T},
    )
    psf_arrays, block_arrays, lag_arrays = (
        [jnp.asarray(array) for array in const.arrays] for const in (psf_const, block_const, lag_const)
    )

    def gradient_at(*refs):
        held = len(block_arrays)
        return {**block_const.at(*refs[:held]), **lag_const.at(*refs[held:])}

    in_hbm = [
        pltpu.with_memory_space_constraint(value, pltpu.HBM)
        for value in (phase, amplitude, picture, measured, *psf_arrays)
    ]
    edge = (planes, HALF, cols)
    chip_rows, core_rows = call(near_kernel, [edge] * 2, in_hbm[2:3], scratch=[pltpu.SemaphoreType.DMA((2,))], spaces={0: pltpu.HBM})
    from_chip, from_core = swap(chip_rows, core_rows)
    pupil, field, spec, far_chip, far_core, *psf_arrays = call(
        functools.partial(first_kernel, at=psf_const.at, arrays=len(psf_arrays)),
        [(pup, 2 * pup), (2 * pad_rows, pad_cols), (length // 2, 2 * cols)]
        + [(2 * planes, HALF, cols)] * 2
        + psf_arrays,
        (*in_hbm, chip_rows),
        flops=3 * 10**9,
        spaces={**dict.fromkeys(range(len(in_hbm)), pltpu.HBM), len(in_hbm): pl.ANY},
        scratch=[pltpu.VMEM(phase.shape, jnp.float32)] * 2 + [pltpu.SemaphoreType.DMA((6 + len(psf_arrays),))],
    )
    far_chip, far_core, from_chip, from_core = lax.optimization_barrier((far_chip, far_core, from_chip, from_core))
    far_chip, far_core = swap(far_chip, far_core)
    keep, give = call(
        functools.partial(gradient_kernel, at=gradient_at),
        [(pup // 2, pup)] * 2,
        (from_chip, from_core, picture, measured, spec, pupil, field, *block_arrays, *lag_arrays),
        flops=4 * 10**10,
    )
    half = keep + exchange(give, 1)
    bits = list(range(2, count.bit_length() - 1))
    for low, high in zip(bits[::2], bits[1::2]):
        half = half + ((exchange(half, 1 << low) + exchange(half, 1 << high)) + exchange(half, (1 << low) | (1 << high)))
    if len(bits) % 2:
        half = half + exchange(half, 1 << bits[-1])
    last_round = [exchange(half, 2)]
    two_strata = lax.axis_size("depth") == 2
    if two_strata:
        last_round += [lax.ppermute(half, "depth", [(0, 1), (1, 0)]), across_depth_and_chip(half)]
    even, odd = call(
        functools.partial(blocks_kernel, at=block_const.at),
        [(planes * length, cols)] * 2,
        (from_chip, from_core, picture, far_chip, far_core, half, *block_arrays),
        spaces={5: pl.ANY},
    )
    even, *last_round = lax.optimization_barrier((even, *last_round))
    (joined,) = call(squares_kernel, [(pup // 2 + 8, pup)], (half, *last_round))
    other = exchange(joined, 1)
    squares = joined[pup // 2 :] + other[pup // 2 :]
    if not two_strata:
        squares = sum_over_depth(squares)
    new_objects, new_phase = call(
        functools.partial(
            second_kernel,
            at=block_const.at,
            psf_at=psf_const.at,
            arrays=len(block_arrays),
            cells=lax.axis_size("depth") * pup * pup,
        ),
        [picture.shape, phase.shape],
        (
            phase, amplitude, joined, other, squares, even, odd, picture, measured,
            far_chip, far_core, *block_arrays, *psf_arrays,
        ),
    )
    return new_objects[None], new_phase[None]


def solution(mesh):
    return jax.shard_map(
        on_device,
        mesh=mesh,
        in_specs=(
            P("depth", None, "tile", None),
            P("depth", None, "tile", None),
            P("depth", None, None),
            P("depth", None, None),
        ),
        out_specs=(P("depth", None, "tile", None), P("depth", None, None)),
        check_vma=False,
    )
```

```python
import functools
import math

import jax
import jax.numpy as jnp
import ml_dtypes
import numpy as np
from jax import lax
from jax.experimental import pallas as pl
from jax.experimental.pallas import tpu as pltpu
from jax.sharding import PartitionSpec as P

HALF = 64
BACKGROUND = 0.1
STEP_SIZE = 0.3
EPSILON = 1e-06
NEEDED_IN_ORDER = ("pupil_right", "pupil_left", "kernel_right")
VMEM_LIMIT = 32 * 1024 * 1024


def round_up(value, step):
    return -(-value // step) * step


def angles(left, right, length):
    return (2.0 * math.pi / length) * np.outer(left, right)


def halves(matrix):
    high = matrix.astype(np.float32).astype(ml_dtypes.bfloat16)
    low = (matrix - high.astype(np.float64)).astype(np.float32).astype(ml_dtypes.bfloat16)
    return high, low


def row_constants(rows, length):
    freqs = np.arange(length // 2) + 0.5
    theta = angles(freqs, np.arange(length), length)
    forward = np.concatenate([np.cos(theta), -np.sin(theta)], 0)
    inner = theta[:, HALF : HALF + rows]
    inverse = np.concatenate([np.cos(inner).T, -np.sin(inner).T], 1) * (2.0 / length)
    return forward, inverse


def col_constants(cols):
    half = cols // 2
    forward, inverse = [], []
    for parity in range(2):
        theta = angles(np.arange(half), 2 * np.arange(half) + parity, cols)
        c, s = np.cos(theta), np.sin(theta)
        forward.append(np.block([[c, -s], [s, c]]))
        inverse.append(np.block([[c.T, s.T], [-s.T, c.T]]) / cols)
    return forward, inverse


def kernel_constants(length, cols, ker, pad_rows, pad_cols):
    lags = np.arange(ker) - HALF
    theta = angles(np.arange(length // 2) + 0.5, lags, length)
    rows = np.zeros((length, pad_rows))
    rows[: length // 2, :ker] = np.cos(theta)
    rows[length // 2 :, :ker] = -np.sin(theta)
    half = cols // 2
    right = np.zeros((2 * pad_cols, 2 * cols))
    for parity in range(2):
        theta = angles(lags, 2 * np.arange(half) + parity, cols)
        c, s = np.cos(theta), np.sin(theta)
        at = parity * cols
        right[:ker, at : at + half] = c
        right[:ker, at + half : at + cols] = -s
        right[pad_cols : pad_cols + ker, at : at + half] = s
        right[pad_cols : pad_cols + ker, at + half : at + cols] = c
    return rows, right


def pupil_constants(pup, ker, pad_rows, pad_cols):
    theta = angles(np.arange(ker) - HALF, np.arange(pup), ker)
    real, imag = np.cos(theta), -np.sin(theta)
    right = np.zeros((2 * pup, 2 * pad_cols))
    right[:pup, :ker] = real.T
    right[:pup, pad_cols : pad_cols + ker] = imag.T
    right[pup:, :ker] = -imag.T
    right[pup:, pad_cols : pad_cols + ker] = real.T
    left = np.zeros((2 * pad_rows, 2 * pup))
    left[:ker, :pup] = real
    left[:ker, pup:] = -imag
    left[pad_rows : pad_rows + ker, :pup] = imag
    left[pad_rows : pad_rows + ker, pup:] = real
    return left, right


class Joined:
    def __init__(self, left, right):
        self.places, groups = {}, {}
        for name, matrix in right.items():
            high, low = halves(matrix)
            groups.setdefault(matrix.shape[0], []).append((name, np.concatenate([high, high, low], 0)))
        for name, matrix in left.items():
            high, low = halves(matrix)
            groups.setdefault("left", []).append((name, np.concatenate([high, low, high], 1)))
        self.arrays = []
        for kind, members in groups.items():
            at = 0
            for name, block in members:
                rows, cols = block.shape
                start = (at, 0) if kind == "left" else (0, at)
                self.places[name] = (len(self.arrays), *start, rows, cols)
                at += rows if kind == "left" else cols
            blocks = [block for _, block in members]
            if kind == "left":
                width = max(block.shape[1] for block in blocks)
                blocks = [np.pad(block, ((0, 0), (0, width - block.shape[1]))) for block in blocks]
            self.arrays.append(np.concatenate(blocks, 0 if kind == "left" else 1))

    def at(self, *refs):
        return {
            name: refs[which].at[top : top + rows, first : first + cols]
            for name, (which, top, first, rows, cols) in self.places.items()
        }


def dot(left, right):
    return jnp.dot(left, right, preferred_element_type=jnp.float32)


def split(value):
    high = value.astype(jnp.bfloat16)
    low = (value - high.astype(jnp.float32)).astype(jnp.bfloat16)
    return high, low


def left_by(const, value):
    high, low = split(value)
    return dot(const[...], jnp.concatenate([high, high, low], 0))


def right_by(value, const):
    high, low = split(value)
    return dot(jnp.concatenate([high, low, high], 1), const[...])


def sine_cosine(angle):
    turns = jnp.floor(angle * (2.0 / math.pi) + 0.5)
    rest = angle - turns * 1.5703125
    rest = rest - turns * 4.837512969970703e-4
    rest = rest - turns * 7.54978995489e-8
    square = rest * rest
    sine = rest + rest * square * (
        -1.6666654611e-1 + square * (8.3321608736e-3 + square * -1.9515295891e-4)
    )
    cosine = 1.0 - 0.5 * square + square * square * (
        4.166664568298827e-2 + square * (-1.388731625493765e-3 + square * 2.443315711809948e-5)
    )
    quadrant = turns.astype(jnp.int32) & 3
    swap = (quadrant & 1) == 1
    sine_out = jnp.where(swap, cosine, sine)
    cosine_out = jnp.where(swap, sine, cosine)
    sine_out = jnp.where(quadrant >= 2, -sine_out, sine_out)
    cosine_out = jnp.where((quadrant == 1) | (quadrant == 2), -cosine_out, cosine_out)
    return sine_out, cosine_out


def total(value):
    return jnp.sum(jnp.sum(value, axis=0, keepdims=True), axis=1, keepdims=True)


def weights(amplitude):
    pup = amplitude.shape[0]
    rows = lax.broadcasted_iota(jnp.int32, amplitude.shape, 0).astype(jnp.float32) - (pup - 1) / 2.0
    cols = lax.broadcasted_iota(jnp.int32, amplitude.shape, 1).astype(jnp.float32) - (pup - 1) / 2.0
    return jnp.where(rows * rows + cols * cols <= (pup / 2.0) ** 2, amplitude, 0.0)


def point_spread(phase, amplitude, const, wait_for=lambda name: None):
    weight = weights(amplitude)
    sine, cosine = sine_cosine(phase)
    pupil = jnp.concatenate([weight * cosine, weight * sine], 1)
    wait_for("pupil_right")
    across = right_by(pupil, const["pupil_right"])
    cols = across.shape[1] // 2
    wait_for("pupil_left")
    field = left_by(const["pupil_left"], jnp.concatenate([across[:, :cols], across[:, cols:]], 0))
    rows = field.shape[0] // 2
    intensity = field[:rows] * field[:rows] + field[rows:] * field[rows:]
    norm = 1.0 / total(intensity)
    left = left_by(const["kernel_rows"], intensity)
    freqs = left.shape[0] // 2
    wait_for("kernel_right")
    spectrum = right_by(jnp.concatenate([left[:freqs], left[freqs:]], 1), const["kernel_right"])
    return pupil, field, spectrum * norm, norm


def forward(strips, row_matrix, const):
    sums, differences = [], []
    for strip in strips:
        half = strip.shape[1] // 2
        first, second = strip[:, :half], strip[:, half:]
        mixed = left_by(row_matrix, jnp.concatenate([first + second, first - second], 1))
        freqs = mixed.shape[0] // 2
        sums.append(jnp.concatenate([mixed[:freqs, :half], mixed[freqs:, :half]], 1))
        differences.append(jnp.concatenate([mixed[:freqs, half:], mixed[freqs:, half:]], 1))
    even = [right_by(jnp.concatenate(sums[p : p + 2], 0), const["forward_even"]) for p in range(0, len(sums), 2)]
    odd = [right_by(jnp.concatenate(differences[p : p + 2], 0), const["forward_odd"]) for p in range(0, len(sums), 2)]
    return even, odd


def inverse(even, odd, freqs, const):
    even = [right_by(spectrum, const["inverse_even"]) for spectrum in even]
    odd = [right_by(spectrum, const["inverse_odd"]) for spectrum in odd]
    strips = []
    for sums, differences in zip(even, odd):
        half = sums.shape[1] // 2
        for top in range(0, sums.shape[0], freqs):
            rows = slice(top, top + freqs)
            stacked = jnp.concatenate(
                [
                    jnp.concatenate([sums[rows, :half], differences[rows, :half]], 1),
                    jnp.concatenate([sums[rows, half:], differences[rows, half:]], 1),
                ],
                0,
            )
            mixed = left_by(const["row_inverse"], stacked)
            first, second = mixed[:, :half], mixed[:, half:]
            strips.append(jnp.concatenate([first + second, first - second], 1))
    return strips


def times(spectra, other, conjugate):
    half = other.shape[1] // 2
    products = []
    for spectrum in spectra:
        planes = spectrum.shape[0] // other.shape[0]
        real = jnp.concatenate([other[:, :half]] * planes, 0)
        imag = jnp.concatenate([other[:, half:]] * planes, 0)
        left, right = spectrum[:, :half], spectrum[:, half:]
        if conjugate:
            product = [left * real + right * imag, right * real - left * imag]
        else:
            product = [left * real - right * imag, left * imag + right * real]
        products.append(jnp.concatenate(product, 1))
    return products


def cross(firsts, seconds, freqs):
    summed = None
    for first, second in zip(firsts, seconds):
        half = first.shape[1] // 2
        left, right = first[:, :half], first[:, half:]
        real, imag = second[:, :half], second[:, half:]
        both = jnp.concatenate([left * real + right * imag, right * real - left * imag], 1)
        for top in range(0, both.shape[0], freqs):
            summed = both[top : top + freqs] if summed is None else summed + both[top : top + freqs]
    return summed


def is_even():
    return lax.axis_index("tile") % 2 == 0


def edge_rows(top, bottom):
    even = is_even()
    return [pl.multiple_of(jnp.where(even, *choice), 8) for choice in ((top, bottom), (bottom, top))]


def run_all(copies):
    for copy in copies:
        copy.start()
    for copy in copies:
        copy.wait()


def near_kernel(own, chip_out, core_out, sems):
    chip, core = edge_rows(0, own.shape[1] - HALF)
    run_all([
        pltpu.make_async_copy(own.at[:, pl.ds(chip, HALF), :], chip_out, sems.at[0]),
        pltpu.make_async_copy(own.at[:, pl.ds(core, HALF), :], core_out, sems.at[1]),
    ])


def first_kernel(
    phase, amplitude, own, observed, *refs, at, places, arrays,
):
    psf_refs, (_, pupil_out, field_out, spec_out, chip_out, core_out, token_out) = refs[:arrays], refs[arrays : arrays + 7]
    psf_outs, (phase_in, amplitude_in, sems) = refs[arrays + 7 : -3], refs[-3:]
    planes, rows, _ = own.shape
    objects_chip, objects_core = edge_rows(HALF, rows - 2 * HALF)
    observed_chip, observed_core = edge_rows(0, rows - HALF)
    pairs = [
        (phase, phase_in),
        (amplitude, amplitude_in),
        *zip(psf_refs, psf_outs),
        (own.at[:, pl.ds(objects_chip, HALF), :], chip_out.at[:planes]),
        (observed.at[:, pl.ds(observed_chip, HALF), :], chip_out.at[planes:]),
        (own.at[:, pl.ds(objects_core, HALF), :], core_out.at[:planes]),
        (observed.at[:, pl.ds(observed_core, HALF), :], core_out.at[planes:]),
    ]
    copies = [pltpu.make_async_copy(source, target, sems.at[i]) for i, (source, target) in enumerate(pairs)]
    for i in (0, 1, *(2 + places[name][0] for name in NEEDED_IN_ORDER), *range(2 + arrays, len(copies))):
        copies[i].start()
    for copy in copies[:2]:
        copy.wait()

    def wait_for(name):
        copies[2 + places[name][0]].wait()

    pupil, field, spectrum, norm = point_spread(phase_in[...], amplitude_in[...], at(*psf_outs), wait_for)
    root = jnp.sqrt(norm)
    pupil_out[...] = pupil * root
    field_out[...] = field * root
    spec_out[...] = spectrum
    token_out[...] = jnp.zeros_like(token_out)
    for copy in copies[2 + arrays :]:
        copy.wait()


def halo_rows(chip, core):
    even = is_even()
    return jnp.where(even, chip, core), jnp.where(even, core, chip)


def gradient_kernel(
    from_chip, from_core, own, observed, spec, pupil, field, _, *refs, at,
):
    planes, rows, cols = own.shape
    const = at(*refs[:-2])
    keep_out, give_out = refs[-2:]
    freqs = spec.shape[0]
    strips = []
    for p in range(planes):
        above, below = halo_rows(from_chip[p], from_core[p])
        strips.append(jnp.concatenate([above, own[p], below], 0))
    even, odd = forward(strips, const["row_forward"], const)
    blurred = inverse(times(even, spec[:, :cols], False), times(odd, spec[:, cols:], False), freqs, const)
    misfit = [1.0 - observed[p] / (blurred[p] + BACKGROUND) for p in range(planes)]
    misfit_even, misfit_odd = forward(misfit, const["row_own"], const)
    shared = jnp.concatenate([cross(misfit_even, even, freqs), cross(misfit_odd, odd, freqs)], 1)
    across = right_by(shared, const["lag_right"])
    pad_cols = across.shape[1] // 2
    psf_grad = left_by(const["lag_left"], jnp.concatenate([across[:, :pad_cols], across[:, pad_cols:]], 0))
    far = field[...]
    pad_rows = far.shape[0] // 2
    real, imag = far[:pad_rows], far[pad_rows:]
    centred = 2.0 * (psf_grad - total(psf_grad * (real * real + imag * imag)))
    back = left_by(const["adjoint_left"], jnp.concatenate([centred * real, centred * imag], 0))
    pup = back.shape[0] // 2
    back = right_by(jnp.concatenate([back[:pup], back[pup:]], 1), const["adjoint_right"])
    near = pupil[...]
    slope = back[:, pup:] * near[:, :pup] - back[:, :pup] * near[:, pup:]
    even_core = is_even()
    keep_out[...] = jnp.where(even_core, slope[: pup // 2], slope[pup // 2 :])
    give_out[...] = jnp.where(even_core, slope[pup // 2 :], slope[: pup // 2])


def square_sums(value):
    rows = value.shape[0]
    squared = value * value
    summed = squared[:8]
    for top in range(8, rows, 8):
        summed = summed + squared[top : top + 8]
    return summed


def squares_kernel(mine, received, *others):
    joined_out = others[-1]
    half = mine[...] + received[...]
    squares = square_sums(half)
    for first, second in zip(others[:-1:2], others[1:-1:2]):
        squares = squares + square_sums(first[...] + second[...])
    joined_out[: half.shape[0]] = half
    joined_out[half.shape[0] :] = squares


def blocks_kernel(from_chip, from_core, own, far_chip, far_core, _, *refs, at):
    planes = own.shape[0]
    const = at(*refs[:-2])
    even_out, odd_out = refs[-2:]
    strips = []
    for p in range(planes):
        above, below = halo_rows(from_chip[p], from_core[p])
        far_above, far_below = halo_rows(far_chip[p], far_core[p])
        strips.append(jnp.concatenate([far_above, above, own[p]], 0))
        strips.append(jnp.concatenate([own[p], below, far_below], 0))
    even, odd = forward(strips, const["row_forward"], const)
    even_out[...] = jnp.concatenate(even, 0)
    odd_out[...] = jnp.concatenate(odd, 0)


def second_kernel(
    phase, amplitude, mine, theirs, squares, even, odd, own, observed, far_chip, far_core,
    *refs, at, psf_at, arrays, cells,
):
    planes, rows, cols = own.shape
    const = at(*refs[:arrays])
    psf_const = psf_at(*refs[arrays:-2])
    objects_out, phase_out = refs[-2:]
    half = phase.shape[0] // 2
    first, second = halo_rows(mine[:half], theirs[:half])
    slope = jnp.concatenate([first, second], 0)
    summed = squares[...]
    mean_square = total(summed) * (1.0 / cells)
    updated = phase[...] - STEP_SIZE * slope / jnp.sqrt(mean_square + EPSILON)
    phase_out[...] = updated
    _, _, spec, _ = point_spread(updated, amplitude[...], psf_const)
    spec_even, spec_odd = spec[:, :cols], spec[:, cols:]
    freqs = spec.shape[0]
    pairs = range(0, even.shape[0], 2 * freqs)
    light = inverse(
        times([even[top : top + 2 * freqs] for top in pairs], spec_even, False),
        times([odd[top : top + 2 * freqs] for top in pairs], spec_odd, False),
        freqs, const,
    )
    ratios = []
    for p in range(planes):
        above, below = halo_rows(far_chip[planes + p], far_core[planes + p])
        blurred = jnp.concatenate(light[2 * p : 2 * p + 2], 0) + BACKGROUND
        ratios.append(jnp.concatenate([above, observed[p], below], 0) / blurred)
    ratio_even, ratio_odd = forward(ratios, const["row_forward"], const)
    correction = inverse(times(ratio_even, spec_even, True), times(ratio_odd, spec_odd, True), freqs, const)
    for p in range(planes):
        objects_out[p] = own[p] * correction[p]


def call(kernel, out_shapes, args, flops=10**6, spaces=None, scratch=()):
    outs = [
        jax.ShapeDtypeStruct(shape, jnp.float32) if isinstance(shape, tuple) else shape for shape in out_shapes
    ]
    spaces = spaces or {}
    return pl.pallas_call(
        kernel,
        out_shape=outs,
        in_specs=[pl.BlockSpec(memory_space=spaces.get(i, pltpu.VMEM)) for i in range(len(args))],
        out_specs=[pl.BlockSpec(memory_space=pltpu.VMEM)] * len(outs),
        scratch_shapes=scratch,
        compiler_params=pltpu.CompilerParams(vmem_limit_bytes=VMEM_LIMIT),
        cost_estimate=pl.CostEstimate(flops=flops, bytes_accessed=10**5, transcendentals=0),
    )(*args)


def to_next_chip(value):
    count = lax.axis_size("tile")
    return lax.ppermute(value, "tile", [(i, (i + 1 if i % 2 else i - 1) % count) for i in range(count)])


def exchange(value, step):
    return lax.ppermute(value, "tile", [(i, i ^ step) for i in range(lax.axis_size("tile"))])


def across_depth_and_chip(value):
    pairs = [(2 * t + d, 2 * (t ^ 2) + 1 - d) for t in range(lax.axis_size("tile")) for d in range(2)]
    return lax.ppermute(value, ("tile", "depth"), pairs)


def sum_over_depth(value):
    count = lax.axis_size("depth")
    if count & (count - 1):
        return lax.psum(value, "depth")
    for bit in range(count.bit_length() - 1):
        value = value + lax.ppermute(value, "depth", [(i, i ^ (1 << bit)) for i in range(count)])
    return value


def on_device(objects, observed, pupil_phase, pupil_amplitude):
    picture, measured, phase, amplitude = objects[0], observed[0], pupil_phase[0], pupil_amplitude[0]
    planes, rows, cols = picture.shape
    pup = phase.shape[0]
    count = lax.axis_size("tile")
    ker = 2 * HALF + 1
    length = rows + 2 * HALF
    pad_rows, pad_cols = round_up(ker, 16), round_up(ker, 128)
    row_forward, row_inverse = row_constants(rows, length)
    col_forward, col_inverse = col_constants(cols)
    kernel_rows, kernel_right = kernel_constants(length, cols, ker, pad_rows, pad_cols)
    pupil_left, pupil_right = pupil_constants(pup, ker, pad_rows, pad_cols)
    psf_const = Joined(
        {"pupil_left": pupil_left, "kernel_rows": kernel_rows},
        {"pupil_right": pupil_right, "kernel_right": kernel_right},
    )
    block_left = {"row_forward": row_forward, "row_inverse": row_inverse}
    block_right = {
        "forward_even": col_forward[0],
        "forward_odd": col_forward[1],
        "inverse_even": col_inverse[0],
        "inverse_odd": col_inverse[1],
    }
    block_const = Joined(block_left, block_right)
    lag_const = Joined(
        {
            "row_own": row_forward[:, HALF : HALF + rows],
            "lag_left": kernel_rows.T * (2.0 / length),
            "adjoint_left": pupil_left.T,
        },
        {"lag_right": kernel_right.T / cols, "adjoint_right": pupil_right.T},
    )
    psf_arrays, block_arrays, lag_arrays = (
        [jnp.asarray(array) for array in const.arrays] for const in (psf_const, block_const, lag_const)
    )

    def gradient_at(*refs):
        held = len(block_arrays)
        return {**block_const.at(*refs[:held]), **lag_const.at(*refs[held:])}

    in_hbm = [
        pltpu.with_memory_space_constraint(value, pltpu.HBM)
        for value in (phase, amplitude, picture, measured, *psf_arrays)
    ]
    edge = (planes, HALF, cols)
    chip_rows, core_rows = call(near_kernel, [edge] * 2, in_hbm[2:3], scratch=[pltpu.SemaphoreType.DMA((2,))], spaces={0: pltpu.HBM})
    from_chip, from_core = to_next_chip(chip_rows), exchange(core_rows, 1)
    pupil, field, spec, far_chip, far_core, token, *psf_arrays = call(
        functools.partial(first_kernel, at=psf_const.at, places=psf_const.places, arrays=len(psf_arrays)),
        [(pup, 2 * pup), (2 * pad_rows, pad_cols), (length // 2, 2 * cols)]
        + [(2 * planes, HALF, cols)] * 2
        + [(8, 128)]
        + psf_arrays,
        (*in_hbm, chip_rows),
        flops=3 * 10**9,
        spaces={**dict.fromkeys(range(len(in_hbm)), pltpu.HBM), len(in_hbm): pl.ANY},
        scratch=[pltpu.VMEM(phase.shape, jnp.float32)] * 2 + [pltpu.SemaphoreType.DMA((6 + len(psf_arrays),))],
    )
    far_core = exchange(far_core, 1)
    far_chip, token = lax.optimization_barrier((far_chip, exchange(token, 1)))
    far_chip = to_next_chip(far_chip)
    keep, give = call(
        functools.partial(gradient_kernel, at=gradient_at),
        [(pup // 2, pup)] * 2,
        (from_chip, from_core, picture, measured, spec, pupil, field, token, *block_arrays, *lag_arrays),
        flops=4 * 10**10,
        spaces={7: pl.ANY},
    )
    half = keep + exchange(give, 1)
    bits = list(range(2, count.bit_length() - 1))
    for low, high in zip(bits[::2], bits[1::2]):
        half = half + ((exchange(half, 1 << low) + exchange(half, 1 << high)) + exchange(half, (1 << low) | (1 << high)))
    if len(bits) % 2:
        half = half + exchange(half, 1 << bits[-1])
    last_round = [exchange(half, 2)]
    two_strata = lax.axis_size("depth") == 2
    if two_strata:
        last_round += [lax.ppermute(half, "depth", [(0, 1), (1, 0)]), across_depth_and_chip(half)]
    even, odd = call(
        functools.partial(blocks_kernel, at=block_const.at),
        [(planes * length, cols)] * 2,
        (from_chip, from_core, picture, far_chip, far_core, half, *block_arrays),
        spaces={5: pl.ANY},
    )
    even, *last_round = lax.optimization_barrier((even, *last_round))
    (joined,) = call(squares_kernel, [(pup // 2 + 8, pup)], (half, *last_round))
    other = exchange(joined, 1)
    squares = joined[pup // 2 :] + other[pup // 2 :]
    if not two_strata:
        squares = sum_over_depth(squares)
    new_objects, new_phase = call(
        functools.partial(
            second_kernel,
            at=block_const.at,
            psf_at=psf_const.at,
            arrays=len(block_arrays),
            cells=lax.axis_size("depth") * pup * pup,
        ),
        [picture.shape, phase.shape],
        (
            phase, amplitude, joined, other, squares, even, odd, picture, measured,
            far_chip, far_core, *block_arrays, *psf_arrays,
        ),
    )
    return new_objects[None], new_phase[None]


def solution(mesh):
    return jax.shard_map(
        on_device,
        mesh=mesh,
        in_specs=(
            P("depth", None, "tile", None),
            P("depth", None, "tile", None),
            P("depth", None, None),
            P("depth", None, None),
        ),
        out_specs=(P("depth", None, "tile", None), P("depth", None, None)),
        check_vma=False,
    )
```

```python
import functools
import math

import jax
import jax.numpy as jnp
import ml_dtypes
import numpy as np
from jax import lax
from jax.experimental import pallas as pl
from jax.experimental.pallas import tpu as pltpu
from jax.sharding import PartitionSpec as P

HALF = 64
BACKGROUND = 0.1
STEP_SIZE = 0.3
EPSILON = 1e-06
STACKED = ("row_inverse",)
NEEDED_IN_ORDER = ("pupil_right", "pupil_left", "kernel_right")
VMEM_LIMIT = 32 * 1024 * 1024


def round_up(value, step):
    return -(-value // step) * step


def angles(left, right, length):
    return (2.0 * math.pi / length) * np.outer(left, right)


def halves(matrix):
    high = matrix.astype(np.float32).astype(ml_dtypes.bfloat16)
    low = (matrix - high.astype(np.float64)).astype(np.float32).astype(ml_dtypes.bfloat16)
    return high, low


def row_constants(rows, length):
    freqs = np.arange(length // 2) + 0.5
    theta = angles(freqs, np.arange(length), length)
    forward = np.concatenate([np.cos(theta), -np.sin(theta)], 0)
    inner = theta[:, HALF : HALF + rows]
    inverse = np.concatenate([np.cos(inner).T, -np.sin(inner).T], 1) * (2.0 / length)
    return forward, inverse


def col_constants(cols):
    half = cols // 2
    forward, inverse = [], []
    for parity in range(2):
        theta = angles(np.arange(half), 2 * np.arange(half) + parity, cols)
        c, s = np.cos(theta), np.sin(theta)
        forward.append(np.block([[c, -s], [s, c]]))
        inverse.append(np.block([[c.T, s.T], [-s.T, c.T]]) / cols)
    return forward, inverse


def kernel_constants(length, cols, ker, pad_rows, pad_cols):
    lags = np.arange(ker) - HALF
    theta = angles(np.arange(length // 2) + 0.5, lags, length)
    rows = np.zeros((length, pad_rows))
    rows[: length // 2, :ker] = np.cos(theta)
    rows[length // 2 :, :ker] = -np.sin(theta)
    half = cols // 2
    right = np.zeros((2 * pad_cols, 2 * cols))
    for parity in range(2):
        theta = angles(lags, 2 * np.arange(half) + parity, cols)
        c, s = np.cos(theta), np.sin(theta)
        at = parity * cols
        right[:ker, at : at + half] = c
        right[:ker, at + half : at + cols] = -s
        right[pad_cols : pad_cols + ker, at : at + half] = s
        right[pad_cols : pad_cols + ker, at + half : at + cols] = c
    return rows, right


def pupil_constants(pup, ker, pad_rows, pad_cols):
    theta = angles(np.arange(ker) - HALF, np.arange(pup), ker)
    real, imag = np.cos(theta), -np.sin(theta)
    right = np.zeros((2 * pup, 2 * pad_cols))
    right[:pup, :ker] = real.T
    right[:pup, pad_cols : pad_cols + ker] = imag.T
    right[pup:, :ker] = -imag.T
    right[pup:, pad_cols : pad_cols + ker] = real.T
    left = np.zeros((2 * pad_rows, 2 * pup))
    left[:ker, :pup] = real
    left[:ker, pup:] = -imag
    left[pad_rows : pad_rows + ker, :pup] = imag
    left[pad_rows : pad_rows + ker, pup:] = real
    return left, right


class Joined:
    def __init__(self, left, right):
        self.places, groups = {}, {}
        for name, matrix in right.items():
            high, low = halves(matrix)
            groups.setdefault(matrix.shape[0], []).append((name, np.concatenate([high, high, low], 0)))
        for name, matrix in left.items():
            high, low = halves(matrix)
            held = np.concatenate([high, low], 0) if name in STACKED else np.concatenate([high, low, high], 1)
            groups.setdefault("left", []).append((name, held))
        self.arrays = []
        for kind, members in groups.items():
            at = 0
            for name, block in members:
                rows, cols = block.shape
                start = (at, 0) if kind == "left" else (0, at)
                self.places[name] = (len(self.arrays), *start, rows, cols)
                at += rows if kind == "left" else cols
            blocks = [block for _, block in members]
            if kind == "left":
                width = max(block.shape[1] for block in blocks)
                blocks = [np.pad(block, ((0, 0), (0, width - block.shape[1]))) for block in blocks]
            self.arrays.append(np.concatenate(blocks, 0 if kind == "left" else 1))

    def at(self, *refs):
        return {
            name: refs[which].at[top : top + rows, first : first + cols]
            for name, (which, top, first, rows, cols) in self.places.items()
        }


def dot(left, right):
    return jnp.dot(left, right, preferred_element_type=jnp.float32)


def split(value):
    high = value.astype(jnp.bfloat16)
    low = (value - high.astype(jnp.float32)).astype(jnp.bfloat16)
    return high, low


def left_by(const, value):
    high, low = split(value)
    return dot(const[...], jnp.concatenate([high, high, low], 0))


def left_stacked(const, value):
    high, low = split(value)
    rows = const.shape[0] // 2
    both = dot(const[...], high)
    return both[:rows] + (both[rows:] + dot(const[:rows], low))


def right_by(value, const):
    high, low = split(value)
    return dot(jnp.concatenate([high, low, high], 1), const[...])


def sine_cosine(angle):
    turns = jnp.floor(angle * (2.0 / math.pi) + 0.5)
    rest = angle - turns * 1.5703125
    rest = rest - turns * 4.837512969970703e-4
    rest = rest - turns * 7.54978995489e-8
    square = rest * rest
    sine = rest + rest * square * (
        -1.6666654611e-1 + square * (8.3321608736e-3 + square * -1.9515295891e-4)
    )
    cosine = 1.0 - 0.5 * square + square * square * (
        4.166664568298827e-2 + square * (-1.388731625493765e-3 + square * 2.443315711809948e-5)
    )
    quadrant = turns.astype(jnp.int32) & 3
    swap = (quadrant & 1) == 1
    sine_out = jnp.where(swap, cosine, sine)
    cosine_out = jnp.where(swap, sine, cosine)
    sine_out = jnp.where(quadrant >= 2, -sine_out, sine_out)
    cosine_out = jnp.where((quadrant == 1) | (quadrant == 2), -cosine_out, cosine_out)
    return sine_out, cosine_out


def total(value):
    return jnp.sum(jnp.sum(value, axis=0, keepdims=True), axis=1, keepdims=True)


def weights(amplitude):
    pup = amplitude.shape[0]
    rows = lax.broadcasted_iota(jnp.int32, amplitude.shape, 0).astype(jnp.float32) - (pup - 1) / 2.0
    cols = lax.broadcasted_iota(jnp.int32, amplitude.shape, 1).astype(jnp.float32) - (pup - 1) / 2.0
    return jnp.where(rows * rows + cols * cols <= (pup / 2.0) ** 2, amplitude, 0.0)


def point_spread(phase, amplitude, const, wait_for=lambda name: None):
    weight = weights(amplitude)
    sine, cosine = sine_cosine(phase)
    pupil = jnp.concatenate([weight * cosine, weight * sine], 1)
    wait_for("pupil_right")
    across = right_by(pupil, const["pupil_right"])
    cols = across.shape[1] // 2
    wait_for("pupil_left")
    field = left_by(const["pupil_left"], jnp.concatenate([across[:, :cols], across[:, cols:]], 0))
    rows = field.shape[0] // 2
    intensity = field[:rows] * field[:rows] + field[rows:] * field[rows:]
    norm = 1.0 / total(intensity)
    left = left_by(const["kernel_rows"], intensity)
    freqs = left.shape[0] // 2
    wait_for("kernel_right")
    spectrum = right_by(jnp.concatenate([left[:freqs], left[freqs:]], 1), const["kernel_right"])
    return pupil, field, spectrum * norm, norm


def forward(strips, row_matrix, const):
    sums, differences = [], []
    for strip in strips:
        half = strip.shape[1] // 2
        first, second = strip[:, :half], strip[:, half:]
        mixed = left_by(row_matrix, jnp.concatenate([first + second, first - second], 1))
        freqs = mixed.shape[0] // 2
        sums.append(jnp.concatenate([mixed[:freqs, :half], mixed[freqs:, :half]], 1))
        differences.append(jnp.concatenate([mixed[:freqs, half:], mixed[freqs:, half:]], 1))
    even = [right_by(jnp.concatenate(sums[p : p + 2], 0), const["forward_even"]) for p in range(0, len(sums), 2)]
    odd = [right_by(jnp.concatenate(differences[p : p + 2], 0), const["forward_odd"]) for p in range(0, len(sums), 2)]
    return even, odd


def inverse(even, odd, freqs, const):
    even = [right_by(spectrum, const["inverse_even"]) for spectrum in even]
    odd = [right_by(spectrum, const["inverse_odd"]) for spectrum in odd]
    strips = []
    for sums, differences in zip(even, odd):
        half = sums.shape[1] // 2
        for top in range(0, sums.shape[0], freqs):
            rows = slice(top, top + freqs)
            stacked = jnp.concatenate(
                [
                    jnp.concatenate([sums[rows, :half], differences[rows, :half]], 1),
                    jnp.concatenate([sums[rows, half:], differences[rows, half:]], 1),
                ],
                0,
            )
            mixed = left_stacked(const["row_inverse"], stacked)
            first, second = mixed[:, :half], mixed[:, half:]
            strips.append(jnp.concatenate([first + second, first - second], 1))
    return strips


def times(spectra, other, conjugate):
    half = other.shape[1] // 2
    products = []
    for spectrum in spectra:
        planes = spectrum.shape[0] // other.shape[0]
        real = jnp.concatenate([other[:, :half]] * planes, 0)
        imag = jnp.concatenate([other[:, half:]] * planes, 0)
        left, right = spectrum[:, :half], spectrum[:, half:]
        if conjugate:
            product = [left * real + right * imag, right * real - left * imag]
        else:
            product = [left * real - right * imag, left * imag + right * real]
        products.append(jnp.concatenate(product, 1))
    return products


def cross(firsts, seconds, freqs):
    summed = None
    for first, second in zip(firsts, seconds):
        half = first.shape[1] // 2
        left, right = first[:, :half], first[:, half:]
        real, imag = second[:, :half], second[:, half:]
        both = jnp.concatenate([left * real + right * imag, right * real - left * imag], 1)
        for top in range(0, both.shape[0], freqs):
            summed = both[top : top + freqs] if summed is None else summed + both[top : top + freqs]
    return summed


def is_even():
    return lax.axis_index("tile") % 2 == 0


def edge_rows(top, bottom):
    even = is_even()
    return [pl.multiple_of(jnp.where(even, *choice), 8) for choice in ((top, bottom), (bottom, top))]


def run_all(copies):
    for copy in copies:
        copy.start()
    for copy in copies:
        copy.wait()


def near_kernel(own, chip_out, core_out, sems):
    chip, core = edge_rows(0, own.shape[1] - HALF)
    run_all([
        pltpu.make_async_copy(own.at[:, pl.ds(chip, HALF), :], chip_out, sems.at[0]),
        pltpu.make_async_copy(own.at[:, pl.ds(core, HALF), :], core_out, sems.at[1]),
    ])


def first_kernel(
    phase, amplitude, own, observed, *refs, at, places, arrays,
):
    psf_refs, (_, pupil_out, field_out, spec_out, chip_out, core_out, token_out) = refs[:arrays], refs[arrays : arrays + 7]
    psf_outs, (phase_in, amplitude_in, sems) = refs[arrays + 7 : -3], refs[-3:]
    planes, rows, _ = own.shape
    objects_chip, objects_core = edge_rows(HALF, rows - 2 * HALF)
    observed_chip, observed_core = edge_rows(0, rows - HALF)
    pairs = [
        (phase, phase_in),
        (amplitude, amplitude_in),
        *zip(psf_refs, psf_outs),
        (own.at[:, pl.ds(objects_chip, HALF), :], chip_out.at[:planes]),
        (observed.at[:, pl.ds(observed_chip, HALF), :], chip_out.at[planes:]),
        (own.at[:, pl.ds(objects_core, HALF), :], core_out.at[:planes]),
        (observed.at[:, pl.ds(observed_core, HALF), :], core_out.at[planes:]),
    ]
    copies = [pltpu.make_async_copy(source, target, sems.at[i]) for i, (source, target) in enumerate(pairs)]
    for i in (0, 1, *(2 + places[name][0] for name in NEEDED_IN_ORDER), *range(2 + arrays, len(copies))):
        copies[i].start()
    for copy in copies[:2]:
        copy.wait()

    def wait_for(name):
        copies[2 + places[name][0]].wait()

    pupil, field, spectrum, norm = point_spread(phase_in[...], amplitude_in[...], at(*psf_outs), wait_for)
    root = jnp.sqrt(norm)
    pupil_out[...] = pupil * root
    field_out[...] = field * root
    spec_out[...] = spectrum
    token_out[...] = jnp.zeros_like(token_out)
    for copy in copies[2 + arrays :]:
        copy.wait()


def halo_rows(chip, core):
    even = is_even()
    return jnp.where(even, chip, core), jnp.where(even, core, chip)


def gradient_kernel(
    from_chip, from_core, own, observed, spec, pupil, field, _, *refs, at,
):
    planes, rows, cols = own.shape
    const = at(*refs[:-2])
    keep_out, give_out = refs[-2:]
    freqs = spec.shape[0]
    strips = []
    for p in range(planes):
        above, below = halo_rows(from_chip[p], from_core[p])
        strips.append(jnp.concatenate([above, own[p], below], 0))
    even, odd = forward(strips, const["row_forward"], const)
    blurred = inverse(times(even, spec[:, :cols], False), times(odd, spec[:, cols:], False), freqs, const)
    misfit = [1.0 - observed[p] / (blurred[p] + BACKGROUND) for p in range(planes)]
    weighted = misfit[0] * blurred[0]
    for p in range(1, planes):
        weighted = weighted + misfit[p] * blurred[p]
    mean = total(weighted)
    misfit_even, misfit_odd = forward(misfit, const["row_own"], const)
    shared = jnp.concatenate([cross(misfit_even, even, freqs), cross(misfit_odd, odd, freqs)], 1)
    across = right_by(shared, const["lag_right"])
    pad_cols = across.shape[1] // 2
    psf_grad = left_by(const["lag_left"], jnp.concatenate([across[:, :pad_cols], across[:, pad_cols:]], 0))
    far = field[...]
    pad_rows = far.shape[0] // 2
    real, imag = far[:pad_rows], far[pad_rows:]
    centred = 2.0 * (psf_grad - mean)
    back = left_by(const["adjoint_left"], jnp.concatenate([centred * real, centred * imag], 0))
    pup = back.shape[0] // 2
    back = right_by(jnp.concatenate([back[:pup], back[pup:]], 1), const["adjoint_right"])
    near = pupil[...]
    slope = back[:, pup:] * near[:, :pup] - back[:, :pup] * near[:, pup:]
    even_core = is_even()
    keep_out[...] = jnp.where(even_core, slope[: pup // 2], slope[pup // 2 :])
    give_out[...] = jnp.where(even_core, slope[pup // 2 :], slope[: pup // 2])


def square_sums(value):
    rows = value.shape[0]
    squared = value * value
    summed = squared[:8]
    for top in range(8, rows, 8):
        summed = summed + squared[top : top + 8]
    return summed


def squares_kernel(mine, received, *others):
    joined_out = others[-1]
    half = mine[...] + received[...]
    squares = square_sums(half)
    for first, second in zip(others[:-1:2], others[1:-1:2]):
        squares = squares + square_sums(first[...] + second[...])
    joined_out[: half.shape[0]] = half
    joined_out[half.shape[0] :] = squares


def blocks_kernel(from_chip, from_core, own, far_chip, far_core, _, *refs, at):
    planes = own.shape[0]
    const = at(*refs[:-2])
    even_out, odd_out = refs[-2:]
    strips = []
    for p in range(planes):
        above, below = halo_rows(from_chip[p], from_core[p])
        far_above, far_below = halo_rows(far_chip[p], far_core[p])
        strips.append(jnp.concatenate([far_above, above, own[p]], 0))
        strips.append(jnp.concatenate([own[p], below, far_below], 0))
    even, odd = forward(strips, const["row_forward"], const)
    even_out[...] = jnp.concatenate(even, 0)
    odd_out[...] = jnp.concatenate(odd, 0)


def second_kernel(phase, amplitude, mine, theirs, *refs, at, psf_at, arrays, cells, squares_apart):
    if squares_apart:
        squares, *refs = refs
    even, odd, own, observed, far_chip, far_core, *refs = refs
    planes, rows, cols = own.shape
    const = at(*refs[:arrays])
    psf_const = psf_at(*refs[arrays:-2])
    objects_out, phase_out = refs[-2:]
    half = phase.shape[0] // 2
    first, second = halo_rows(mine[:half], theirs[:half])
    slope = jnp.concatenate([first, second], 0)
    summed = squares[...] if squares_apart else mine[half:] + theirs[half:]
    mean_square = total(summed) * (1.0 / cells)
    updated = phase[...] - STEP_SIZE * slope / jnp.sqrt(mean_square + EPSILON)
    phase_out[...] = updated
    _, _, spec, _ = point_spread(updated, amplitude[...], psf_const)
    spec_even, spec_odd = spec[:, :cols], spec[:, cols:]
    freqs = spec.shape[0]
    pairs = range(0, even.shape[0], 2 * freqs)
    light = inverse(
        times([even[top : top + 2 * freqs] for top in pairs], spec_even, False),
        times([odd[top : top + 2 * freqs] for top in pairs], spec_odd, False),
        freqs, const,
    )
    ratios = []
    for p in range(planes):
        above, below = halo_rows(far_chip[planes + p], far_core[planes + p])
        blurred = jnp.concatenate(light[2 * p : 2 * p + 2], 0) + BACKGROUND
        ratios.append(jnp.concatenate([above, observed[p], below], 0) / blurred)
    ratio_even, ratio_odd = forward(ratios, const["row_forward"], const)
    correction = inverse(times(ratio_even, spec_even, True), times(ratio_odd, spec_odd, True), freqs, const)
    for p in range(planes):
        objects_out[p] = own[p] * correction[p]


def call(kernel, out_shapes, args, flops=10**6, spaces=None, scratch=()):
    outs = [
        jax.ShapeDtypeStruct(shape, jnp.float32) if isinstance(shape, tuple) else shape for shape in out_shapes
    ]
    spaces = spaces or {}
    return pl.pallas_call(
        kernel,
        out_shape=outs,
        in_specs=[pl.BlockSpec(memory_space=spaces.get(i, pltpu.VMEM)) for i in range(len(args))],
        out_specs=[pl.BlockSpec(memory_space=pltpu.VMEM)] * len(outs),
        scratch_shapes=scratch,
        compiler_params=pltpu.CompilerParams(vmem_limit_bytes=VMEM_LIMIT),
        cost_estimate=pl.CostEstimate(flops=flops, bytes_accessed=10**5, transcendentals=0),
    )(*args)


def to_next_chip(value):
    count = lax.axis_size("tile")
    return lax.ppermute(value, "tile", [(i, (i + 1 if i % 2 else i - 1) % count) for i in range(count)])


def exchange(value, step):
    return lax.ppermute(value, "tile", [(i, i ^ step) for i in range(lax.axis_size("tile"))])


def across_depth_and_chip(value):
    pairs = [(2 * t + d, 2 * (t ^ 2) + 1 - d) for t in range(lax.axis_size("tile")) for d in range(2)]
    return lax.ppermute(value, ("tile", "depth"), pairs)


def sum_over_depth(value):
    count = lax.axis_size("depth")
    if count & (count - 1):
        return lax.psum(value, "depth")
    for bit in range(count.bit_length() - 1):
        value = value + lax.ppermute(value, "depth", [(i, i ^ (1 << bit)) for i in range(count)])
    return value


def on_device(objects, observed, pupil_phase, pupil_amplitude):
    picture, measured, phase, amplitude = objects[0], observed[0], pupil_phase[0], pupil_amplitude[0]
    planes, rows, cols = picture.shape
    pup = phase.shape[0]
    count = lax.axis_size("tile")
    ker = 2 * HALF + 1
    length = rows + 2 * HALF
    pad_rows, pad_cols = round_up(ker, 16), round_up(ker, 128)
    row_forward, row_inverse = row_constants(rows, length)
    col_forward, col_inverse = col_constants(cols)
    kernel_rows, kernel_right = kernel_constants(length, cols, ker, pad_rows, pad_cols)
    pupil_left, pupil_right = pupil_constants(pup, ker, pad_rows, pad_cols)
    psf_const = Joined(
        {"pupil_left": pupil_left, "kernel_rows": kernel_rows},
        {"pupil_right": pupil_right, "kernel_right": kernel_right},
    )
    block_left = {"row_forward": row_forward, "row_inverse": row_inverse}
    block_right = {
        "forward_even": col_forward[0],
        "forward_odd": col_forward[1],
        "inverse_even": col_inverse[0],
        "inverse_odd": col_inverse[1],
    }
    block_const = Joined(block_left, block_right)
    lag_const = Joined(
        {
            "row_own": row_forward[:, HALF : HALF + rows],
            "lag_left": kernel_rows.T * (2.0 / length),
            "adjoint_left": pupil_left.T,
        },
        {"lag_right": kernel_right.T / cols, "adjoint_right": pupil_right.T},
    )
    psf_arrays, block_arrays, lag_arrays = (
        [jnp.asarray(array) for array in const.arrays] for const in (psf_const, block_const, lag_const)
    )

    def gradient_at(*refs):
        held = len(block_arrays)
        return {**block_const.at(*refs[:held]), **lag_const.at(*refs[held:])}

    in_hbm = [
        pltpu.with_memory_space_constraint(value, pltpu.HBM)
        for value in (phase, amplitude, picture, measured, *psf_arrays)
    ]
    edge = (planes, HALF, cols)
    chip_rows, core_rows = call(near_kernel, [edge] * 2, in_hbm[2:3], scratch=[pltpu.SemaphoreType.DMA((2,))], spaces={0: pltpu.HBM})
    from_core = exchange(core_rows, 1)
    from_chip = to_next_chip(chip_rows)
    pupil, field, spec, far_chip, far_core, token, *psf_arrays = call(
        functools.partial(first_kernel, at=psf_const.at, places=psf_const.places, arrays=len(psf_arrays)),
        [(pup, 2 * pup), (2 * pad_rows, pad_cols), (length // 2, 2 * cols)]
        + [(2 * planes, HALF, cols)] * 2
        + [(8, 128)]
        + psf_arrays,
        (*in_hbm, chip_rows),
        flops=3 * 10**9,
        spaces={**dict.fromkeys(range(len(in_hbm)), pltpu.HBM), len(in_hbm): pl.ANY},
        scratch=[pltpu.VMEM(phase.shape, jnp.float32)] * 2 + [pltpu.SemaphoreType.DMA((6 + len(psf_arrays),))],
    )
    far_core = exchange(far_core, 1)
    far_chip, token = lax.optimization_barrier((far_chip, exchange(token, 1)))
    far_chip = to_next_chip(far_chip)
    keep, give = call(
        functools.partial(gradient_kernel, at=gradient_at),
        [(pup // 2, pup)] * 2,
        (from_chip, from_core, picture, measured, spec, pupil, field, token, *block_arrays, *lag_arrays),
        flops=4 * 10**10,
        spaces={7: pl.ANY},
    )
    half = keep + exchange(give, 1)
    bits = list(range(2, count.bit_length() - 1))
    for low, high in zip(bits[::2], bits[1::2]):
        half = half + ((exchange(half, 1 << low) + exchange(half, (1 << low) | (1 << high))) + exchange(half, 1 << high))
    if len(bits) % 2:
        half = half + exchange(half, 1 << bits[-1])
    last_round = [exchange(half, 2)]
    two_strata = lax.axis_size("depth") == 2
    if two_strata:
        last_round += [lax.ppermute(half, "depth", [(0, 1), (1, 0)]), across_depth_and_chip(half)]
    even, odd = call(
        functools.partial(blocks_kernel, at=block_const.at),
        [(planes * length, cols)] * 2,
        (from_chip, from_core, picture, far_chip, far_core, half, *block_arrays),
        spaces={5: pl.ANY},
    )
    even, *last_round = lax.optimization_barrier((even, *last_round))
    (joined,) = call(squares_kernel, [(pup // 2 + 8, pup)], (half, *last_round))
    other = exchange(joined, 1)
    squares = []
    if not two_strata:
        squares = [sum_over_depth(joined[pup // 2 :] + other[pup // 2 :])]
    new_objects, new_phase = call(
        functools.partial(
            second_kernel,
            at=block_const.at,
            psf_at=psf_const.at,
            arrays=len(block_arrays),
            cells=lax.axis_size("depth") * pup * pup,
            squares_apart=bool(squares),
        ),
        [picture.shape, phase.shape],
        (
            phase, amplitude, joined, other, *squares, even, odd, picture, measured,
            far_chip, far_core, *block_arrays, *psf_arrays,
        ),
    )
    return new_objects[None], new_phase[None]


def solution(mesh):
    return jax.shard_map(
        on_device,
        mesh=mesh,
        in_specs=(
            P("depth", None, "tile", None),
            P("depth", None, "tile", None),
            P("depth", None, None),
            P("depth", None, None),
        ),
        out_specs=(P("depth", None, "tile", None), P("depth", None, None)),
        check_vma=False,
    )
```

```python
import functools
import math

import jax
import jax.numpy as jnp
import ml_dtypes
import numpy as np
from jax import lax
from jax.experimental import pallas as pl
from jax.experimental.pallas import tpu as pltpu
from jax.sharding import PartitionSpec as P

HALF = 64
BACKGROUND = 0.1
STEP_SIZE = 0.3
EPSILON = 1e-06
STACKED = ("row_inverse",)
NEEDED_IN_ORDER = ("pupil_right", "pupil_left", "kernel_right")
VMEM_LIMIT = 32 * 1024 * 1024


def round_up(value, step):
    return -(-value // step) * step


def angles(left, right, length):
    return (2.0 * math.pi / length) * np.outer(left, right)


def halves(matrix):
    high = matrix.astype(np.float32).astype(ml_dtypes.bfloat16)
    low = (matrix - high.astype(np.float64)).astype(np.float32).astype(ml_dtypes.bfloat16)
    return high, low


def row_constants(rows, length):
    freqs = np.arange(length // 2) + 0.5
    theta = angles(freqs, np.arange(length), length)
    forward = np.concatenate([np.cos(theta), -np.sin(theta)], 0)
    inner = theta[:, HALF : HALF + rows]
    inverse = np.concatenate([np.cos(inner).T, -np.sin(inner).T], 1) * (2.0 / length)
    return forward, inverse


def col_constants(cols):
    half = cols // 2
    forward, inverse = [], []
    for parity in range(2):
        theta = angles(np.arange(half), 2 * np.arange(half) + parity, cols)
        c, s = np.cos(theta), np.sin(theta)
        forward.append(np.block([[c, -s], [s, c]]))
        inverse.append(np.block([[c.T, s.T], [-s.T, c.T]]) / cols)
    return forward, inverse


def kernel_constants(length, cols, ker, pad_rows, pad_cols):
    lags = np.arange(ker) - HALF
    theta = angles(np.arange(length // 2) + 0.5, lags, length)
    rows = np.zeros((length, pad_rows))
    rows[: length // 2, :ker] = np.cos(theta)
    rows[length // 2 :, :ker] = -np.sin(theta)
    half = cols // 2
    right = np.zeros((2 * pad_cols, 2 * cols))
    for parity in range(2):
        theta = angles(lags, 2 * np.arange(half) + parity, cols)
        c, s = np.cos(theta), np.sin(theta)
        at = parity * cols
        right[:ker, at : at + half] = c
        right[:ker, at + half : at + cols] = -s
        right[pad_cols : pad_cols + ker, at : at + half] = s
        right[pad_cols : pad_cols + ker, at + half : at + cols] = c
    return rows, right


def pupil_constants(pup, ker, pad_rows, pad_cols):
    theta = angles(np.arange(ker) - HALF, np.arange(pup), ker)
    real, imag = np.cos(theta), -np.sin(theta)
    right = np.zeros((2 * pup, 2 * pad_cols))
    right[:pup, :ker] = real.T
    right[:pup, pad_cols : pad_cols + ker] = imag.T
    right[pup:, :ker] = -imag.T
    right[pup:, pad_cols : pad_cols + ker] = real.T
    left = np.zeros((2 * pad_rows, 2 * pup))
    left[:ker, :pup] = real
    left[:ker, pup:] = -imag
    left[pad_rows : pad_rows + ker, :pup] = imag
    left[pad_rows : pad_rows + ker, pup:] = real
    return left, right


class Joined:
    def __init__(self, left, right):
        self.places, groups = {}, {}
        for name, matrix in right.items():
            high, low = halves(matrix)
            groups.setdefault(matrix.shape[0], []).append((name, np.concatenate([high, high, low], 0)))
        for name, matrix in left.items():
            high, low = halves(matrix)
            held = np.concatenate([high, low], 0) if name in STACKED else np.concatenate([high, low, high], 1)
            groups.setdefault("left", []).append((name, held))
        self.arrays = []
        for kind, members in groups.items():
            at = 0
            for name, block in members:
                rows, cols = block.shape
                start = (at, 0) if kind == "left" else (0, at)
                self.places[name] = (len(self.arrays), *start, rows, cols)
                at += rows if kind == "left" else cols
            blocks = [block for _, block in members]
            if kind == "left":
                width = max(block.shape[1] for block in blocks)
                blocks = [np.pad(block, ((0, 0), (0, width - block.shape[1]))) for block in blocks]
            self.arrays.append(np.concatenate(blocks, 0 if kind == "left" else 1))

    def at(self, *refs):
        return {
            name: refs[which].at[top : top + rows, first : first + cols]
            for name, (which, top, first, rows, cols) in self.places.items()
        }


def dot(left, right):
    return jnp.dot(left, right, preferred_element_type=jnp.float32)


def split(value):
    high = value.astype(jnp.bfloat16)
    low = (value - high.astype(jnp.float32)).astype(jnp.bfloat16)
    return high, low


def left_by(const, value):
    high, low = split(value)
    return dot(const[...], jnp.concatenate([high, high, low], 0))


def left_stacked(const, value):
    high, low = split(value)
    rows = const.shape[0] // 2
    both = dot(const[...], high)
    return both[:rows] + (both[rows:] + dot(const[:rows], low))


def right_by(value, const):
    high, low = split(value)
    return dot(jnp.concatenate([high, low, high], 1), const[...])


def sine_cosine(angle):
    turns = jnp.floor(angle * (2.0 / math.pi) + 0.5)
    rest = angle - turns * 1.5703125
    rest = rest - turns * 4.837512969970703e-4
    rest = rest - turns * 7.54978995489e-8
    square = rest * rest
    sine = rest + rest * square * (
        -1.6666654611e-1 + square * (8.3321608736e-3 + square * -1.9515295891e-4)
    )
    cosine = 1.0 - 0.5 * square + square * square * (
        4.166664568298827e-2 + square * (-1.388731625493765e-3 + square * 2.443315711809948e-5)
    )
    quadrant = turns.astype(jnp.int32) & 3
    swap = (quadrant & 1) == 1
    sine_out = jnp.where(swap, cosine, sine)
    cosine_out = jnp.where(swap, sine, cosine)
    sine_out = jnp.where(quadrant >= 2, -sine_out, sine_out)
    cosine_out = jnp.where((quadrant == 1) | (quadrant == 2), -cosine_out, cosine_out)
    return sine_out, cosine_out


def total(value):
    return jnp.sum(jnp.sum(value, axis=0, keepdims=True), axis=1, keepdims=True)


def weights(amplitude):
    pup = amplitude.shape[0]
    rows = lax.broadcasted_iota(jnp.int32, amplitude.shape, 0).astype(jnp.float32) - (pup - 1) / 2.0
    cols = lax.broadcasted_iota(jnp.int32, amplitude.shape, 1).astype(jnp.float32) - (pup - 1) / 2.0
    return jnp.where(rows * rows + cols * cols <= (pup / 2.0) ** 2, amplitude, 0.0)


def point_spread(phase, amplitude, const, wait_for=lambda name: None):
    weight = weights(amplitude)
    sine, cosine = sine_cosine(phase)
    pupil = jnp.concatenate([weight * cosine, weight * sine], 1)
    wait_for("pupil_right")
    across = right_by(pupil, const["pupil_right"])
    cols = across.shape[1] // 2
    wait_for("pupil_left")
    field = left_by(const["pupil_left"], jnp.concatenate([across[:, :cols], across[:, cols:]], 0))
    rows = field.shape[0] // 2
    intensity = field[:rows] * field[:rows] + field[rows:] * field[rows:]
    norm = 1.0 / total(intensity)
    left = left_by(const["kernel_rows"], intensity)
    freqs = left.shape[0] // 2
    wait_for("kernel_right")
    spectrum = right_by(jnp.concatenate([left[:freqs], left[freqs:]], 1), const["kernel_right"])
    return pupil, field, spectrum * norm, norm


def forward(strips, row_matrix, const):
    sums, differences = [], []
    for strip in strips:
        half = strip.shape[1] // 2
        first, second = strip[:, :half], strip[:, half:]
        mixed = left_by(row_matrix, jnp.concatenate([first + second, first - second], 1))
        freqs = mixed.shape[0] // 2
        sums.append(jnp.concatenate([mixed[:freqs, :half], mixed[freqs:, :half]], 1))
        differences.append(jnp.concatenate([mixed[:freqs, half:], mixed[freqs:, half:]], 1))
    even = [right_by(jnp.concatenate(sums[p : p + 2], 0), const["forward_even"]) for p in range(0, len(sums), 2)]
    odd = [right_by(jnp.concatenate(differences[p : p + 2], 0), const["forward_odd"]) for p in range(0, len(sums), 2)]
    return even, odd


def inverse(even, odd, freqs, const):
    even = [right_by(spectrum, const["inverse_even"]) for spectrum in even]
    odd = [right_by(spectrum, const["inverse_odd"]) for spectrum in odd]
    strips = []
    for sums, differences in zip(even, odd):
        half = sums.shape[1] // 2
        for top in range(0, sums.shape[0], freqs):
            rows = slice(top, top + freqs)
            stacked = jnp.concatenate(
                [
                    jnp.concatenate([sums[rows, :half], differences[rows, :half]], 1),
                    jnp.concatenate([sums[rows, half:], differences[rows, half:]], 1),
                ],
                0,
            )
            mixed = left_stacked(const["row_inverse"], stacked)
            first, second = mixed[:, :half], mixed[:, half:]
            strips.append(jnp.concatenate([first + second, first - second], 1))
    return strips


def times(spectra, other, conjugate):
    half = other.shape[1] // 2
    products = []
    for spectrum in spectra:
        planes = spectrum.shape[0] // other.shape[0]
        real = jnp.concatenate([other[:, :half]] * planes, 0)
        imag = jnp.concatenate([other[:, half:]] * planes, 0)
        left, right = spectrum[:, :half], spectrum[:, half:]
        if conjugate:
            product = [left * real + right * imag, right * real - left * imag]
        else:
            product = [left * real - right * imag, left * imag + right * real]
        products.append(jnp.concatenate(product, 1))
    return products


def cross(firsts, seconds, freqs):
    summed = None
    for first, second in zip(firsts, seconds):
        half = first.shape[1] // 2
        left, right = first[:, :half], first[:, half:]
        real, imag = second[:, :half], second[:, half:]
        both = jnp.concatenate([left * real + right * imag, right * real - left * imag], 1)
        for top in range(0, both.shape[0], freqs):
            summed = both[top : top + freqs] if summed is None else summed + both[top : top + freqs]
    return summed


def is_even():
    return lax.axis_index("tile") % 2 == 0


def edge_rows(top, bottom):
    even = is_even()
    return [pl.multiple_of(jnp.where(even, *choice), 8) for choice in ((top, bottom), (bottom, top))]


def near_kernel(own, chip_out, sem):
    chip, _ = edge_rows(0, own.shape[1] - HALF)
    copy = pltpu.make_async_copy(own.at[:, pl.ds(chip, HALF), :], chip_out, sem)
    copy.start()
    copy.wait()


def first_kernel(
    phase, amplitude, own, observed, *refs, at, places, arrays,
):
    psf_refs, outs = refs[:arrays], refs[arrays + 1 : arrays + 9]
    pupil_out, field_out, spec_out, chip_out, core_out, early_out, late_out, token_out = outs
    psf_outs, (phase_in, amplitude_in, sems) = refs[arrays + 9 : -3], refs[-3:]
    planes, rows, _ = own.shape
    early = early_out.shape[0]
    objects_chip, objects_core = edge_rows(HALF, rows - 2 * HALF)
    observed_chip, observed_core = edge_rows(0, rows - HALF)
    pairs = [
        (phase, phase_in),
        (amplitude, amplitude_in),
        *zip(psf_refs, psf_outs),
        (own.at[:early, pl.ds(observed_core, HALF), :], early_out),
        (own.at[early:, pl.ds(observed_core, HALF), :], late_out),
        (own.at[:, pl.ds(objects_chip, HALF), :], chip_out.at[:planes]),
        (observed.at[:, pl.ds(observed_chip, HALF), :], chip_out.at[planes:]),
        (own.at[:, pl.ds(objects_core, HALF), :], core_out.at[:planes]),
        (observed.at[:, pl.ds(observed_core, HALF), :], core_out.at[planes:]),
    ]
    copies = [pltpu.make_async_copy(source, target, sems.at[i]) for i, (source, target) in enumerate(pairs)]
    for i in (0, 1, *(2 + places[name][0] for name in NEEDED_IN_ORDER), *range(2 + arrays, len(copies))):
        copies[i].start()
    for copy in copies[:2]:
        copy.wait()

    def wait_for(name):
        copies[2 + places[name][0]].wait()

    pupil, field, spectrum, norm = point_spread(phase_in[...], amplitude_in[...], at(*psf_outs), wait_for)
    root = jnp.sqrt(norm)
    pupil_out[...] = pupil * root
    field_out[...] = field * root
    spec_out[...] = spectrum
    token_out[...] = jnp.zeros_like(token_out)
    for copy in copies[2 + arrays :]:
        copy.wait()


def halo_rows(chip, core):
    even = is_even()
    return jnp.where(even, chip, core), jnp.where(even, core, chip)


def gradient_kernel(
    from_chip, early_core, late_core, own, observed, spec, pupil, field, _, *refs, at,
):
    planes, rows, cols = own.shape
    const = at(*refs[:-2])
    keep_out, give_out = refs[-2:]
    freqs = spec.shape[0]
    early = early_core.shape[0]
    strips = []
    for p in range(planes):
        above, below = halo_rows(from_chip[p], early_core[p] if p < early else late_core[p - early])
        strips.append(jnp.concatenate([above, own[p], below], 0))
    even, odd = forward(strips, const["row_forward"], const)
    blurred = inverse(times(even, spec[:, :cols], False), times(odd, spec[:, cols:], False), freqs, const)
    misfit = [1.0 - observed[p] / (blurred[p] + BACKGROUND) for p in range(planes)]
    weighted = misfit[0] * blurred[0]
    for p in range(1, planes):
        weighted = weighted + misfit[p] * blurred[p]
    mean = total(weighted)
    misfit_even, misfit_odd = forward(misfit, const["row_own"], const)
    shared = jnp.concatenate([cross(misfit_even, even, freqs), cross(misfit_odd, odd, freqs)], 1)
    across = right_by(shared, const["lag_right"])
    pad_cols = across.shape[1] // 2
    psf_grad = left_by(const["lag_left"], jnp.concatenate([across[:, :pad_cols], across[:, pad_cols:]], 0))
    far = field[...]
    pad_rows = far.shape[0] // 2
    real, imag = far[:pad_rows], far[pad_rows:]
    centred = 2.0 * (psf_grad - mean)
    back = left_by(const["adjoint_left"], jnp.concatenate([centred * real, centred * imag], 0))
    pup = back.shape[0] // 2
    back = right_by(jnp.concatenate([back[:pup], back[pup:]], 1), const["adjoint_right"])
    near = pupil[...]
    slope = back[:, pup:] * near[:, :pup] - back[:, :pup] * near[:, pup:]
    even_core = is_even()
    keep_out[...] = jnp.where(even_core, slope[: pup // 2], slope[pup // 2 :])
    give_out[...] = jnp.where(even_core, slope[pup // 2 :], slope[: pup // 2])


def square_sums(value):
    rows = value.shape[0]
    squared = value * value
    summed = squared[:8]
    for top in range(8, rows, 8):
        summed = summed + squared[top : top + 8]
    return summed


def squares_kernel(mine, received, *others):
    joined_out = others[-1]
    half = mine[...] + received[...]
    squares = square_sums(half)
    for first, second in zip(others[:-1:2], others[1:-1:2]):
        squares = squares + square_sums(first[...] + second[...])
    joined_out[: half.shape[0]] = half
    joined_out[half.shape[0] :] = squares


def blocks_kernel(from_chip, early_core, late_core, own, far_chip, far_core, _, *refs, at):
    planes = own.shape[0]
    const = at(*refs[:-2])
    even_out, odd_out = refs[-2:]
    early = early_core.shape[0]
    strips = []
    for p in range(planes):
        above, below = halo_rows(from_chip[p], early_core[p] if p < early else late_core[p - early])
        far_above, far_below = halo_rows(far_chip[p], far_core[p])
        strips.append(jnp.concatenate([far_above, above, own[p]], 0))
        strips.append(jnp.concatenate([own[p], below, far_below], 0))
    even, odd = forward(strips, const["row_forward"], const)
    even_out[...] = jnp.concatenate(even, 0)
    odd_out[...] = jnp.concatenate(odd, 0)


def second_kernel(phase, amplitude, mine, theirs, *refs, at, psf_at, arrays, cells, squares_apart):
    if squares_apart:
        squares, *refs = refs
    even, odd, own, observed, far_chip, far_core, *refs = refs
    planes, rows, cols = own.shape
    const = at(*refs[:arrays])
    psf_const = psf_at(*refs[arrays:-2])
    objects_out, phase_out = refs[-2:]
    half = phase.shape[0] // 2
    first, second = halo_rows(mine[:half], theirs[:half])
    slope = jnp.concatenate([first, second], 0)
    summed = squares[...] if squares_apart else mine[half:] + theirs[half:]
    mean_square = total(summed) * (1.0 / cells)
    updated = phase[...] - STEP_SIZE * slope / jnp.sqrt(mean_square + EPSILON)
    phase_out[...] = updated
    _, _, spec, _ = point_spread(updated, amplitude[...], psf_const)
    spec_even, spec_odd = spec[:, :cols], spec[:, cols:]
    freqs = spec.shape[0]
    pairs = range(0, even.shape[0], 2 * freqs)
    light = inverse(
        times([even[top : top + 2 * freqs] for top in pairs], spec_even, False),
        times([odd[top : top + 2 * freqs] for top in pairs], spec_odd, False),
        freqs, const,
    )
    ratios = []
    for p in range(planes):
        above, below = halo_rows(far_chip[planes + p], far_core[planes + p])
        blurred = jnp.concatenate(light[2 * p : 2 * p + 2], 0) + BACKGROUND
        ratios.append(jnp.concatenate([above, observed[p], below], 0) / blurred)
    ratio_even, ratio_odd = forward(ratios, const["row_forward"], const)
    correction = inverse(times(ratio_even, spec_even, True), times(ratio_odd, spec_odd, True), freqs, const)
    for p in range(planes):
        objects_out[p] = own[p] * correction[p]


def call(kernel, out_shapes, args, flops=10**6, spaces=None, scratch=()):
    outs = [
        jax.ShapeDtypeStruct(shape, jnp.float32) if isinstance(shape, tuple) else shape for shape in out_shapes
    ]
    spaces = spaces or {}
    return pl.pallas_call(
        kernel,
        out_shape=outs,
        in_specs=[pl.BlockSpec(memory_space=spaces.get(i, pltpu.VMEM)) for i in range(len(args))],
        out_specs=[pl.BlockSpec(memory_space=pltpu.VMEM)] * len(outs),
        scratch_shapes=scratch,
        compiler_params=pltpu.CompilerParams(vmem_limit_bytes=VMEM_LIMIT),
        cost_estimate=pl.CostEstimate(flops=flops, bytes_accessed=10**5, transcendentals=0),
    )(*args)


def to_next_chip(value):
    count = lax.axis_size("tile")
    return lax.ppermute(value, "tile", [(i, (i + 1 if i % 2 else i - 1) % count) for i in range(count)])


def exchange(value, step):
    return lax.ppermute(value, "tile", [(i, i ^ step) for i in range(lax.axis_size("tile"))])


def across_depth_and_chip(value):
    pairs = [(2 * t + d, 2 * (t ^ 2) + 1 - d) for t in range(lax.axis_size("tile")) for d in range(2)]
    return lax.ppermute(value, ("tile", "depth"), pairs)


def sum_over_depth(value):
    count = lax.axis_size("depth")
    if count & (count - 1):
        return lax.psum(value, "depth")
    for bit in range(count.bit_length() - 1):
        value = value + lax.ppermute(value, "depth", [(i, i ^ (1 << bit)) for i in range(count)])
    return value


def on_device(objects, observed, pupil_phase, pupil_amplitude):
    picture, measured, phase, amplitude = objects[0], observed[0], pupil_phase[0], pupil_amplitude[0]
    planes, rows, cols = picture.shape
    pup = phase.shape[0]
    count = lax.axis_size("tile")
    ker = 2 * HALF + 1
    length = rows + 2 * HALF
    pad_rows, pad_cols = round_up(ker, 16), round_up(ker, 128)
    row_forward, row_inverse = row_constants(rows, length)
    col_forward, col_inverse = col_constants(cols)
    kernel_rows, kernel_right = kernel_constants(length, cols, ker, pad_rows, pad_cols)
    pupil_left, pupil_right = pupil_constants(pup, ker, pad_rows, pad_cols)
    psf_const = Joined(
        {"pupil_left": pupil_left, "kernel_rows": kernel_rows},
        {"pupil_right": pupil_right, "kernel_right": kernel_right},
    )
    block_left = {"row_forward": row_forward, "row_inverse": row_inverse}
    block_right = {
        "forward_even": col_forward[0],
        "forward_odd": col_forward[1],
        "inverse_even": col_inverse[0],
        "inverse_odd": col_inverse[1],
    }
    block_const = Joined(block_left, block_right)
    lag_const = Joined(
        {
            "row_own": row_forward[:, HALF : HALF + rows],
            "lag_left": kernel_rows.T * (2.0 / length),
            "adjoint_left": pupil_left.T,
        },
        {"lag_right": kernel_right.T / cols, "adjoint_right": pupil_right.T},
    )
    psf_arrays, block_arrays, lag_arrays = (
        [jnp.asarray(array) for array in const.arrays] for const in (psf_const, block_const, lag_const)
    )

    def gradient_at(*refs):
        held = len(block_arrays)
        return {**block_const.at(*refs[:held]), **lag_const.at(*refs[held:])}

    in_hbm = [
        pltpu.with_memory_space_constraint(value, pltpu.HBM)
        for value in (phase, amplitude, picture, measured, *psf_arrays)
    ]
    (chip_rows,) = call(
        near_kernel, [(planes, HALF, cols)], in_hbm[2:3], scratch=[pltpu.SemaphoreType.DMA(())], spaces={0: pltpu.HBM}
    )
    from_chip = to_next_chip(chip_rows)
    pupil, field, spec, far_chip, far_core, early_rows, late_rows, token, *psf_arrays = call(
        functools.partial(first_kernel, at=psf_const.at, places=psf_const.places, arrays=len(psf_arrays)),
        [(pup, 2 * pup), (2 * pad_rows, pad_cols), (length // 2, 2 * cols)]
        + [(2 * planes, HALF, cols)] * 2
        + [(planes // 2, HALF, cols), (planes - planes // 2, HALF, cols), (8, 128)]
        + psf_arrays,
        (*in_hbm, chip_rows),
        flops=3 * 10**9,
        spaces={**dict.fromkeys(range(len(in_hbm)), pltpu.HBM), len(in_hbm): pl.ANY},
        scratch=[pltpu.VMEM(phase.shape, jnp.float32)] * 2 + [pltpu.SemaphoreType.DMA((8 + len(psf_arrays),))],
    )
    early_core, late_core, far_core = (exchange(value, 1) for value in (early_rows, late_rows, far_core))
    far_chip, late_core = lax.optimization_barrier((far_chip, late_core))
    far_chip = to_next_chip(far_chip)
    keep, give = call(
        functools.partial(gradient_kernel, at=gradient_at),
        [(pup // 2, pup)] * 2,
        (from_chip, early_core, late_core, picture, measured, spec, pupil, field, token, *block_arrays, *lag_arrays),
        flops=4 * 10**10,
        spaces={8: pl.ANY},
    )
    half = keep + exchange(give, 1)
    bits = list(range(2, count.bit_length() - 1))
    for low, high in zip(bits[::2], bits[1::2]):
        half = half + ((exchange(half, 1 << low) + exchange(half, (1 << low) | (1 << high))) + exchange(half, 1 << high))
    if len(bits) % 2:
        half = half + exchange(half, 1 << bits[-1])
    last_round = [exchange(half, 2)]
    two_strata = lax.axis_size("depth") == 2
    if two_strata:
        last_round += [lax.ppermute(half, "depth", [(0, 1), (1, 0)]), across_depth_and_chip(half)]
    even, odd = call(
        functools.partial(blocks_kernel, at=block_const.at),
        [(planes * length, cols)] * 2,
        (from_chip, early_core, late_core, picture, far_chip, far_core, half, *block_arrays),
        spaces={6: pl.ANY},
    )
    even, *last_round = lax.optimization_barrier((even, *last_round))
    (joined,) = call(squares_kernel, [(pup // 2 + 8, pup)], (half, *last_round))
    other = exchange(joined, 1)
    squares = []
    if not two_strata:
        squares = [sum_over_depth(joined[pup // 2 :] + other[pup // 2 :])]
    new_objects, new_phase = call(
        functools.partial(
            second_kernel,
            at=block_const.at,
            psf_at=psf_const.at,
            arrays=len(block_arrays),
            cells=lax.axis_size("depth") * pup * pup,
            squares_apart=bool(squares),
        ),
        [picture.shape, phase.shape],
        (
            phase, amplitude, joined, other, *squares, even, odd, picture, measured,
            far_chip, far_core, *block_arrays, *psf_arrays,
        ),
    )
    return new_objects[None], new_phase[None]


def solution(mesh):
    return jax.shard_map(
        on_device,
        mesh=mesh,
        in_specs=(
            P("depth", None, "tile", None),
            P("depth", None, "tile", None),
            P("depth", None, None),
            P("depth", None, None),
        ),
        out_specs=(P("depth", None, "tile", None), P("depth", None, None)),
        check_vma=False,
    )
```

```python
import functools
import math

import jax
import jax.numpy as jnp
import ml_dtypes
import numpy as np
from jax import lax
from jax.experimental import pallas as pl
from jax.experimental.pallas import tpu as pltpu
from jax.sharding import PartitionSpec as P

HALF = 64
BACKGROUND = 0.1
STEP_SIZE = 0.3
EPSILON = 1e-06
STACKED = ("row_inverse",)
NEEDED_IN_ORDER = ("pupil_right", "pupil_left", "kernel_right")
VMEM_LIMIT = 32 * 1024 * 1024


def round_up(value, step):
    return -(-value // step) * step


def angles(left, right, length):
    return (2.0 * math.pi / length) * np.outer(left, right)


def halves(matrix):
    high = matrix.astype(np.float32).astype(ml_dtypes.bfloat16)
    low = (matrix - high.astype(np.float64)).astype(np.float32).astype(ml_dtypes.bfloat16)
    return high, low


def row_constants(rows, length):
    freqs = np.arange(length // 2) + 0.5
    theta = angles(freqs, np.arange(length), length)
    forward = np.concatenate([np.cos(theta), -np.sin(theta)], 0)
    inner = theta[:, HALF : HALF + rows]
    inverse = np.concatenate([np.cos(inner).T, -np.sin(inner).T], 1) * (2.0 / length)
    return forward, inverse


def col_constants(cols):
    half = cols // 2
    forward, inverse = [], []
    for parity in range(2):
        theta = angles(np.arange(half), 2 * np.arange(half) + parity, cols)
        c, s = np.cos(theta), np.sin(theta)
        forward.append(np.block([[c, -s], [s, c]]))
        inverse.append(np.block([[c.T, s.T], [-s.T, c.T]]) / cols)
    return forward, inverse


def kernel_constants(length, cols, ker, pad_rows, pad_cols):
    lags = np.arange(ker) - HALF
    theta = angles(np.arange(length // 2) + 0.5, lags, length)
    rows = np.zeros((length, pad_rows))
    rows[: length // 2, :ker] = np.cos(theta)
    rows[length // 2 :, :ker] = -np.sin(theta)
    half = cols // 2
    right = np.zeros((2 * pad_cols, 2 * cols))
    for parity in range(2):
        theta = angles(lags, 2 * np.arange(half) + parity, cols)
        c, s = np.cos(theta), np.sin(theta)
        at = parity * cols
        right[:ker, at : at + half] = c
        right[:ker, at + half : at + cols] = -s
        right[pad_cols : pad_cols + ker, at : at + half] = s
        right[pad_cols : pad_cols + ker, at + half : at + cols] = c
    return rows, right


def pupil_constants(pup, ker, pad_rows, pad_cols):
    theta = angles(np.arange(ker) - HALF, np.arange(pup), ker)
    real, imag = np.cos(theta), -np.sin(theta)
    right = np.zeros((2 * pup, 2 * pad_cols))
    right[:pup, :ker] = real.T
    right[:pup, pad_cols : pad_cols + ker] = imag.T
    right[pup:, :ker] = -imag.T
    right[pup:, pad_cols : pad_cols + ker] = real.T
    left = np.zeros((2 * pad_rows, 2 * pup))
    left[:ker, :pup] = real
    left[:ker, pup:] = -imag
    left[pad_rows : pad_rows + ker, :pup] = imag
    left[pad_rows : pad_rows + ker, pup:] = real
    return left, right


class Joined:
    def __init__(self, left, right):
        self.places, groups = {}, {}
        for name, matrix in right.items():
            high, low = halves(matrix)
            groups.setdefault(matrix.shape[0], []).append((name, np.concatenate([high, high, low], 0)))
        for name, matrix in left.items():
            high, low = halves(matrix)
            held = np.concatenate([high, low], 0) if name in STACKED else np.concatenate([high, low, high], 1)
            groups.setdefault("left", []).append((name, held))
        self.arrays = []
        for kind, members in groups.items():
            at = 0
            for name, block in members:
                rows, cols = block.shape
                start = (at, 0) if kind == "left" else (0, at)
                self.places[name] = (len(self.arrays), *start, rows, cols)
                at += rows if kind == "left" else cols
            blocks = [block for _, block in members]
            if kind == "left":
                width = max(block.shape[1] for block in blocks)
                blocks = [np.pad(block, ((0, 0), (0, width - block.shape[1]))) for block in blocks]
            self.arrays.append(np.concatenate(blocks, 0 if kind == "left" else 1))

    def at(self, *refs):
        return {
            name: refs[which].at[top : top + rows, first : first + cols]
            for name, (which, top, first, rows, cols) in self.places.items()
        }


def dot(left, right):
    return jnp.dot(left, right, preferred_element_type=jnp.float32)


def split(value):
    high = value.astype(jnp.bfloat16)
    low = (value - high.astype(jnp.float32)).astype(jnp.bfloat16)
    return high, low


def left_by(const, value):
    high, low = split(value)
    return dot(const[...], jnp.concatenate([high, high, low], 0))


def left_stacked(const, value):
    high, low = split(value)
    rows = const.shape[0] // 2
    both = dot(const[...], high)
    return both[:rows] + (both[rows:] + dot(const[:rows], low))


def right_by(value, const):
    high, low = split(value)
    return dot(jnp.concatenate([high, low, high], 1), const[...])


def sine_cosine(angle):
    turns = jnp.floor(angle * (2.0 / math.pi) + 0.5)
    rest = angle - turns * 1.5703125
    rest = rest - turns * 4.837512969970703e-4
    rest = rest - turns * 7.54978995489e-8
    square = rest * rest
    sine = rest + rest * square * (
        -1.6666654611e-1 + square * (8.3321608736e-3 + square * -1.9515295891e-4)
    )
    cosine = 1.0 - 0.5 * square + square * square * (
        4.166664568298827e-2 + square * (-1.388731625493765e-3 + square * 2.443315711809948e-5)
    )
    quadrant = turns.astype(jnp.int32) & 3
    swap = (quadrant & 1) == 1
    sine_out = jnp.where(swap, cosine, sine)
    cosine_out = jnp.where(swap, sine, cosine)
    sine_out = jnp.where(quadrant >= 2, -sine_out, sine_out)
    cosine_out = jnp.where((quadrant == 1) | (quadrant == 2), -cosine_out, cosine_out)
    return sine_out, cosine_out


def total(value):
    return jnp.sum(jnp.sum(value, axis=0, keepdims=True), axis=1, keepdims=True)


def weights(amplitude):
    pup = amplitude.shape[0]
    rows = lax.broadcasted_iota(jnp.int32, amplitude.shape, 0).astype(jnp.float32) - (pup - 1) / 2.0
    cols = lax.broadcasted_iota(jnp.int32, amplitude.shape, 1).astype(jnp.float32) - (pup - 1) / 2.0
    return jnp.where(rows * rows + cols * cols <= (pup / 2.0) ** 2, amplitude, 0.0)


def point_spread(phase, amplitude, const, wait_for=lambda name: None):
    weight = weights(amplitude)
    sine, cosine = sine_cosine(phase)
    pupil = jnp.concatenate([weight * cosine, weight * sine], 1)
    wait_for("pupil_right")
    across = right_by(pupil, const["pupil_right"])
    cols = across.shape[1] // 2
    wait_for("pupil_left")
    field = left_by(const["pupil_left"], jnp.concatenate([across[:, :cols], across[:, cols:]], 0))
    rows = field.shape[0] // 2
    intensity = field[:rows] * field[:rows] + field[rows:] * field[rows:]
    norm = 1.0 / total(intensity)
    left = left_by(const["kernel_rows"], intensity)
    freqs = left.shape[0] // 2
    wait_for("kernel_right")
    spectrum = right_by(jnp.concatenate([left[:freqs], left[freqs:]], 1), const["kernel_right"])
    return pupil, field, spectrum * norm, norm


def forward(strips, row_matrix, const, levels=None):
    sums, differences = [], []
    for plane, strip in enumerate(strips):
        half = strip.shape[1] // 2
        first, second = strip[:, :half], strip[:, half:]
        both = first + second
        if levels is not None:
            both = both - 2.0 * levels[plane]
        mixed = left_by(row_matrix, jnp.concatenate([both, first - second], 1))
        freqs = mixed.shape[0] // 2
        sums.append(jnp.concatenate([mixed[:freqs, :half], mixed[freqs:, :half]], 1))
        differences.append(jnp.concatenate([mixed[:freqs, half:], mixed[freqs:, half:]], 1))
    even = [right_by(jnp.concatenate(sums[p : p + 2], 0), const["forward_even"]) for p in range(0, len(sums), 2)]
    odd = [right_by(jnp.concatenate(differences[p : p + 2], 0), const["forward_odd"]) for p in range(0, len(sums), 2)]
    return even, odd


def inverse(even, odd, freqs, const):
    even = [right_by(spectrum, const["inverse_even"]) for spectrum in even]
    odd = [right_by(spectrum, const["inverse_odd"]) for spectrum in odd]
    strips = []
    for sums, differences in zip(even, odd):
        half = sums.shape[1] // 2
        for top in range(0, sums.shape[0], freqs):
            rows = slice(top, top + freqs)
            stacked = jnp.concatenate(
                [
                    jnp.concatenate([sums[rows, :half], differences[rows, :half]], 1),
                    jnp.concatenate([sums[rows, half:], differences[rows, half:]], 1),
                ],
                0,
            )
            mixed = left_stacked(const["row_inverse"], stacked)
            first, second = mixed[:, :half], mixed[:, half:]
            strips.append(jnp.concatenate([first + second, first - second], 1))
    return strips


def times(spectra, other, conjugate):
    half = other.shape[1] // 2
    products = []
    for spectrum in spectra:
        planes = spectrum.shape[0] // other.shape[0]
        real = jnp.concatenate([other[:, :half]] * planes, 0)
        imag = jnp.concatenate([other[:, half:]] * planes, 0)
        left, right = spectrum[:, :half], spectrum[:, half:]
        if conjugate:
            product = [left * real + right * imag, right * real - left * imag]
        else:
            product = [left * real - right * imag, left * imag + right * real]
        products.append(jnp.concatenate(product, 1))
    return products


def cross(firsts, seconds, freqs):
    summed = None
    for first, second in zip(firsts, seconds):
        half = first.shape[1] // 2
        left, right = first[:, :half], first[:, half:]
        real, imag = second[:, :half], second[:, half:]
        both = jnp.concatenate([left * real + right * imag, right * real - left * imag], 1)
        for top in range(0, both.shape[0], freqs):
            summed = both[top : top + freqs] if summed is None else summed + both[top : top + freqs]
    return summed


def is_even():
    return lax.axis_index("tile") % 2 == 0


def edge_rows(top, bottom):
    even = is_even()
    return [pl.multiple_of(jnp.where(even, *choice), 8) for choice in ((top, bottom), (bottom, top))]


def near_kernel(own, chip_out, sem):
    chip, _ = edge_rows(0, own.shape[1] - HALF)
    copy = pltpu.make_async_copy(own.at[:, pl.ds(chip, HALF), :], chip_out, sem)
    copy.start()
    copy.wait()


def first_kernel(
    phase, amplitude, own, observed, *refs, at, places, arrays,
):
    psf_refs, outs = refs[:arrays], refs[arrays + 1 : arrays + 9]
    pupil_out, field_out, spec_out, chip_out, core_out, early_out, late_out, means_out = outs
    psf_outs, (phase_in, amplitude_in, own_in, sems) = refs[arrays + 9 : -4], refs[-4:]
    planes, rows, cols = own.shape
    early = early_out.shape[0]
    objects_chip, objects_core = edge_rows(HALF, rows - 2 * HALF)
    observed_chip, observed_core = edge_rows(0, rows - HALF)
    pairs = [
        (phase, phase_in),
        (amplitude, amplitude_in),
        *zip(psf_refs, psf_outs),
        (own.at[:early, pl.ds(observed_core, HALF), :], early_out),
        (own.at[early:, pl.ds(observed_core, HALF), :], late_out),
        (own.at[:, pl.ds(objects_chip, HALF), :], chip_out.at[:planes]),
        (observed.at[:, pl.ds(observed_chip, HALF), :], chip_out.at[planes:]),
        (own.at[:, pl.ds(objects_core, HALF), :], core_out.at[:planes]),
        (observed.at[:, pl.ds(observed_core, HALF), :], core_out.at[planes:]),
        (own, own_in),
    ]
    copies = [pltpu.make_async_copy(source, target, sems.at[i]) for i, (source, target) in enumerate(pairs)]
    for i in (0, 1, *(2 + places[name][0] for name in NEEDED_IN_ORDER), *range(2 + arrays, len(copies))):
        copies[i].start()
    for copy in copies[:2]:
        copy.wait()

    def wait_for(name):
        copies[2 + places[name][0]].wait()

    pupil, field, spectrum, norm = point_spread(phase_in[...], amplitude_in[...], at(*psf_outs), wait_for)
    root = jnp.sqrt(norm)
    pupil_out[...] = pupil * root
    field_out[...] = field * root
    spec_out[...] = spectrum
    for copy in copies[2 + arrays :]:
        copy.wait()
    for p in range(planes):
        means_out[p] = jnp.broadcast_to(total(own_in[p]) * (1.0 / (rows * cols)), means_out.shape[1:])


def halo_rows(chip, core):
    even = is_even()
    return jnp.where(even, chip, core), jnp.where(even, core, chip)


def gradient_kernel(
    from_chip, early_core, late_core, own, observed, spec, pupil, field, means, *refs, at,
):
    planes, rows, cols = own.shape
    const = at(*refs[:-2])
    keep_out, give_out = refs[-2:]
    freqs = spec.shape[0]
    early = early_core.shape[0]
    strips = []
    for p in range(planes):
        above, below = halo_rows(from_chip[p], early_core[p] if p < early else late_core[p - early])
        strips.append(jnp.concatenate([above, own[p], below], 0))
    levels = [means[p][:1, :1] for p in range(planes)]
    even, odd = forward(strips, const["row_forward"], const, levels)
    blurred = inverse(times(even, spec[:, :cols], False), times(odd, spec[:, cols:], False), freqs, const)
    misfit = [1.0 - observed[p] / (blurred[p] + (levels[p] + BACKGROUND)) for p in range(planes)]
    weighted = misfit[0] * blurred[0]
    for p in range(1, planes):
        weighted = weighted + misfit[p] * blurred[p]
    mean = total(weighted)
    misfit_even, misfit_odd = forward(misfit, const["row_own"], const)
    shared = jnp.concatenate([cross(misfit_even, even, freqs), cross(misfit_odd, odd, freqs)], 1)
    across = right_by(shared, const["lag_right"])
    pad_cols = across.shape[1] // 2
    psf_grad = left_by(const["lag_left"], jnp.concatenate([across[:, :pad_cols], across[:, pad_cols:]], 0))
    far = field[...]
    pad_rows = far.shape[0] // 2
    real, imag = far[:pad_rows], far[pad_rows:]
    centred = 2.0 * (psf_grad - mean)
    back = left_by(const["adjoint_left"], jnp.concatenate([centred * real, centred * imag], 0))
    pup = back.shape[0] // 2
    back = right_by(jnp.concatenate([back[:pup], back[pup:]], 1), const["adjoint_right"])
    near = pupil[...]
    slope = back[:, pup:] * near[:, :pup] - back[:, :pup] * near[:, pup:]
    even_core = is_even()
    keep_out[...] = jnp.where(even_core, slope[: pup // 2], slope[pup // 2 :])
    give_out[...] = jnp.where(even_core, slope[pup // 2 :], slope[: pup // 2])


def square_sums(value):
    rows = value.shape[0]
    squared = value * value
    summed = squared[:8]
    for top in range(8, rows, 8):
        summed = summed + squared[top : top + 8]
    return summed


def squares_kernel(mine, received, *others):
    joined_out = others[-1]
    half = mine[...] + received[...]
    squares = square_sums(half)
    for first, second in zip(others[:-1:2], others[1:-1:2]):
        squares = squares + square_sums(first[...] + second[...])
    joined_out[: half.shape[0]] = half
    joined_out[half.shape[0] :] = squares


def blocks_kernel(from_chip, early_core, late_core, own, far_chip, far_core, _, *refs, at):
    planes = own.shape[0]
    const = at(*refs[:-2])
    even_out, odd_out = refs[-2:]
    early = early_core.shape[0]
    strips = []
    for p in range(planes):
        above, below = halo_rows(from_chip[p], early_core[p] if p < early else late_core[p - early])
        far_above, far_below = halo_rows(far_chip[p], far_core[p])
        strips.append(jnp.concatenate([far_above, above, own[p]], 0))
        strips.append(jnp.concatenate([own[p], below, far_below], 0))
    even, odd = forward(strips, const["row_forward"], const)
    even_out[...] = jnp.concatenate(even, 0)
    odd_out[...] = jnp.concatenate(odd, 0)


def second_kernel(phase, amplitude, mine, theirs, *refs, at, psf_at, arrays, cells, squares_apart):
    if squares_apart:
        squares, *refs = refs
    even, odd, own, observed, far_chip, far_core, *refs = refs
    planes, rows, cols = own.shape
    const = at(*refs[:arrays])
    psf_const = psf_at(*refs[arrays:-2])
    objects_out, phase_out = refs[-2:]
    half = phase.shape[0] // 2
    first, second = halo_rows(mine[:half], theirs[:half])
    slope = jnp.concatenate([first, second], 0)
    summed = squares[...] if squares_apart else mine[half:] + theirs[half:]
    mean_square = total(summed) * (1.0 / cells)
    updated = phase[...] - STEP_SIZE * slope / jnp.sqrt(mean_square + EPSILON)
    phase_out[...] = updated
    _, _, spec, _ = point_spread(updated, amplitude[...], psf_const)
    spec_even, spec_odd = spec[:, :cols], spec[:, cols:]
    freqs = spec.shape[0]
    pairs = range(0, even.shape[0], 2 * freqs)
    light = inverse(
        times([even[top : top + 2 * freqs] for top in pairs], spec_even, False),
        times([odd[top : top + 2 * freqs] for top in pairs], spec_odd, False),
        freqs, const,
    )
    ratios = []
    for p in range(planes):
        above, below = halo_rows(far_chip[planes + p], far_core[planes + p])
        blurred = jnp.concatenate(light[2 * p : 2 * p + 2], 0) + BACKGROUND
        ratios.append(jnp.concatenate([above, observed[p], below], 0) / blurred)
    ratio_even, ratio_odd = forward(ratios, const["row_forward"], const)
    correction = inverse(times(ratio_even, spec_even, True), times(ratio_odd, spec_odd, True), freqs, const)
    for p in range(planes):
        objects_out[p] = own[p] * correction[p]


def call(kernel, out_shapes, args, flops=10**6, spaces=None, scratch=()):
    outs = [
        jax.ShapeDtypeStruct(shape, jnp.float32) if isinstance(shape, tuple) else shape for shape in out_shapes
    ]
    spaces = spaces or {}
    return pl.pallas_call(
        kernel,
        out_shape=outs,
        in_specs=[pl.BlockSpec(memory_space=spaces.get(i, pltpu.VMEM)) for i in range(len(args))],
        out_specs=[pl.BlockSpec(memory_space=pltpu.VMEM)] * len(outs),
        scratch_shapes=scratch,
        compiler_params=pltpu.CompilerParams(vmem_limit_bytes=VMEM_LIMIT),
        cost_estimate=pl.CostEstimate(flops=flops, bytes_accessed=10**5, transcendentals=0),
    )(*args)


def to_next_chip(value):
    count = lax.axis_size("tile")
    return lax.ppermute(value, "tile", [(i, (i + 1 if i % 2 else i - 1) % count) for i in range(count)])


def exchange(value, step):
    return lax.ppermute(value, "tile", [(i, i ^ step) for i in range(lax.axis_size("tile"))])


def across_depth_and_chip(value):
    pairs = [(2 * t + d, 2 * (t ^ 2) + 1 - d) for t in range(lax.axis_size("tile")) for d in range(2)]
    return lax.ppermute(value, ("tile", "depth"), pairs)


def sum_over_depth(value):
    count = lax.axis_size("depth")
    if count & (count - 1):
        return lax.psum(value, "depth")
    for bit in range(count.bit_length() - 1):
        value = value + lax.ppermute(value, "depth", [(i, i ^ (1 << bit)) for i in range(count)])
    return value


def on_device(objects, observed, pupil_phase, pupil_amplitude):
    picture, measured, phase, amplitude = objects[0], observed[0], pupil_phase[0], pupil_amplitude[0]
    planes, rows, cols = picture.shape
    pup = phase.shape[0]
    count = lax.axis_size("tile")
    ker = 2 * HALF + 1
    length = rows + 2 * HALF
    pad_rows, pad_cols = round_up(ker, 16), round_up(ker, 128)
    row_forward, row_inverse = row_constants(rows, length)
    col_forward, col_inverse = col_constants(cols)
    kernel_rows, kernel_right = kernel_constants(length, cols, ker, pad_rows, pad_cols)
    pupil_left, pupil_right = pupil_constants(pup, ker, pad_rows, pad_cols)
    psf_const = Joined(
        {"pupil_left": pupil_left, "kernel_rows": kernel_rows},
        {"pupil_right": pupil_right, "kernel_right": kernel_right},
    )
    block_left = {"row_forward": row_forward, "row_inverse": row_inverse}
    block_right = {
        "forward_even": col_forward[0],
        "forward_odd": col_forward[1],
        "inverse_even": col_inverse[0],
        "inverse_odd": col_inverse[1],
    }
    block_const = Joined(block_left, block_right)
    lag_const = Joined(
        {
            "row_own": row_forward[:, HALF : HALF + rows],
            "lag_left": kernel_rows.T * (2.0 / length),
            "adjoint_left": pupil_left.T,
        },
        {"lag_right": kernel_right.T / cols, "adjoint_right": pupil_right.T},
    )
    psf_arrays, block_arrays, lag_arrays = (
        [jnp.asarray(array) for array in const.arrays] for const in (psf_const, block_const, lag_const)
    )

    def gradient_at(*refs):
        held = len(block_arrays)
        return {**block_const.at(*refs[:held]), **lag_const.at(*refs[held:])}

    in_hbm = [
        pltpu.with_memory_space_constraint(value, pltpu.HBM)
        for value in (phase, amplitude, picture, measured, *psf_arrays)
    ]
    (chip_rows,) = call(
        near_kernel, [(planes, HALF, cols)], in_hbm[2:3], scratch=[pltpu.SemaphoreType.DMA(())], spaces={0: pltpu.HBM}
    )
    from_chip = to_next_chip(chip_rows)
    pupil, field, spec, far_chip, far_core, early_rows, late_rows, means, *psf_arrays = call(
        functools.partial(first_kernel, at=psf_const.at, places=psf_const.places, arrays=len(psf_arrays)),
        [(pup, 2 * pup), (2 * pad_rows, pad_cols), (length // 2, 2 * cols)]
        + [(2 * planes, HALF, cols)] * 2
        + [(planes // 2, HALF, cols), (planes - planes // 2, HALF, cols), (planes, 8, 128)]
        + psf_arrays,
        (*in_hbm, chip_rows),
        flops=3 * 10**9,
        spaces={**dict.fromkeys(range(len(in_hbm)), pltpu.HBM), len(in_hbm): pl.ANY},
        scratch=[pltpu.VMEM(value.shape, jnp.float32) for value in (phase, amplitude, picture)]
        + [pltpu.SemaphoreType.DMA((9 + len(psf_arrays),))],
    )
    early_core, late_core, far_core = (exchange(value, 1) for value in (early_rows, late_rows, far_core))
    far_chip, late_core = lax.optimization_barrier((far_chip, late_core))
    far_chip = to_next_chip(far_chip)
    keep, give = call(
        functools.partial(gradient_kernel, at=gradient_at),
        [(pup // 2, pup)] * 2,
        (from_chip, early_core, late_core, picture, measured, spec, pupil, field, means, *block_arrays, *lag_arrays),
        flops=4 * 10**10,
    )
    half = keep + exchange(give, 1)
    bits = list(range(2, count.bit_length() - 1))
    for low, high in zip(bits[::2], bits[1::2]):
        half = half + ((exchange(half, 1 << low) + exchange(half, (1 << low) | (1 << high))) + exchange(half, 1 << high))
    if len(bits) % 2:
        half = half + exchange(half, 1 << bits[-1])
    last_round = [exchange(half, 2)]
    two_strata = lax.axis_size("depth") == 2
    if two_strata:
        last_round += [lax.ppermute(half, "depth", [(0, 1), (1, 0)]), across_depth_and_chip(half)]
    even, odd = call(
        functools.partial(blocks_kernel, at=block_const.at),
        [(planes * length, cols)] * 2,
        (from_chip, early_core, late_core, picture, far_chip, far_core, half, *block_arrays),
        spaces={6: pl.ANY},
    )
    even, *last_round = lax.optimization_barrier((even, *last_round))
    (joined,) = call(squares_kernel, [(pup // 2 + 8, pup)], (half, *last_round))
    other = exchange(joined, 1)
    squares = []
    if not two_strata:
        squares = [sum_over_depth(joined[pup // 2 :] + other[pup // 2 :])]
    new_objects, new_phase = call(
        functools.partial(
            second_kernel,
            at=block_const.at,
            psf_at=psf_const.at,
            arrays=len(block_arrays),
            cells=lax.axis_size("depth") * pup * pup,
            squares_apart=bool(squares),
        ),
        [picture.shape, phase.shape],
        (
            phase, amplitude, joined, other, *squares, even, odd, picture, measured,
            far_chip, far_core, *block_arrays, *psf_arrays,
        ),
    )
    return new_objects[None], new_phase[None]


def solution(mesh):
    return jax.shard_map(
        on_device,
        mesh=mesh,
        in_specs=(
            P("depth", None, "tile", None),
            P("depth", None, "tile", None),
            P("depth", None, None),
            P("depth", None, None),
        ),
        out_specs=(P("depth", None, "tile", None), P("depth", None, None)),
        check_vma=False,
    )
```

```python
import functools
import math

import jax
import jax.numpy as jnp
import ml_dtypes
import numpy as np
from jax import lax
from jax.experimental import pallas as pl
from jax.experimental.pallas import tpu as pltpu
from jax.sharding import PartitionSpec as P

HALF = 64
BACKGROUND = 0.1
STEP_SIZE = 0.3
EPSILON = 1e-06
STACKED = ("row_inverse",)
NEEDED_IN_ORDER = ("pupil_right", "pupil_left", "kernel_right")
VMEM_LIMIT = 32 * 1024 * 1024


def round_up(value, step):
    return -(-value // step) * step


def angles(left, right, length):
    return (2.0 * math.pi / length) * np.outer(left, right)


def halves(matrix):
    high = matrix.astype(np.float32).astype(ml_dtypes.bfloat16)
    low = (matrix - high.astype(np.float64)).astype(np.float32).astype(ml_dtypes.bfloat16)
    return high, low


def row_constants(rows, length):
    freqs = np.arange(length // 2) + 0.5
    theta = angles(freqs, np.arange(length), length)
    forward = np.concatenate([np.cos(theta), -np.sin(theta)], 0)
    inner = theta[:, HALF : HALF + rows]
    inverse = np.concatenate([np.cos(inner).T, -np.sin(inner).T], 1) * (2.0 / length)
    return forward, inverse


def col_constants(cols):
    half = cols // 2
    forward, inverse = [], []
    for parity in range(2):
        theta = angles(np.arange(half), 2 * np.arange(half) + parity, cols)
        c, s = np.cos(theta), np.sin(theta)
        forward.append(np.block([[c, -s], [s, c]]))
        inverse.append(np.block([[c.T, s.T], [-s.T, c.T]]) / cols)
    return forward, inverse


def kernel_constants(length, cols, ker, pad_rows, pad_cols):
    lags = np.arange(ker) - HALF
    theta = angles(np.arange(length // 2) + 0.5, lags, length)
    rows = np.zeros((length, pad_rows))
    rows[: length // 2, :ker] = np.cos(theta)
    rows[length // 2 :, :ker] = -np.sin(theta)
    half = cols // 2
    right = np.zeros((2 * pad_cols, 2 * cols))
    for parity in range(2):
        theta = angles(lags, 2 * np.arange(half) + parity, cols)
        c, s = np.cos(theta), np.sin(theta)
        at = parity * cols
        right[:ker, at : at + half] = c
        right[:ker, at + half : at + cols] = -s
        right[pad_cols : pad_cols + ker, at : at + half] = s
        right[pad_cols : pad_cols + ker, at + half : at + cols] = c
    return rows, right


def pupil_constants(pup, ker, pad_rows, pad_cols):
    theta = angles(np.arange(ker) - HALF, np.arange(pup), ker)
    real, imag = np.cos(theta), -np.sin(theta)
    right = np.zeros((2 * pup, 2 * pad_cols))
    right[:pup, :ker] = real.T
    right[:pup, pad_cols : pad_cols + ker] = imag.T
    right[pup:, :ker] = -imag.T
    right[pup:, pad_cols : pad_cols + ker] = real.T
    left = np.zeros((2 * pad_rows, 2 * pup))
    left[:ker, :pup] = real
    left[:ker, pup:] = -imag
    left[pad_rows : pad_rows + ker, :pup] = imag
    left[pad_rows : pad_rows + ker, pup:] = real
    return left, right


class Joined:
    def __init__(self, left, right):
        self.places, groups = {}, {}
        for name, matrix in right.items():
            high, low = halves(matrix)
            groups.setdefault(matrix.shape[0], []).append((name, np.concatenate([high, high, low], 0)))
        for name, matrix in left.items():
            high, low = halves(matrix)
            held = np.concatenate([high, low], 0) if name in STACKED else np.concatenate([high, low, high], 1)
            groups.setdefault("left", []).append((name, held))
        self.arrays = []
        for kind, members in groups.items():
            at = 0
            for name, block in members:
                rows, cols = block.shape
                start = (at, 0) if kind == "left" else (0, at)
                self.places[name] = (len(self.arrays), *start, rows, cols)
                at += rows if kind == "left" else cols
            blocks = [block for _, block in members]
            if kind == "left":
                width = max(block.shape[1] for block in blocks)
                blocks = [np.pad(block, ((0, 0), (0, width - block.shape[1]))) for block in blocks]
            self.arrays.append(np.concatenate(blocks, 0 if kind == "left" else 1))

    def at(self, *refs):
        return {
            name: refs[which].at[top : top + rows, first : first + cols]
            for name, (which, top, first, rows, cols) in self.places.items()
        }


def dot(left, right):
    return jnp.dot(left, right, preferred_element_type=jnp.float32)


def split(value):
    high = value.astype(jnp.bfloat16)
    low = (value - high.astype(jnp.float32)).astype(jnp.bfloat16)
    return high, low


def left_by(const, value):
    high, low = split(value)
    return dot(const[...], jnp.concatenate([high, high, low], 0))


def left_stacked(const, value):
    high, low = split(value)
    rows = const.shape[0] // 2
    both = dot(const[...], high)
    return both[:rows] + (both[rows:] + dot(const[:rows], low))


def right_by(value, const):
    high, low = split(value)
    return dot(jnp.concatenate([high, low, high], 1), const[...])


def sine_cosine(angle):
    turns = jnp.floor(angle * (2.0 / math.pi) + 0.5)
    rest = angle - turns * 1.5703125
    rest = rest - turns * 4.837512969970703e-4
    rest = rest - turns * 7.54978995489e-8
    square = rest * rest
    sine = rest + rest * square * (
        -1.6666654611e-1 + square * (8.3321608736e-3 + square * -1.9515295891e-4)
    )
    cosine = 1.0 - 0.5 * square + square * square * (
        4.166664568298827e-2 + square * (-1.388731625493765e-3 + square * 2.443315711809948e-5)
    )
    quadrant = turns.astype(jnp.int32) & 3
    swap = (quadrant & 1) == 1
    sine_out = jnp.where(swap, cosine, sine)
    cosine_out = jnp.where(swap, sine, cosine)
    sine_out = jnp.where(quadrant >= 2, -sine_out, sine_out)
    cosine_out = jnp.where((quadrant == 1) | (quadrant == 2), -cosine_out, cosine_out)
    return sine_out, cosine_out


def total(value):
    return jnp.sum(jnp.sum(value, axis=0, keepdims=True), axis=1, keepdims=True)


def weights(amplitude):
    pup = amplitude.shape[0]
    rows = lax.broadcasted_iota(jnp.int32, amplitude.shape, 0).astype(jnp.float32) - (pup - 1) / 2.0
    cols = lax.broadcasted_iota(jnp.int32, amplitude.shape, 1).astype(jnp.float32) - (pup - 1) / 2.0
    return jnp.where(rows * rows + cols * cols <= (pup / 2.0) ** 2, amplitude, 0.0)


def point_spread(phase, amplitude, const, wait_for=lambda name: None):
    weight = weights(amplitude)
    sine, cosine = sine_cosine(phase)
    pupil = jnp.concatenate([weight * cosine, weight * sine], 1)
    wait_for("pupil_right")
    across = right_by(pupil, const["pupil_right"])
    cols = across.shape[1] // 2
    wait_for("pupil_left")
    field = left_by(const["pupil_left"], jnp.concatenate([across[:, :cols], across[:, cols:]], 0))
    rows = field.shape[0] // 2
    intensity = field[:rows] * field[:rows] + field[rows:] * field[rows:]
    norm = 1.0 / total(intensity)
    left = left_by(const["kernel_rows"], intensity)
    freqs = left.shape[0] // 2
    wait_for("kernel_right")
    spectrum = right_by(jnp.concatenate([left[:freqs], left[freqs:]], 1), const["kernel_right"])
    return pupil, field, spectrum * norm, norm


def forward(strips, row_matrix, const, levels=None):
    sums, differences = [], []
    for plane, strip in enumerate(strips):
        half = strip.shape[1] // 2
        first, second = strip[:, :half], strip[:, half:]
        both = first + second
        if levels is not None:
            both = both - 2.0 * levels[plane]
        mixed = left_by(row_matrix, jnp.concatenate([both, first - second], 1))
        freqs = mixed.shape[0] // 2
        sums.append(jnp.concatenate([mixed[:freqs, :half], mixed[freqs:, :half]], 1))
        differences.append(jnp.concatenate([mixed[:freqs, half:], mixed[freqs:, half:]], 1))
    even = [right_by(jnp.concatenate(sums[p : p + 2], 0), const["forward_even"]) for p in range(0, len(sums), 2)]
    odd = [right_by(jnp.concatenate(differences[p : p + 2], 0), const["forward_odd"]) for p in range(0, len(sums), 2)]
    return even, odd


def inverse(even, odd, freqs, const):
    even = [right_by(spectrum, const["inverse_even"]) for spectrum in even]
    odd = [right_by(spectrum, const["inverse_odd"]) for spectrum in odd]
    strips = []
    for sums, differences in zip(even, odd):
        half = sums.shape[1] // 2
        for top in range(0, sums.shape[0], freqs):
            rows = slice(top, top + freqs)
            stacked = jnp.concatenate(
                [
                    jnp.concatenate([sums[rows, :half], differences[rows, :half]], 1),
                    jnp.concatenate([sums[rows, half:], differences[rows, half:]], 1),
                ],
                0,
            )
            mixed = left_stacked(const["row_inverse"], stacked)
            first, second = mixed[:, :half], mixed[:, half:]
            strips.append(jnp.concatenate([first + second, first - second], 1))
    return strips


def times(spectra, other, conjugate):
    half = other.shape[1] // 2
    products = []
    for spectrum in spectra:
        planes = spectrum.shape[0] // other.shape[0]
        real = jnp.concatenate([other[:, :half]] * planes, 0)
        imag = jnp.concatenate([other[:, half:]] * planes, 0)
        left, right = spectrum[:, :half], spectrum[:, half:]
        if conjugate:
            product = [left * real + right * imag, right * real - left * imag]
        else:
            product = [left * real - right * imag, left * imag + right * real]
        products.append(jnp.concatenate(product, 1))
    return products


def cross(firsts, seconds, freqs):
    summed = None
    for first, second in zip(firsts, seconds):
        half = first.shape[1] // 2
        left, right = first[:, :half], first[:, half:]
        real, imag = second[:, :half], second[:, half:]
        both = jnp.concatenate([left * real + right * imag, right * real - left * imag], 1)
        for top in range(0, both.shape[0], freqs):
            summed = both[top : top + freqs] if summed is None else summed + both[top : top + freqs]
    return summed


def is_even():
    return lax.axis_index("tile") % 2 == 0


def edge_rows(top, bottom):
    even = is_even()
    return [pl.multiple_of(jnp.where(even, *choice), 8) for choice in ((top, bottom), (bottom, top))]


def near_kernel(own, chip_out, sem):
    chip, _ = edge_rows(0, own.shape[1] - HALF)
    copy = pltpu.make_async_copy(own.at[:, pl.ds(chip, HALF), :], chip_out, sem)
    copy.start()
    copy.wait()


def first_kernel(
    phase, amplitude, own, observed, *refs, at, places, arrays,
):
    psf_refs, outs = refs[:arrays], refs[arrays + 1 : arrays + 9]
    pupil_out, field_out, spec_out, chip_out, core_out, early_out, late_out, means_out = outs
    psf_outs, (phase_in, amplitude_in, own_in, sems) = refs[arrays + 9 : -4], refs[-4:]
    planes, rows, cols = own.shape
    early = early_out.shape[0]
    objects_chip, objects_core = edge_rows(HALF, rows - 2 * HALF)
    observed_chip, observed_core = edge_rows(0, rows - HALF)
    pairs = [
        (phase, phase_in),
        (amplitude, amplitude_in),
        *zip(psf_refs, psf_outs),
        (own.at[:early, pl.ds(observed_core, HALF), :], early_out),
        (own.at[early:, pl.ds(observed_core, HALF), :], late_out),
        (own.at[:, pl.ds(objects_chip, HALF), :], chip_out.at[:planes]),
        (observed.at[:, pl.ds(observed_chip, HALF), :], chip_out.at[planes:]),
        (own.at[:, pl.ds(objects_core, HALF), :], core_out.at[:planes]),
        (observed.at[:, pl.ds(observed_core, HALF), :], core_out.at[planes:]),
        (own, own_in),
    ]
    copies = [pltpu.make_async_copy(source, target, sems.at[i]) for i, (source, target) in enumerate(pairs)]
    for i in (0, 1, *(2 + places[name][0] for name in NEEDED_IN_ORDER), *range(2 + arrays, len(copies))):
        copies[i].start()
    for copy in copies[:2]:
        copy.wait()

    def wait_for(name):
        copies[2 + places[name][0]].wait()

    pupil, field, spectrum, norm = point_spread(phase_in[...], amplitude_in[...], at(*psf_outs), wait_for)
    root = jnp.sqrt(norm)
    pupil_out[...] = pupil * root
    field_out[...] = field * root
    spec_out[...] = spectrum
    for copy in copies[2 + arrays :]:
        copy.wait()
    for p in range(planes):
        means_out[p] = jnp.broadcast_to(total(own_in[p]) * (1.0 / (rows * cols)), means_out.shape[1:])


def halo_rows(chip, core):
    even = is_even()
    return jnp.where(even, chip, core), jnp.where(even, core, chip)


def gradient_kernel(
    from_chip, early_core, late_core, own, observed, spec, pupil, field, means, *refs, at,
):
    planes, rows, cols = own.shape
    const = at(*refs[:-2])
    keep_out, give_out = refs[-2:]
    freqs = spec.shape[0]
    early = early_core.shape[0]
    strips = []
    for p in range(planes):
        above, below = halo_rows(from_chip[p], early_core[p] if p < early else late_core[p - early])
        strips.append(jnp.concatenate([above, own[p], below], 0))
    levels = [means[p][:1, :1] for p in range(planes)]
    even, odd = forward(strips, const["row_forward"], const, levels)
    blurred = inverse(times(even, spec[:, :cols], False), times(odd, spec[:, cols:], False), freqs, const)
    misfit = [1.0 - observed[p] / (blurred[p] + (levels[p] + BACKGROUND)) for p in range(planes)]
    weighted = misfit[0] * blurred[0]
    for p in range(1, planes):
        weighted = weighted + misfit[p] * blurred[p]
    mean = total(weighted)
    misfit_even, misfit_odd = forward(misfit, const["row_own"], const)
    shared = jnp.concatenate([cross(misfit_even, even, freqs), cross(misfit_odd, odd, freqs)], 1)
    across = right_by(shared, const["lag_right"])
    pad_cols = across.shape[1] // 2
    psf_grad = left_by(const["lag_left"], jnp.concatenate([across[:, :pad_cols], across[:, pad_cols:]], 0))
    far = field[...]
    pad_rows = far.shape[0] // 2
    real, imag = far[:pad_rows], far[pad_rows:]
    centred = 2.0 * (psf_grad - mean)
    back = left_by(const["adjoint_left"], jnp.concatenate([centred * real, centred * imag], 0))
    pup = back.shape[0] // 2
    back = right_by(jnp.concatenate([back[:pup], back[pup:]], 1), const["adjoint_right"])
    near = pupil[...]
    slope = back[:, pup:] * near[:, :pup] - back[:, :pup] * near[:, pup:]
    even_core = is_even()
    keep_out[...] = jnp.where(even_core, slope[: pup // 2], slope[pup // 2 :])
    give_out[...] = jnp.where(even_core, slope[pup // 2 :], slope[: pup // 2])


def square_sums(value):
    rows = value.shape[0]
    squared = value * value
    summed = squared[:8]
    for top in range(8, rows, 8):
        summed = summed + squared[top : top + 8]
    return summed


def squares_kernel(mine, received, *others):
    joined_out = others[-1]
    half = mine[...] + received[...]
    squares = square_sums(half)
    for first, second in zip(others[:-1:2], others[1:-1:2]):
        squares = squares + square_sums(first[...] + second[...])
    joined_out[: half.shape[0]] = half
    joined_out[half.shape[0] :] = squares


def blocks_kernel(from_chip, early_core, late_core, own, far_chip, far_core, _, *refs, at):
    planes = own.shape[0]
    const = at(*refs[:-2])
    even_out, odd_out = refs[-2:]
    early = early_core.shape[0]
    strips = []
    for p in range(planes):
        above, below = halo_rows(from_chip[p], early_core[p] if p < early else late_core[p - early])
        far_above, far_below = halo_rows(far_chip[p], far_core[p])
        strips.append(jnp.concatenate([far_above, above, own[p]], 0))
        strips.append(jnp.concatenate([own[p], below, far_below], 0))
    even, odd = forward(strips, const["row_forward"], const)
    even_out[...] = jnp.concatenate(even, 0)
    odd_out[...] = jnp.concatenate(odd, 0)


def second_kernel(phase, amplitude, mine, theirs, *refs, at, psf_at, arrays, cells, squares_apart):
    if squares_apart:
        squares, *refs = refs
    even, odd, own, observed, far_chip, far_core, *refs = refs
    planes, rows, cols = own.shape
    const = at(*refs[:arrays])
    psf_const = psf_at(*refs[arrays:-5])
    objects_out, phase_out, objects, new_phase, sems = refs[-5:]
    writes = [pltpu.make_async_copy(new_phase, phase_out, sems.at[planes])]
    half = phase.shape[0] // 2
    first, second = halo_rows(mine[:half], theirs[:half])
    slope = jnp.concatenate([first, second], 0)
    summed = squares[...] if squares_apart else mine[half:] + theirs[half:]
    mean_square = total(summed) * (1.0 / cells)
    updated = phase[...] - STEP_SIZE * slope / jnp.sqrt(mean_square + EPSILON)
    new_phase[...] = updated
    writes[0].start()
    _, _, spec, _ = point_spread(updated, amplitude[...], psf_const)
    spec_even, spec_odd = spec[:, :cols], spec[:, cols:]
    freqs = spec.shape[0]
    pairs = range(0, even.shape[0], 2 * freqs)
    light = inverse(
        times([even[top : top + 2 * freqs] for top in pairs], spec_even, False),
        times([odd[top : top + 2 * freqs] for top in pairs], spec_odd, False),
        freqs, const,
    )
    ratios = []
    for p in range(planes):
        above, below = halo_rows(far_chip[planes + p], far_core[planes + p])
        blurred = jnp.concatenate(light[2 * p : 2 * p + 2], 0) + BACKGROUND
        ratios.append(jnp.concatenate([above, observed[p], below], 0) / blurred)
    ratio_even, ratio_odd = forward(ratios, const["row_forward"], const)
    correction = inverse(times(ratio_even, spec_even, True), times(ratio_odd, spec_odd, True), freqs, const)
    for p in range(planes):
        objects[p] = own[p] * correction[p]
        writes.append(pltpu.make_async_copy(objects.at[p], objects_out.at[p], sems.at[p]))
        writes[-1].start()
    for write in writes:
        write.wait()


def call(kernel, out_shapes, args, flops=10**6, spaces=None, scratch=(), out_space=pltpu.VMEM):
    outs = [
        jax.ShapeDtypeStruct(shape, jnp.float32) if isinstance(shape, tuple) else shape for shape in out_shapes
    ]
    spaces = spaces or {}
    return pl.pallas_call(
        kernel,
        out_shape=outs,
        in_specs=[pl.BlockSpec(memory_space=spaces.get(i, pltpu.VMEM)) for i in range(len(args))],
        out_specs=[pl.BlockSpec(memory_space=out_space)] * len(outs),
        scratch_shapes=scratch,
        compiler_params=pltpu.CompilerParams(vmem_limit_bytes=VMEM_LIMIT),
        cost_estimate=pl.CostEstimate(flops=flops, bytes_accessed=10**5, transcendentals=0),
    )(*args)


def to_next_chip(value):
    count = lax.axis_size("tile")
    return lax.ppermute(value, "tile", [(i, (i + 1 if i % 2 else i - 1) % count) for i in range(count)])


def exchange(value, step):
    return lax.ppermute(value, "tile", [(i, i ^ step) for i in range(lax.axis_size("tile"))])


def across_depth_and_chip(value):
    pairs = [(2 * t + d, 2 * (t ^ 2) + 1 - d) for t in range(lax.axis_size("tile")) for d in range(2)]
    return lax.ppermute(value, ("tile", "depth"), pairs)


def sum_over_depth(value):
    count = lax.axis_size("depth")
    if count & (count - 1):
        return lax.psum(value, "depth")
    for bit in range(count.bit_length() - 1):
        value = value + lax.ppermute(value, "depth", [(i, i ^ (1 << bit)) for i in range(count)])
    return value


def on_device(objects, observed, pupil_phase, pupil_amplitude):
    picture, measured, phase, amplitude = objects[0], observed[0], pupil_phase[0], pupil_amplitude[0]
    planes, rows, cols = picture.shape
    pup = phase.shape[0]
    count = lax.axis_size("tile")
    ker = 2 * HALF + 1
    length = rows + 2 * HALF
    pad_rows, pad_cols = round_up(ker, 16), round_up(ker, 128)
    row_forward, row_inverse = row_constants(rows, length)
    col_forward, col_inverse = col_constants(cols)
    kernel_rows, kernel_right = kernel_constants(length, cols, ker, pad_rows, pad_cols)
    pupil_left, pupil_right = pupil_constants(pup, ker, pad_rows, pad_cols)
    psf_const = Joined(
        {"pupil_left": pupil_left, "kernel_rows": kernel_rows},
        {"pupil_right": pupil_right, "kernel_right": kernel_right},
    )
    block_left = {"row_forward": row_forward, "row_inverse": row_inverse}
    block_right = {
        "forward_even": col_forward[0],
        "forward_odd": col_forward[1],
        "inverse_even": col_inverse[0],
        "inverse_odd": col_inverse[1],
    }
    block_const = Joined(block_left, block_right)
    lag_const = Joined(
        {
            "row_own": row_forward[:, HALF : HALF + rows],
            "lag_left": kernel_rows.T * (2.0 / length),
            "adjoint_left": pupil_left.T,
        },
        {"lag_right": kernel_right.T / cols, "adjoint_right": pupil_right.T},
    )
    psf_arrays, block_arrays, lag_arrays = (
        [jnp.asarray(array) for array in const.arrays] for const in (psf_const, block_const, lag_const)
    )

    def gradient_at(*refs):
        held = len(block_arrays)
        return {**block_const.at(*refs[:held]), **lag_const.at(*refs[held:])}

    in_hbm = [
        pltpu.with_memory_space_constraint(value, pltpu.HBM)
        for value in (phase, amplitude, picture, measured, *psf_arrays)
    ]
    (chip_rows,) = call(
        near_kernel, [(planes, HALF, cols)], in_hbm[2:3], scratch=[pltpu.SemaphoreType.DMA(())], spaces={0: pltpu.HBM}
    )
    from_chip = to_next_chip(chip_rows)
    pupil, field, spec, far_chip, far_core, early_rows, late_rows, means, *psf_arrays = call(
        functools.partial(first_kernel, at=psf_const.at, places=psf_const.places, arrays=len(psf_arrays)),
        [(pup, 2 * pup), (2 * pad_rows, pad_cols), (length // 2, 2 * cols)]
        + [(2 * planes, HALF, cols)] * 2
        + [(planes // 2, HALF, cols), (planes - planes // 2, HALF, cols), (planes, 8, 128)]
        + psf_arrays,
        (*in_hbm, chip_rows),
        flops=3 * 10**9,
        spaces={**dict.fromkeys(range(len(in_hbm)), pltpu.HBM), len(in_hbm): pl.ANY},
        scratch=[pltpu.VMEM(value.shape, jnp.float32) for value in (phase, amplitude, picture)]
        + [pltpu.SemaphoreType.DMA((9 + len(psf_arrays),))],
    )
    early_core, late_core, far_core = (exchange(value, 1) for value in (early_rows, late_rows, far_core))
    far_chip, late_core = lax.optimization_barrier((far_chip, late_core))
    far_chip = to_next_chip(far_chip)
    keep, give = call(
        functools.partial(gradient_kernel, at=gradient_at),
        [(pup // 2, pup)] * 2,
        (from_chip, early_core, late_core, picture, measured, spec, pupil, field, means, *block_arrays, *lag_arrays),
        flops=4 * 10**10,
    )
    half = keep + exchange(give, 1)
    bits = list(range(2, count.bit_length() - 1))
    for low, high in zip(bits[::2], bits[1::2]):
        half = half + ((exchange(half, 1 << low) + exchange(half, (1 << low) | (1 << high))) + exchange(half, 1 << high))
    if len(bits) % 2:
        half = half + exchange(half, 1 << bits[-1])
    last_round = [exchange(half, 2)]
    two_strata = lax.axis_size("depth") == 2
    if two_strata:
        last_round += [lax.ppermute(half, "depth", [(0, 1), (1, 0)]), across_depth_and_chip(half)]
    even, odd = call(
        functools.partial(blocks_kernel, at=block_const.at),
        [(planes * length, cols)] * 2,
        (from_chip, early_core, late_core, picture, far_chip, far_core, half, *block_arrays),
        spaces={6: pl.ANY},
    )
    even, *last_round = lax.optimization_barrier((even, *last_round))
    (joined,) = call(squares_kernel, [(pup // 2 + 8, pup)], (half, *last_round))
    other = exchange(joined, 1)
    squares = []
    if not two_strata:
        squares = [sum_over_depth(joined[pup // 2 :] + other[pup // 2 :])]
    new_objects, new_phase = call(
        functools.partial(
            second_kernel,
            at=block_const.at,
            psf_at=psf_const.at,
            arrays=len(block_arrays),
            cells=lax.axis_size("depth") * pup * pup,
            squares_apart=bool(squares),
        ),
        [picture.shape, phase.shape],
        (
            phase, amplitude, joined, other, *squares, even, odd, picture, measured,
            far_chip, far_core, *block_arrays, *psf_arrays,
        ),
        scratch=[pltpu.VMEM(value.shape, jnp.float32) for value in (picture, phase)]
        + [pltpu.SemaphoreType.DMA((planes + 1,))],
        out_space=pltpu.HBM,
    )
    return new_objects[None], new_phase[None]


def solution(mesh):
    return jax.shard_map(
        on_device,
        mesh=mesh,
        in_specs=(
            P("depth", None, "tile", None),
            P("depth", None, "tile", None),
            P("depth", None, None),
            P("depth", None, None),
        ),
        out_specs=(P("depth", None, "tile", None), P("depth", None, None)),
        check_vma=False,
    )
```

```python
import functools
import math

import jax
import jax.numpy as jnp
import ml_dtypes
import numpy as np
from jax import lax
from jax.experimental import pallas as pl
from jax.experimental.pallas import tpu as pltpu
from jax.sharding import PartitionSpec as P

HALF = 64
BACKGROUND = 0.1
STEP_SIZE = 0.3
EPSILON = 1e-06
STACKED = ("row_inverse",)
NEEDED_IN_ORDER = ("pupil_right", "pupil_left", "kernel_right")
VMEM_LIMIT = 32 * 1024 * 1024


def round_up(value, step):
    return -(-value // step) * step


def angles(left, right, length):
    return (2.0 * math.pi / length) * np.outer(left, right)


def halves(matrix):
    high = matrix.astype(np.float32).astype(ml_dtypes.bfloat16)
    low = (matrix - high.astype(np.float64)).astype(np.float32).astype(ml_dtypes.bfloat16)
    return high, low


def row_constants(rows, length):
    freqs = np.arange(length // 2) + 0.5
    theta = angles(freqs, np.arange(length), length)
    forward = np.concatenate([np.cos(theta), -np.sin(theta)], 0)
    inner = theta[:, HALF : HALF + rows]
    inverse = np.concatenate([np.cos(inner).T, -np.sin(inner).T], 1) * (2.0 / length)
    return forward, inverse


def col_constants(cols):
    half = cols // 2
    forward, inverse = [], []
    for parity in range(2):
        theta = angles(np.arange(half), 2 * np.arange(half) + parity, cols)
        c, s = np.cos(theta), np.sin(theta)
        forward.append(np.block([[c, -s], [s, c]]))
        inverse.append(np.block([[c.T, s.T], [-s.T, c.T]]) / cols)
    return forward, inverse


def kernel_constants(length, cols, ker, pad_rows, pad_cols):
    lags = np.arange(ker) - HALF
    theta = angles(np.arange(length // 2) + 0.5, lags, length)
    rows = np.zeros((length, pad_rows))
    rows[: length // 2, :ker] = np.cos(theta)
    rows[length // 2 :, :ker] = -np.sin(theta)
    half = cols // 2
    right = np.zeros((2 * pad_cols, 2 * cols))
    for parity in range(2):
        theta = angles(lags, 2 * np.arange(half) + parity, cols)
        c, s = np.cos(theta), np.sin(theta)
        at = parity * cols
        right[:ker, at : at + half] = c
        right[:ker, at + half : at + cols] = -s
        right[pad_cols : pad_cols + ker, at : at + half] = s
        right[pad_cols : pad_cols + ker, at + half : at + cols] = c
    return rows, right


def pupil_constants(pup, ker, pad_rows, pad_cols):
    theta = angles(np.arange(ker) - HALF, np.arange(pup), ker)
    real, imag = np.cos(theta), -np.sin(theta)
    right = np.zeros((2 * pup, 2 * pad_cols))
    right[:pup, :ker] = real.T
    right[:pup, pad_cols : pad_cols + ker] = imag.T
    right[pup:, :ker] = -imag.T
    right[pup:, pad_cols : pad_cols + ker] = real.T
    left = np.zeros((2 * pad_rows, 2 * pup))
    left[:ker, :pup] = real
    left[:ker, pup:] = -imag
    left[pad_rows : pad_rows + ker, :pup] = imag
    left[pad_rows : pad_rows + ker, pup:] = real
    return left, right


class Joined:
    def __init__(self, left, right):
        self.places, groups = {}, {}
        for name, matrix in right.items():
            high, low = halves(matrix)
            groups.setdefault(matrix.shape[0], []).append((name, np.concatenate([high, high, low], 0)))
        for name, matrix in left.items():
            high, low = halves(matrix)
            held = np.concatenate([high, low], 0) if name in STACKED else np.concatenate([high, low, high], 1)
            groups.setdefault("left", []).append((name, held))
        self.arrays = []
        for kind, members in groups.items():
            at = 0
            for name, block in members:
                rows, cols = block.shape
                start = (at, 0) if kind == "left" else (0, at)
                self.places[name] = (len(self.arrays), *start, rows, cols)
                at += rows if kind == "left" else cols
            blocks = [block for _, block in members]
            if kind == "left":
                width = max(block.shape[1] for block in blocks)
                blocks = [np.pad(block, ((0, 0), (0, width - block.shape[1]))) for block in blocks]
            self.arrays.append(np.concatenate(blocks, 0 if kind == "left" else 1))

    def at(self, *refs):
        return {
            name: refs[which].at[top : top + rows, first : first + cols]
            for name, (which, top, first, rows, cols) in self.places.items()
        }


def dot(left, right):
    return jnp.dot(left, right, preferred_element_type=jnp.float32)


def split(value):
    high = value.astype(jnp.bfloat16)
    low = (value - high.astype(jnp.float32)).astype(jnp.bfloat16)
    return high, low


def left_by(const, value):
    high, low = split(value)
    return dot(const[...], jnp.concatenate([high, high, low], 0))


def left_stacked(const, value):
    high, low = split(value)
    rows = const.shape[0] // 2
    both = dot(const[...], high)
    return both[:rows] + (both[rows:] + dot(const[:rows], low))


def right_by(value, const):
    high, low = split(value)
    return dot(jnp.concatenate([high, low, high], 1), const[...])


def sine_cosine(angle):
    turns = jnp.floor(angle * (2.0 / math.pi) + 0.5)
    rest = angle - turns * 1.5703125
    rest = rest - turns * 4.837512969970703e-4
    rest = rest - turns * 7.54978995489e-8
    square = rest * rest
    sine = rest + rest * square * (
        -1.6666654611e-1 + square * (8.3321608736e-3 + square * -1.9515295891e-4)
    )
    cosine = 1.0 - 0.5 * square + square * square * (
        4.166664568298827e-2 + square * (-1.388731625493765e-3 + square * 2.443315711809948e-5)
    )
    quadrant = turns.astype(jnp.int32) & 3
    swap = (quadrant & 1) == 1
    sine_out = jnp.where(swap, cosine, sine)
    cosine_out = jnp.where(swap, sine, cosine)
    sine_out = jnp.where(quadrant >= 2, -sine_out, sine_out)
    cosine_out = jnp.where((quadrant == 1) | (quadrant == 2), -cosine_out, cosine_out)
    return sine_out, cosine_out


def total(value):
    return jnp.sum(jnp.sum(value, axis=0, keepdims=True), axis=1, keepdims=True)


def weights(amplitude):
    pup = amplitude.shape[0]
    rows = lax.broadcasted_iota(jnp.int32, amplitude.shape, 0).astype(jnp.float32) - (pup - 1) / 2.0
    cols = lax.broadcasted_iota(jnp.int32, amplitude.shape, 1).astype(jnp.float32) - (pup - 1) / 2.0
    return jnp.where(rows * rows + cols * cols <= (pup / 2.0) ** 2, amplitude, 0.0)


def point_spread(phase, amplitude, const, wait_for=lambda name: None):
    weight = weights(amplitude)
    sine, cosine = sine_cosine(phase)
    pupil = jnp.concatenate([weight * cosine, weight * sine], 1)
    wait_for("pupil_right")
    across = right_by(pupil, const["pupil_right"])
    cols = across.shape[1] // 2
    wait_for("pupil_left")
    field = left_by(const["pupil_left"], jnp.concatenate([across[:, :cols], across[:, cols:]], 0))
    rows = field.shape[0] // 2
    intensity = field[:rows] * field[:rows] + field[rows:] * field[rows:]
    norm = 1.0 / total(intensity)
    left = left_by(const["kernel_rows"], intensity)
    freqs = left.shape[0] // 2
    wait_for("kernel_right")
    spectrum = right_by(jnp.concatenate([left[:freqs], left[freqs:]], 1), const["kernel_right"])
    return pupil, field, spectrum * norm, norm


def mixed_halves(strip, level=None):
    half = strip.shape[1] // 2
    first, second = strip[:, :half], strip[:, half:]
    both = first + second if level is None else first + second - 2.0 * level
    return jnp.concatenate([both, first - second], 1)


def columns(mixed, const):
    sums, differences = [], []
    for strip in mixed:
        half, freqs = strip.shape[1] // 2, strip.shape[0] // 2
        sums.append(jnp.concatenate([strip[:freqs, :half], strip[freqs:, :half]], 1))
        differences.append(jnp.concatenate([strip[:freqs, half:], strip[freqs:, half:]], 1))
    even = [right_by(jnp.concatenate(sums[p : p + 2], 0), const["forward_even"]) for p in range(0, len(sums), 2)]
    odd = [right_by(jnp.concatenate(differences[p : p + 2], 0), const["forward_odd"]) for p in range(0, len(sums), 2)]
    return even, odd


def forward(strips, row_matrix, const):
    return columns([left_by(row_matrix, mixed_halves(strip)) for strip in strips], const)


def inverse(even, odd, freqs, const):
    even = [right_by(spectrum, const["inverse_even"]) for spectrum in even]
    odd = [right_by(spectrum, const["inverse_odd"]) for spectrum in odd]
    strips = []
    for sums, differences in zip(even, odd):
        half = sums.shape[1] // 2
        for top in range(0, sums.shape[0], freqs):
            rows = slice(top, top + freqs)
            stacked = jnp.concatenate(
                [
                    jnp.concatenate([sums[rows, :half], differences[rows, :half]], 1),
                    jnp.concatenate([sums[rows, half:], differences[rows, half:]], 1),
                ],
                0,
            )
            mixed = left_stacked(const["row_inverse"], stacked)
            first, second = mixed[:, :half], mixed[:, half:]
            strips.append(jnp.concatenate([first + second, first - second], 1))
    return strips


def times(spectra, other, conjugate):
    half = other.shape[1] // 2
    products = []
    for spectrum in spectra:
        planes = spectrum.shape[0] // other.shape[0]
        real = jnp.concatenate([other[:, :half]] * planes, 0)
        imag = jnp.concatenate([other[:, half:]] * planes, 0)
        left, right = spectrum[:, :half], spectrum[:, half:]
        if conjugate:
            product = [left * real + right * imag, right * real - left * imag]
        else:
            product = [left * real - right * imag, left * imag + right * real]
        products.append(jnp.concatenate(product, 1))
    return products


def cross(firsts, seconds, freqs):
    summed = None
    for first, second in zip(firsts, seconds):
        half = first.shape[1] // 2
        left, right = first[:, :half], first[:, half:]
        real, imag = second[:, :half], second[:, half:]
        both = jnp.concatenate([left * real + right * imag, right * real - left * imag], 1)
        for top in range(0, both.shape[0], freqs):
            summed = both[top : top + freqs] if summed is None else summed + both[top : top + freqs]
    return summed


def is_even():
    return lax.axis_index("tile") % 2 == 0


def edge_rows(top, bottom):
    even = is_even()
    return [pl.multiple_of(jnp.where(even, *choice), 8) for choice in ((top, bottom), (bottom, top))]


def near_kernel(own, chip_out, sem):
    chip, _ = edge_rows(0, own.shape[1] - HALF)
    copy = pltpu.make_async_copy(own.at[:, pl.ds(chip, HALF), :], chip_out, sem)
    copy.start()
    copy.wait()


def first_kernel(
    phase, amplitude, own, observed, *refs, at, places, arrays,
):
    psf_refs, outs = refs[:arrays], refs[arrays + 1 : arrays + 9]
    pupil_out, field_out, spec_out, chip_out, core_out, early_out, late_out, means_out = outs
    psf_outs, (phase_in, amplitude_in, own_in, sems) = refs[arrays + 9 : -4], refs[-4:]
    planes, rows, cols = own.shape
    early = early_out.shape[0]
    objects_chip, objects_core = edge_rows(HALF, rows - 2 * HALF)
    observed_chip, observed_core = edge_rows(0, rows - HALF)
    pairs = [
        (phase, phase_in),
        (amplitude, amplitude_in),
        *zip(psf_refs, psf_outs),
        (own.at[:early, pl.ds(observed_core, HALF), :], early_out),
        (own.at[early:, pl.ds(observed_core, HALF), :], late_out),
        (own.at[:, pl.ds(objects_chip, HALF), :], chip_out.at[:planes]),
        (observed.at[:, pl.ds(observed_chip, HALF), :], chip_out.at[planes:]),
        (own.at[:, pl.ds(objects_core, HALF), :], core_out.at[:planes]),
        (observed.at[:, pl.ds(observed_core, HALF), :], core_out.at[planes:]),
        (own, own_in),
    ]
    copies = [pltpu.make_async_copy(source, target, sems.at[i]) for i, (source, target) in enumerate(pairs)]
    for i in (0, 1, *(2 + places[name][0] for name in NEEDED_IN_ORDER), *range(2 + arrays, len(copies))):
        copies[i].start()
    for copy in copies[:2]:
        copy.wait()

    def wait_for(name):
        copies[2 + places[name][0]].wait()

    pupil, field, spectrum, norm = point_spread(phase_in[...], amplitude_in[...], at(*psf_outs), wait_for)
    root = jnp.sqrt(norm)
    pupil_out[...] = pupil * root
    field_out[...] = field * root
    spec_out[...] = spectrum
    for copy in copies[2 + arrays :]:
        copy.wait()
    for p in range(planes):
        means_out[p] = jnp.broadcast_to(total(own_in[p]) * (1.0 / (rows * cols)), means_out.shape[1:])


def halo_rows(chip, core):
    even = is_even()
    return jnp.where(even, chip, core), jnp.where(even, core, chip)


def known_kernel(own, means, *refs, at):
    const, known_out = at(*refs[:-1]), refs[-1]
    for p in range(own.shape[0]):
        known_out[p] = left_by(const["row_own"], mixed_halves(own[p], means[p][:1, :1]))


def gradient_kernel(
    from_chip, early_core, late_core, known, observed, spec, pupil, field, means, *refs, at,
):
    planes = known.shape[0]
    cols = known.shape[2]
    const = at(*refs[:-2])
    keep_out, give_out = refs[-2:]
    freqs = spec.shape[0]
    early = early_core.shape[0]
    levels = [means[p][:1, :1] for p in range(planes)]
    mixed = []
    for p in range(planes):
        edges = halo_rows(from_chip[p], early_core[p] if p < early else late_core[p - early])
        edges = mixed_halves(jnp.concatenate(edges, 0), levels[p])
        mixed.append(known[p] + left_by(const["row_edges"], edges))
    even, odd = columns(mixed, const)
    blurred = inverse(times(even, spec[:, :cols], False), times(odd, spec[:, cols:], False), freqs, const)
    misfit = [1.0 - observed[p] / (blurred[p] + (levels[p] + BACKGROUND)) for p in range(planes)]
    weighted = misfit[0] * blurred[0]
    for p in range(1, planes):
        weighted = weighted + misfit[p] * blurred[p]
    mean = total(weighted)
    misfit_even, misfit_odd = forward(misfit, const["row_own"], const)
    shared = jnp.concatenate([cross(misfit_even, even, freqs), cross(misfit_odd, odd, freqs)], 1)
    across = right_by(shared, const["lag_right"])
    pad_cols = across.shape[1] // 2
    psf_grad = left_by(const["lag_left"], jnp.concatenate([across[:, :pad_cols], across[:, pad_cols:]], 0))
    far = field[...]
    pad_rows = far.shape[0] // 2
    real, imag = far[:pad_rows], far[pad_rows:]
    centred = 2.0 * (psf_grad - mean)
    back = left_by(const["adjoint_left"], jnp.concatenate([centred * real, centred * imag], 0))
    pup = back.shape[0] // 2
    back = right_by(jnp.concatenate([back[:pup], back[pup:]], 1), const["adjoint_right"])
    near = pupil[...]
    slope = back[:, pup:] * near[:, :pup] - back[:, :pup] * near[:, pup:]
    even_core = is_even()
    keep_out[...] = jnp.where(even_core, slope[: pup // 2], slope[pup // 2 :])
    give_out[...] = jnp.where(even_core, slope[pup // 2 :], slope[: pup // 2])


def square_sums(value):
    rows = value.shape[0]
    squared = value * value
    summed = squared[:8]
    for top in range(8, rows, 8):
        summed = summed + squared[top : top + 8]
    return summed


def squares_kernel(mine, received, *others):
    joined_out = others[-1]
    half = mine[...] + received[...]
    squares = square_sums(half)
    for first, second in zip(others[:-1:2], others[1:-1:2]):
        squares = squares + square_sums(first[...] + second[...])
    joined_out[: half.shape[0]] = half
    joined_out[half.shape[0] :] = squares


def blocks_kernel(from_chip, early_core, late_core, own, far_chip, far_core, _, *refs, at):
    planes = own.shape[0]
    const = at(*refs[:-2])
    even_out, odd_out = refs[-2:]
    early = early_core.shape[0]
    strips = []
    for p in range(planes):
        above, below = halo_rows(from_chip[p], early_core[p] if p < early else late_core[p - early])
        far_above, far_below = halo_rows(far_chip[p], far_core[p])
        strips.append(jnp.concatenate([far_above, above, own[p]], 0))
        strips.append(jnp.concatenate([own[p], below, far_below], 0))
    even, odd = forward(strips, const["row_forward"], const)
    even_out[...] = jnp.concatenate(even, 0)
    odd_out[...] = jnp.concatenate(odd, 0)


def second_kernel(phase, amplitude, mine, theirs, *refs, at, psf_at, arrays, cells, squares_apart):
    if squares_apart:
        squares, *refs = refs
    even, odd, own, observed, far_chip, far_core, *refs = refs
    planes, rows, cols = own.shape
    const = at(*refs[:arrays])
    psf_const = psf_at(*refs[arrays:-5])
    objects_out, phase_out, objects, new_phase, sems = refs[-5:]
    writes = [pltpu.make_async_copy(new_phase, phase_out, sems.at[planes])]
    half = phase.shape[0] // 2
    first, second = halo_rows(mine[:half], theirs[:half])
    slope = jnp.concatenate([first, second], 0)
    summed = squares[...] if squares_apart else mine[half:] + theirs[half:]
    mean_square = total(summed) * (1.0 / cells)
    updated = phase[...] - STEP_SIZE * slope / jnp.sqrt(mean_square + EPSILON)
    new_phase[...] = updated
    writes[0].start()
    _, _, spec, _ = point_spread(updated, amplitude[...], psf_const)
    spec_even, spec_odd = spec[:, :cols], spec[:, cols:]
    freqs = spec.shape[0]
    pairs = range(0, even.shape[0], 2 * freqs)
    light = inverse(
        times([even[top : top + 2 * freqs] for top in pairs], spec_even, False),
        times([odd[top : top + 2 * freqs] for top in pairs], spec_odd, False),
        freqs, const,
    )
    ratios = []
    for p in range(planes):
        above, below = halo_rows(far_chip[planes + p], far_core[planes + p])
        blurred = jnp.concatenate(light[2 * p : 2 * p + 2], 0) + BACKGROUND
        ratios.append(jnp.concatenate([above, observed[p], below], 0) / blurred)
    ratio_even, ratio_odd = forward(ratios, const["row_forward"], const)
    correction = inverse(times(ratio_even, spec_even, True), times(ratio_odd, spec_odd, True), freqs, const)
    for p in range(planes):
        objects[p] = own[p] * correction[p]
        writes.append(pltpu.make_async_copy(objects.at[p], objects_out.at[p], sems.at[p]))
        writes[-1].start()
    for write in writes:
        write.wait()


def call(kernel, out_shapes, args, flops=10**6, spaces=None, scratch=(), out_space=pltpu.VMEM):
    outs = [
        jax.ShapeDtypeStruct(shape, jnp.float32) if isinstance(shape, tuple) else shape for shape in out_shapes
    ]
    spaces = spaces or {}
    return pl.pallas_call(
        kernel,
        out_shape=outs,
        in_specs=[pl.BlockSpec(memory_space=spaces.get(i, pltpu.VMEM)) for i in range(len(args))],
        out_specs=[pl.BlockSpec(memory_space=out_space)] * len(outs),
        scratch_shapes=scratch,
        compiler_params=pltpu.CompilerParams(vmem_limit_bytes=VMEM_LIMIT),
        cost_estimate=pl.CostEstimate(flops=flops, bytes_accessed=10**5, transcendentals=0),
    )(*args)


def to_next_chip(value):
    count = lax.axis_size("tile")
    return lax.ppermute(value, "tile", [(i, (i + 1 if i % 2 else i - 1) % count) for i in range(count)])


def exchange(value, step):
    return lax.ppermute(value, "tile", [(i, i ^ step) for i in range(lax.axis_size("tile"))])


def across_depth_and_chip(value):
    pairs = [(2 * t + d, 2 * (t ^ 2) + 1 - d) for t in range(lax.axis_size("tile")) for d in range(2)]
    return lax.ppermute(value, ("tile", "depth"), pairs)


def sum_over_depth(value):
    count = lax.axis_size("depth")
    if count & (count - 1):
        return lax.psum(value, "depth")
    for bit in range(count.bit_length() - 1):
        value = value + lax.ppermute(value, "depth", [(i, i ^ (1 << bit)) for i in range(count)])
    return value


def on_device(objects, observed, pupil_phase, pupil_amplitude):
    picture, measured, phase, amplitude = objects[0], observed[0], pupil_phase[0], pupil_amplitude[0]
    planes, rows, cols = picture.shape
    pup = phase.shape[0]
    count = lax.axis_size("tile")
    ker = 2 * HALF + 1
    length = rows + 2 * HALF
    pad_rows, pad_cols = round_up(ker, 16), round_up(ker, 128)
    row_forward, row_inverse = row_constants(rows, length)
    col_forward, col_inverse = col_constants(cols)
    kernel_rows, kernel_right = kernel_constants(length, cols, ker, pad_rows, pad_cols)
    pupil_left, pupil_right = pupil_constants(pup, ker, pad_rows, pad_cols)
    psf_const = Joined(
        {"pupil_left": pupil_left, "kernel_rows": kernel_rows},
        {"pupil_right": pupil_right, "kernel_right": kernel_right},
    )
    block_left = {"row_forward": row_forward, "row_inverse": row_inverse}
    block_right = {
        "forward_even": col_forward[0],
        "forward_odd": col_forward[1],
        "inverse_even": col_inverse[0],
        "inverse_odd": col_inverse[1],
    }
    block_const = Joined(block_left, block_right)
    lag_const = Joined(
        {
            "row_edges": np.concatenate([row_forward[:, :HALF], row_forward[:, HALF + rows :]], 1),
            "lag_left": kernel_rows.T * (2.0 / length),
            "adjoint_left": pupil_left.T,
        },
        {"lag_right": kernel_right.T / cols, "adjoint_right": pupil_right.T},
    )
    own_const = Joined({"row_own": row_forward[:, HALF : HALF + rows]}, {})
    psf_arrays, block_arrays, lag_arrays, own_arrays = (
        [jnp.asarray(array) for array in const.arrays] for const in (psf_const, block_const, lag_const, own_const)
    )

    def gradient_at(*refs):
        held = len(block_arrays)
        end = held + len(lag_arrays)
        return {**block_const.at(*refs[:held]), **lag_const.at(*refs[held:end]), **own_const.at(*refs[end:])}

    in_hbm = [
        pltpu.with_memory_space_constraint(value, pltpu.HBM)
        for value in (phase, amplitude, picture, measured, *psf_arrays)
    ]
    (chip_rows,) = call(
        near_kernel, [(planes, HALF, cols)], in_hbm[2:3], scratch=[pltpu.SemaphoreType.DMA(())], spaces={0: pltpu.HBM}
    )
    from_chip = to_next_chip(chip_rows)
    pupil, field, spec, far_chip, far_core, early_rows, late_rows, means, *psf_arrays = call(
        functools.partial(first_kernel, at=psf_const.at, places=psf_const.places, arrays=len(psf_arrays)),
        [(pup, 2 * pup), (2 * pad_rows, pad_cols), (length // 2, 2 * cols)]
        + [(2 * planes, HALF, cols)] * 2
        + [(planes // 2, HALF, cols), (planes - planes // 2, HALF, cols), (planes, 8, 128)]
        + psf_arrays,
        (*in_hbm, chip_rows),
        flops=3 * 10**9,
        spaces={**dict.fromkeys(range(len(in_hbm)), pltpu.HBM), len(in_hbm): pl.ANY},
        scratch=[pltpu.VMEM(value.shape, jnp.float32) for value in (phase, amplitude, picture)]
        + [pltpu.SemaphoreType.DMA((9 + len(psf_arrays),))],
    )
    early_core, late_core, far_core = (exchange(value, 1) for value in (early_rows, late_rows, far_core))
    (known,) = call(
        functools.partial(known_kernel, at=own_const.at),
        [(planes, length, cols)],
        (picture, means, *own_arrays),
        flops=10**3,
    )
    far_chip, late_core, known = lax.optimization_barrier((far_chip, late_core, known))
    far_chip = to_next_chip(far_chip)
    keep, give = call(
        functools.partial(gradient_kernel, at=gradient_at),
        [(pup // 2, pup)] * 2,
        (
            from_chip, early_core, late_core, known, measured, spec, pupil, field, means, *block_arrays, *lag_arrays,
            *own_arrays,
        ),
        flops=4 * 10**10,
    )
    half = keep + exchange(give, 1)
    bits = list(range(2, count.bit_length() - 1))
    for low, high in zip(bits[::2], bits[1::2]):
        half = half + ((exchange(half, 1 << low) + exchange(half, (1 << low) | (1 << high))) + exchange(half, 1 << high))
    if len(bits) % 2:
        half = half + exchange(half, 1 << bits[-1])
    last_round = [exchange(half, 2)]
    two_strata = lax.axis_size("depth") == 2
    if two_strata:
        last_round += [lax.ppermute(half, "depth", [(0, 1), (1, 0)]), across_depth_and_chip(half)]
    even, odd = call(
        functools.partial(blocks_kernel, at=block_const.at),
        [(planes * length, cols)] * 2,
        (from_chip, early_core, late_core, picture, far_chip, far_core, half, *block_arrays),
        spaces={6: pl.ANY},
    )
    even, *last_round = lax.optimization_barrier((even, *last_round))
    (joined,) = call(squares_kernel, [(pup // 2 + 8, pup)], (half, *last_round))
    other = exchange(joined, 1)
    squares = []
    if not two_strata:
        squares = [sum_over_depth(joined[pup // 2 :] + other[pup // 2 :])]
    new_objects, new_phase = call(
        functools.partial(
            second_kernel,
            at=block_const.at,
            psf_at=psf_const.at,
            arrays=len(block_arrays),
            cells=lax.axis_size("depth") * pup * pup,
            squares_apart=bool(squares),
        ),
        [picture.shape, phase.shape],
        (
            phase, amplitude, joined, other, *squares, even, odd, picture, measured,
            far_chip, far_core, *block_arrays, *psf_arrays,
        ),
        scratch=[pltpu.VMEM(value.shape, jnp.float32) for value in (picture, phase)]
        + [pltpu.SemaphoreType.DMA((planes + 1,))],
        out_space=pltpu.HBM,
    )
    return new_objects[None], new_phase[None]


def solution(mesh):
    return jax.shard_map(
        on_device,
        mesh=mesh,
        in_specs=(
            P("depth", None, "tile", None),
            P("depth", None, "tile", None),
            P("depth", None, None),
            P("depth", None, None),
        ),
        out_specs=(P("depth", None, "tile", None), P("depth", None, None)),
        check_vma=False,
    )
```

```python
import functools
import math

import jax
import jax.numpy as jnp
import ml_dtypes
import numpy as np
from jax import lax
from jax.experimental import pallas as pl
from jax.experimental.pallas import tpu as pltpu
from jax.sharding import PartitionSpec as P

HALF = 64
BACKGROUND = 0.1
STEP_SIZE = 0.3
EPSILON = 1e-06
STACKED = ("row_inverse",)
NEEDED_IN_ORDER = ("pupil_right", "pupil_left", "kernel_right")
VMEM_LIMIT = 32 * 1024 * 1024


def round_up(value, step):
    return -(-value // step) * step


def angles(left, right, length):
    return (2.0 * math.pi / length) * np.outer(left, right)


def halves(matrix):
    high = matrix.astype(np.float32).astype(ml_dtypes.bfloat16)
    low = (matrix - high.astype(np.float64)).astype(np.float32).astype(ml_dtypes.bfloat16)
    return high, low


def row_constants(rows, length):
    freqs = np.arange(length // 2) + 0.5
    theta = angles(freqs, np.arange(length), length)
    forward = np.concatenate([np.cos(theta), -np.sin(theta)], 0)
    inner = theta[:, HALF : HALF + rows]
    inverse = np.concatenate([np.cos(inner).T, -np.sin(inner).T], 1) * (2.0 / length)
    return forward, inverse


def col_constants(cols):
    half = cols // 2
    forward, inverse = [], []
    for parity in range(2):
        theta = angles(np.arange(half), 2 * np.arange(half) + parity, cols)
        c, s = np.cos(theta), np.sin(theta)
        forward.append(np.block([[c, -s], [s, c]]))
        inverse.append(np.block([[c.T, s.T], [-s.T, c.T]]) / cols)
    return forward, inverse


def kernel_constants(length, cols, ker, pad_rows, pad_cols):
    lags = np.arange(ker) - HALF
    theta = angles(np.arange(length // 2) + 0.5, lags, length)
    rows = np.zeros((length, pad_rows))
    rows[: length // 2, :ker] = np.cos(theta)
    rows[length // 2 :, :ker] = -np.sin(theta)
    half = cols // 2
    right = np.zeros((2 * pad_cols, 2 * cols))
    for parity in range(2):
        theta = angles(lags, 2 * np.arange(half) + parity, cols)
        c, s = np.cos(theta), np.sin(theta)
        at = parity * cols
        right[:ker, at : at + half] = c
        right[:ker, at + half : at + cols] = -s
        right[pad_cols : pad_cols + ker, at : at + half] = s
        right[pad_cols : pad_cols + ker, at + half : at + cols] = c
    return rows, right


def pupil_constants(pup, ker, pad_rows, pad_cols):
    theta = angles(np.arange(ker) - HALF, np.arange(pup), ker)
    real, imag = np.cos(theta), -np.sin(theta)
    right = np.zeros((2 * pup, 2 * pad_cols))
    right[:pup, :ker] = real.T
    right[:pup, pad_cols : pad_cols + ker] = imag.T
    right[pup:, :ker] = -imag.T
    right[pup:, pad_cols : pad_cols + ker] = real.T
    left = np.zeros((2 * pad_rows, 2 * pup))
    left[:ker, :pup] = real
    left[:ker, pup:] = -imag
    left[pad_rows : pad_rows + ker, :pup] = imag
    left[pad_rows : pad_rows + ker, pup:] = real
    return left, right


class Joined:
    def __init__(self, left, right):
        self.places, groups = {}, {}
        for name, matrix in right.items():
            high, low = halves(matrix)
            groups.setdefault(matrix.shape[0], []).append((name, np.concatenate([high, high, low], 0)))
        for name, matrix in left.items():
            high, low = halves(matrix)
            held = np.concatenate([high, low], 0) if name in STACKED else np.concatenate([high, low, high], 1)
            groups.setdefault("left", []).append((name, held))
        self.arrays = []
        for kind, members in groups.items():
            at = 0
            for name, block in members:
                rows, cols = block.shape
                start = (at, 0) if kind == "left" else (0, at)
                self.places[name] = (len(self.arrays), *start, rows, cols)
                at += rows if kind == "left" else cols
            blocks = [block for _, block in members]
            if kind == "left":
                width = max(block.shape[1] for block in blocks)
                blocks = [np.pad(block, ((0, 0), (0, width - block.shape[1]))) for block in blocks]
            self.arrays.append(np.concatenate(blocks, 0 if kind == "left" else 1))

    def at(self, *refs):
        return {
            name: refs[which].at[top : top + rows, first : first + cols]
            for name, (which, top, first, rows, cols) in self.places.items()
        }


def dot(left, right):
    return jnp.dot(left, right, preferred_element_type=jnp.float32)


def split(value):
    high = value.astype(jnp.bfloat16)
    low = (value - high.astype(jnp.float32)).astype(jnp.bfloat16)
    return high, low


def left_by(const, value):
    high, low = split(value)
    return dot(const[...], jnp.concatenate([high, high, low], 0))


def left_stacked(const, value):
    high, low = split(value)
    rows = const.shape[0] // 2
    both = dot(const[...], high)
    return both[:rows] + (both[rows:] + dot(const[:rows], low))


def right_by(value, const):
    high, low = split(value)
    return dot(jnp.concatenate([high, low, high], 1), const[...])


def sine_cosine(angle):
    turns = jnp.floor(angle * (2.0 / math.pi) + 0.5)
    rest = angle - turns * 1.5703125
    rest = rest - turns * 4.837512969970703e-4
    rest = rest - turns * 7.54978995489e-8
    square = rest * rest
    sine = rest + rest * square * (
        -1.6666654611e-1 + square * (8.3321608736e-3 + square * -1.9515295891e-4)
    )
    cosine = 1.0 - 0.5 * square + square * square * (
        4.166664568298827e-2 + square * (-1.388731625493765e-3 + square * 2.443315711809948e-5)
    )
    quadrant = turns.astype(jnp.int32) & 3
    swap = (quadrant & 1) == 1
    sine_out = jnp.where(swap, cosine, sine)
    cosine_out = jnp.where(swap, sine, cosine)
    sine_out = jnp.where(quadrant >= 2, -sine_out, sine_out)
    cosine_out = jnp.where((quadrant == 1) | (quadrant == 2), -cosine_out, cosine_out)
    return sine_out, cosine_out


def total(value):
    return jnp.sum(jnp.sum(value, axis=0, keepdims=True), axis=1, keepdims=True)


def weights(amplitude):
    pup = amplitude.shape[0]
    rows = lax.broadcasted_iota(jnp.int32, amplitude.shape, 0).astype(jnp.float32) - (pup - 1) / 2.0
    cols = lax.broadcasted_iota(jnp.int32, amplitude.shape, 1).astype(jnp.float32) - (pup - 1) / 2.0
    return jnp.where(rows * rows + cols * cols <= (pup / 2.0) ** 2, amplitude, 0.0)


def point_spread(phase, amplitude, const, wait_for=lambda name: None):
    weight = weights(amplitude)
    sine, cosine = sine_cosine(phase)
    pupil = jnp.concatenate([weight * cosine, weight * sine], 1)
    wait_for("pupil_right")
    across = right_by(pupil, const["pupil_right"])
    cols = across.shape[1] // 2
    wait_for("pupil_left")
    field = left_by(const["pupil_left"], jnp.concatenate([across[:, :cols], across[:, cols:]], 0))
    rows = field.shape[0] // 2
    intensity = field[:rows] * field[:rows] + field[rows:] * field[rows:]
    norm = 1.0 / total(intensity)
    left = left_by(const["kernel_rows"], intensity)
    freqs = left.shape[0] // 2
    wait_for("kernel_right")
    spectrum = right_by(jnp.concatenate([left[:freqs], left[freqs:]], 1), const["kernel_right"])
    return pupil, field, spectrum * norm, norm


def mixed_halves(strip, level=None):
    half = strip.shape[1] // 2
    first, second = strip[:, :half], strip[:, half:]
    both = first + second if level is None else first + second - 2.0 * level
    return jnp.concatenate([both, first - second], 1)


def columns(mixed, const):
    sums, differences = [], []
    for strip in mixed:
        half, freqs = strip.shape[1] // 2, strip.shape[0] // 2
        sums.append(jnp.concatenate([strip[:freqs, :half], strip[freqs:, :half]], 1))
        differences.append(jnp.concatenate([strip[:freqs, half:], strip[freqs:, half:]], 1))
    even = [right_by(jnp.concatenate(sums[p : p + 2], 0), const["forward_even"]) for p in range(0, len(sums), 2)]
    odd = [right_by(jnp.concatenate(differences[p : p + 2], 0), const["forward_odd"]) for p in range(0, len(sums), 2)]
    return even, odd


def forward(strips, row_matrix, const):
    return columns([left_by(row_matrix, mixed_halves(strip)) for strip in strips], const)


def inverse(even, odd, freqs, const):
    even = [right_by(spectrum, const["inverse_even"]) for spectrum in even]
    odd = [right_by(spectrum, const["inverse_odd"]) for spectrum in odd]
    strips = []
    for sums, differences in zip(even, odd):
        half = sums.shape[1] // 2
        for top in range(0, sums.shape[0], freqs):
            rows = slice(top, top + freqs)
            stacked = jnp.concatenate(
                [
                    jnp.concatenate([sums[rows, :half], differences[rows, :half]], 1),
                    jnp.concatenate([sums[rows, half:], differences[rows, half:]], 1),
                ],
                0,
            )
            mixed = left_stacked(const["row_inverse"], stacked)
            first, second = mixed[:, :half], mixed[:, half:]
            strips.append(jnp.concatenate([first + second, first - second], 1))
    return strips


def times(spectra, other, conjugate):
    half = other.shape[1] // 2
    products = []
    for spectrum in spectra:
        planes = spectrum.shape[0] // other.shape[0]
        real = jnp.concatenate([other[:, :half]] * planes, 0)
        imag = jnp.concatenate([other[:, half:]] * planes, 0)
        left, right = spectrum[:, :half], spectrum[:, half:]
        if conjugate:
            product = [left * real + right * imag, right * real - left * imag]
        else:
            product = [left * real - right * imag, left * imag + right * real]
        products.append(jnp.concatenate(product, 1))
    return products


def cross(firsts, seconds, freqs):
    summed = None
    for first, second in zip(firsts, seconds):
        half = first.shape[1] // 2
        left, right = first[:, :half], first[:, half:]
        real, imag = second[:, :half], second[:, half:]
        both = jnp.concatenate([left * real + right * imag, right * real - left * imag], 1)
        for top in range(0, both.shape[0], freqs):
            summed = both[top : top + freqs] if summed is None else summed + both[top : top + freqs]
    return summed


def is_even():
    return lax.axis_index("tile") % 2 == 0


def edge_rows(top, bottom):
    even = is_even()
    return [pl.multiple_of(jnp.where(even, *choice), 8) for choice in ((top, bottom), (bottom, top))]


def near_kernel(own, chip_out, sem):
    chip, _ = edge_rows(0, own.shape[1] - HALF)
    copy = pltpu.make_async_copy(own.at[:, pl.ds(chip, HALF), :], chip_out, sem)
    copy.start()
    copy.wait()


def first_kernel(
    phase, amplitude, own, observed, *refs, at, places, arrays,
):
    psf_refs, outs = refs[:arrays], refs[arrays + 1 : arrays + 9]
    pupil_out, field_out, spec_out, chip_out, core_out, early_out, late_out, means_out = outs
    psf_outs, (phase_in, amplitude_in, own_in, sems) = refs[arrays + 9 : -4], refs[-4:]
    planes, rows, cols = own.shape
    early = early_out.shape[0]
    objects_chip, objects_core = edge_rows(HALF, rows - 2 * HALF)
    observed_chip, observed_core = edge_rows(0, rows - HALF)
    pairs = [
        (phase, phase_in),
        (amplitude, amplitude_in),
        *zip(psf_refs, psf_outs),
        (own.at[:early, pl.ds(observed_core, HALF), :], early_out),
        (own.at[early:, pl.ds(observed_core, HALF), :], late_out),
        (own.at[:, pl.ds(objects_chip, HALF), :], chip_out.at[:planes]),
        (observed.at[:, pl.ds(observed_chip, HALF), :], chip_out.at[planes:]),
        (own.at[:, pl.ds(objects_core, HALF), :], core_out.at[:planes]),
        (observed.at[:, pl.ds(observed_core, HALF), :], core_out.at[planes:]),
        (own, own_in),
    ]
    copies = [pltpu.make_async_copy(source, target, sems.at[i]) for i, (source, target) in enumerate(pairs)]
    for i in (0, 1, *(2 + places[name][0] for name in NEEDED_IN_ORDER), *range(2 + arrays, len(copies))):
        copies[i].start()
    for copy in copies[:2]:
        copy.wait()

    def wait_for(name):
        copies[2 + places[name][0]].wait()

    pupil, field, spectrum, norm = point_spread(phase_in[...], amplitude_in[...], at(*psf_outs), wait_for)
    root = jnp.sqrt(norm)
    pupil_out[...] = pupil * root
    field_out[...] = field * root
    spec_out[...] = spectrum
    for copy in copies[2 + arrays :]:
        copy.wait()
    for p in range(planes):
        means_out[p] = jnp.broadcast_to(total(own_in[p]) * (1.0 / (rows * cols)), means_out.shape[1:])


def halo_rows(chip, core):
    even = is_even()
    return jnp.where(even, chip, core), jnp.where(even, core, chip)


def known_kernel(own, means, *refs, at):
    const, known_out = at(*refs[:-1]), refs[-1]
    for p in range(own.shape[0]):
        known_out[p] = left_by(const["row_own"], mixed_halves(own[p], means[p][:1, :1]))


def gradient_kernel(
    from_chip, early_core, late_core, known, observed, spec, pupil, field, means, *refs, at,
):
    planes = known.shape[0]
    cols = known.shape[2]
    const = at(*refs[:-2])
    keep_out, give_out = refs[-2:]
    freqs = spec.shape[0]
    early = early_core.shape[0]
    levels = [means[p][:1, :1] for p in range(planes)]
    mixed = []
    for p in range(planes):
        edges = halo_rows(from_chip[p], early_core[p] if p < early else late_core[p - early])
        edges = mixed_halves(jnp.concatenate(edges, 0), levels[p])
        mixed.append(known[p] + left_by(const["row_edges"], edges))
    even, odd = columns(mixed, const)
    blurred = inverse(times(even, spec[:, :cols], False), times(odd, spec[:, cols:], False), freqs, const)
    misfit = [1.0 - observed[p] / (blurred[p] + (levels[p] + BACKGROUND)) for p in range(planes)]
    weighted = misfit[0] * blurred[0]
    for p in range(1, planes):
        weighted = weighted + misfit[p] * blurred[p]
    mean = total(weighted)
    misfit_even, misfit_odd = forward(misfit, const["row_own"], const)
    shared = jnp.concatenate([cross(misfit_even, even, freqs), cross(misfit_odd, odd, freqs)], 1)
    across = right_by(shared, const["lag_right"])
    pad_cols = across.shape[1] // 2
    psf_grad = left_by(const["lag_left"], jnp.concatenate([across[:, :pad_cols], across[:, pad_cols:]], 0))
    far = field[...]
    pad_rows = far.shape[0] // 2
    real, imag = far[:pad_rows], far[pad_rows:]
    centred = 2.0 * (psf_grad - mean)
    back = left_by(const["adjoint_left"], jnp.concatenate([centred * real, centred * imag], 0))
    pup = back.shape[0] // 2
    back = right_by(jnp.concatenate([back[:pup], back[pup:]], 1), const["adjoint_right"])
    near = pupil[...]
    slope = back[:, pup:] * near[:, :pup] - back[:, :pup] * near[:, pup:]
    even_core = is_even()
    keep_out[...] = jnp.where(even_core, slope[: pup // 2], slope[pup // 2 :])
    give_out[...] = jnp.where(even_core, slope[pup // 2 :], slope[: pup // 2])


def square_sums(value):
    rows = value.shape[0]
    squared = value * value
    summed = squared[:8]
    for top in range(8, rows, 8):
        summed = summed + squared[top : top + 8]
    return summed


def squares_kernel(mine, received, *others):
    joined_out = others[-1]
    half = mine[...] + received[...]
    squares = square_sums(half)
    for first, second in zip(others[:-1:2], others[1:-1:2]):
        squares = squares + square_sums(first[...] + second[...])
    joined_out[: half.shape[0]] = half
    joined_out[half.shape[0] :] = squares


def blocks_kernel(from_chip, early_core, late_core, own, far_chip, far_core, _, *refs, at):
    planes = own.shape[0]
    const = at(*refs[:-2])
    even_out, odd_out = refs[-2:]
    early = early_core.shape[0]
    strips = []
    for p in range(planes):
        above, below = halo_rows(from_chip[p], early_core[p] if p < early else late_core[p - early])
        far_above, far_below = halo_rows(far_chip[p], far_core[p])
        strips.append(jnp.concatenate([far_above, above, own[p]], 0))
        strips.append(jnp.concatenate([own[p], below, far_below], 0))
    even, odd = forward(strips, const["row_forward"], const)
    even_out[...] = jnp.concatenate(even, 0)
    odd_out[...] = jnp.concatenate(odd, 0)


def second_kernel(phase, amplitude, mine, theirs, *refs, at, psf_at, arrays, cells, squares_apart):
    if squares_apart:
        squares, *refs = refs
    even, odd, own, observed, far_chip, far_core, *refs = refs
    planes, rows, cols = own.shape
    const = at(*refs[:arrays])
    psf_const = psf_at(*refs[arrays:-5])
    objects_out, phase_out, objects, new_phase, sems = refs[-5:]
    writes = [pltpu.make_async_copy(new_phase, phase_out, sems.at[planes])]
    half = phase.shape[0] // 2
    first, second = halo_rows(mine[:half], theirs[:half])
    slope = jnp.concatenate([first, second], 0)
    summed = squares[...] if squares_apart else mine[half:] + theirs[half:]
    mean_square = total(summed) * (1.0 / cells)
    updated = phase[...] - STEP_SIZE * slope / jnp.sqrt(mean_square + EPSILON)
    new_phase[...] = updated
    writes[0].start()
    _, _, spec, _ = point_spread(updated, amplitude[...], psf_const)
    spec_even, spec_odd = spec[:, :cols], spec[:, cols:]
    freqs = spec.shape[0]
    pairs = range(0, even.shape[0], 2 * freqs)
    light = inverse(
        times([even[top : top + 2 * freqs] for top in pairs], spec_even, False),
        times([odd[top : top + 2 * freqs] for top in pairs], spec_odd, False),
        freqs, const,
    )
    ratios = []
    for p in range(planes):
        above, below = halo_rows(far_chip[planes + p], far_core[planes + p])
        blurred = jnp.concatenate(light[2 * p : 2 * p + 2], 0) + BACKGROUND
        ratios.append(jnp.concatenate([above, observed[p], below], 0) / blurred)
    ratio_even, ratio_odd = forward(ratios, const["row_forward"], const)
    correction = inverse(times(ratio_even, spec_even, True), times(ratio_odd, spec_odd, True), freqs, const)
    for p in range(planes):
        objects[p] = own[p] * correction[p]
        writes.append(pltpu.make_async_copy(objects.at[p], objects_out.at[p], sems.at[p]))
        writes[-1].start()
    for write in writes:
        write.wait()


def call(kernel, out_shapes, args, flops=10**6, spaces=None, scratch=(), out_space=pltpu.VMEM):
    outs = [
        jax.ShapeDtypeStruct(shape, jnp.float32) if isinstance(shape, tuple) else shape for shape in out_shapes
    ]
    spaces = spaces or {}
    return pl.pallas_call(
        kernel,
        out_shape=outs,
        in_specs=[pl.BlockSpec(memory_space=spaces.get(i, pltpu.VMEM)) for i in range(len(args))],
        out_specs=[pl.BlockSpec(memory_space=out_space)] * len(outs),
        scratch_shapes=scratch,
        compiler_params=pltpu.CompilerParams(vmem_limit_bytes=VMEM_LIMIT),
        cost_estimate=pl.CostEstimate(flops=flops, bytes_accessed=10**5, transcendentals=0),
    )(*args)


def to_next_chip(value):
    count = lax.axis_size("tile")
    return lax.ppermute(value, "tile", [(i, (i + 1 if i % 2 else i - 1) % count) for i in range(count)])


def exchange(value, step):
    return lax.ppermute(value, "tile", [(i, i ^ step) for i in range(lax.axis_size("tile"))])


def across_depth_and_chip(value):
    pairs = [(2 * t + d, 2 * (t ^ 2) + 1 - d) for t in range(lax.axis_size("tile")) for d in range(2)]
    return lax.ppermute(value, ("tile", "depth"), pairs)


def sum_over_depth(value):
    count = lax.axis_size("depth")
    if count & (count - 1):
        return lax.psum(value, "depth")
    for bit in range(count.bit_length() - 1):
        value = value + lax.ppermute(value, "depth", [(i, i ^ (1 << bit)) for i in range(count)])
    return value


def on_device(objects, observed, pupil_phase, pupil_amplitude):
    picture, measured, phase, amplitude = objects[0], observed[0], pupil_phase[0], pupil_amplitude[0]
    planes, rows, cols = picture.shape
    pup = phase.shape[0]
    count = lax.axis_size("tile")
    ker = 2 * HALF + 1
    length = rows + 2 * HALF
    pad_rows, pad_cols = round_up(ker, 16), round_up(ker, 128)
    row_forward, row_inverse = row_constants(rows, length)
    col_forward, col_inverse = col_constants(cols)
    kernel_rows, kernel_right = kernel_constants(length, cols, ker, pad_rows, pad_cols)
    pupil_left, pupil_right = pupil_constants(pup, ker, pad_rows, pad_cols)
    psf_const = Joined(
        {"pupil_left": pupil_left, "kernel_rows": kernel_rows},
        {"pupil_right": pupil_right, "kernel_right": kernel_right},
    )
    block_left = {"row_forward": row_forward, "row_inverse": row_inverse}
    block_right = {
        "forward_even": col_forward[0],
        "forward_odd": col_forward[1],
        "inverse_even": col_inverse[0],
        "inverse_odd": col_inverse[1],
    }
    block_const = Joined(block_left, block_right)
    lag_const = Joined(
        {
            "row_edges": np.concatenate([row_forward[:, :HALF], row_forward[:, HALF + rows :]], 1),
            "lag_left": kernel_rows.T * (2.0 / length),
            "adjoint_left": pupil_left.T,
        },
        {"lag_right": kernel_right.T / cols, "adjoint_right": pupil_right.T},
    )
    own_const = Joined({"row_own": row_forward[:, HALF : HALF + rows]}, {})
    psf_arrays, block_arrays, lag_arrays, own_arrays = (
        [jnp.asarray(array) for array in const.arrays] for const in (psf_const, block_const, lag_const, own_const)
    )

    def gradient_at(*refs):
        held = len(block_arrays)
        end = held + len(lag_arrays)
        return {**block_const.at(*refs[:held]), **lag_const.at(*refs[held:end]), **own_const.at(*refs[end:])}

    in_hbm = [
        pltpu.with_memory_space_constraint(value, pltpu.HBM)
        for value in (phase, amplitude, picture, measured, *psf_arrays)
    ]
    (chip_rows,) = call(
        near_kernel, [(planes, HALF, cols)], in_hbm[2:3], scratch=[pltpu.SemaphoreType.DMA(())], spaces={0: pltpu.HBM}
    )
    from_chip = to_next_chip(chip_rows)
    pupil, field, spec, far_chip, far_core, early_rows, late_rows, means, *psf_arrays = call(
        functools.partial(first_kernel, at=psf_const.at, places=psf_const.places, arrays=len(psf_arrays)),
        [(pup, 2 * pup), (2 * pad_rows, pad_cols), (length // 2, 2 * cols)]
        + [(2 * planes, HALF, cols)] * 2
        + [(planes // 2, HALF, cols), (planes - planes // 2, HALF, cols), (planes, 8, 128)]
        + psf_arrays,
        (*in_hbm, chip_rows),
        flops=3 * 10**9,
        spaces={**dict.fromkeys(range(len(in_hbm)), pltpu.HBM), len(in_hbm): pl.ANY},
        scratch=[pltpu.VMEM(value.shape, jnp.float32) for value in (phase, amplitude, picture)]
        + [pltpu.SemaphoreType.DMA((9 + len(psf_arrays),))],
    )
    early_core, late_core, far_core = (exchange(value, 1) for value in (early_rows, late_rows, far_core))
    (known,) = call(
        functools.partial(known_kernel, at=own_const.at),
        [(planes, length, cols)],
        (picture, means, *own_arrays),
        flops=10**3,
    )
    far_chip, known = lax.optimization_barrier((far_chip, known))
    far_chip = to_next_chip(far_chip)
    keep, give = call(
        functools.partial(gradient_kernel, at=gradient_at),
        [(pup // 2, pup)] * 2,
        (
            from_chip, early_core, late_core, known, measured, spec, pupil, field, means, *block_arrays, *lag_arrays,
            *own_arrays,
        ),
        flops=4 * 10**10,
    )
    half = keep + exchange(give, 1)
    bits = list(range(2, count.bit_length() - 1))
    for low, high in zip(bits[::2], bits[1::2]):
        half = half + ((exchange(half, 1 << low) + exchange(half, 1 << high)) + exchange(half, (1 << low) | (1 << high)))
    if len(bits) % 2:
        half = half + exchange(half, 1 << bits[-1])
    last_round = [exchange(half, 2)]
    two_strata = lax.axis_size("depth") == 2
    if two_strata:
        last_round += [lax.ppermute(half, "depth", [(0, 1), (1, 0)]), across_depth_and_chip(half)]
    even, odd = call(
        functools.partial(blocks_kernel, at=block_const.at),
        [(planes * length, cols)] * 2,
        (from_chip, early_core, late_core, picture, far_chip, far_core, half, *block_arrays),
        spaces={6: pl.ANY},
    )
    even, *last_round = lax.optimization_barrier((even, *last_round))
    (joined,) = call(squares_kernel, [(pup // 2 + 8, pup)], (half, *last_round))
    other = exchange(joined, 1)
    squares = []
    if not two_strata:
        squares = [sum_over_depth(joined[pup // 2 :] + other[pup // 2 :])]
    new_objects, new_phase = call(
        functools.partial(
            second_kernel,
            at=block_const.at,
            psf_at=psf_const.at,
            arrays=len(block_arrays),
            cells=lax.axis_size("depth") * pup * pup,
            squares_apart=bool(squares),
        ),
        [picture.shape, phase.shape],
        (
            phase, amplitude, joined, other, *squares, even, odd, picture, measured,
            far_chip, far_core, *block_arrays, *psf_arrays,
        ),
        scratch=[pltpu.VMEM(value.shape, jnp.float32) for value in (picture, phase)]
        + [pltpu.SemaphoreType.DMA((planes + 1,))],
        out_space=pltpu.HBM,
    )
    return new_objects[None], new_phase[None]


def solution(mesh):
    return jax.shard_map(
        on_device,
        mesh=mesh,
        in_specs=(
            P("depth", None, "tile", None),
            P("depth", None, "tile", None),
            P("depth", None, None),
            P("depth", None, None),
        ),
        out_specs=(P("depth", None, "tile", None), P("depth", None, None)),
        check_vma=False,
    )
```

```python
import functools
import math

import jax
import jax.numpy as jnp
import ml_dtypes
import numpy as np
from jax import lax
from jax.experimental import pallas as pl
from jax.experimental.pallas import tpu as pltpu
from jax.sharding import PartitionSpec as P

HALF = 64
BACKGROUND = 0.1
STEP_SIZE = 0.3
EPSILON = 1e-06
STACKED = ("row_inverse",)
NEEDED_IN_ORDER = ("pupil_right", "pupil_left", "kernel_right")
VMEM_LIMIT = 32 * 1024 * 1024


def round_up(value, step):
    return -(-value // step) * step


def angles(left, right, length):
    return (2.0 * math.pi / length) * np.outer(left, right)


def halves(matrix):
    high = matrix.astype(np.float32).astype(ml_dtypes.bfloat16)
    low = (matrix - high.astype(np.float64)).astype(np.float32).astype(ml_dtypes.bfloat16)
    return high, low


def row_constants(rows, length):
    freqs = np.arange(length // 2) + 0.5
    theta = angles(freqs, np.arange(length), length)
    forward = np.concatenate([np.cos(theta), -np.sin(theta)], 0)
    inner = theta[:, HALF : HALF + rows]
    inverse = np.concatenate([np.cos(inner).T, -np.sin(inner).T], 1) * (2.0 / length)
    return forward, inverse


def col_constants(cols):
    half = cols // 2
    forward, inverse = [], []
    for parity in range(2):
        theta = angles(np.arange(half), 2 * np.arange(half) + parity, cols)
        c, s = np.cos(theta), np.sin(theta)
        forward.append(np.block([[c, -s], [s, c]]))
        inverse.append(np.block([[c.T, s.T], [-s.T, c.T]]) / cols)
    return forward, inverse


def kernel_constants(length, cols, ker, pad_rows, pad_cols):
    lags = np.arange(ker) - HALF
    theta = angles(np.arange(length // 2) + 0.5, lags, length)
    rows = np.zeros((length, pad_rows))
    rows[: length // 2, :ker] = np.cos(theta)
    rows[length // 2 :, :ker] = -np.sin(theta)
    half = cols // 2
    right = np.zeros((2 * pad_cols, 2 * cols))
    for parity in range(2):
        theta = angles(lags, 2 * np.arange(half) + parity, cols)
        c, s = np.cos(theta), np.sin(theta)
        at = parity * cols
        right[:ker, at : at + half] = c
        right[:ker, at + half : at + cols] = -s
        right[pad_cols : pad_cols + ker, at : at + half] = s
        right[pad_cols : pad_cols + ker, at + half : at + cols] = c
    return rows, right


def pupil_constants(pup, ker, pad_rows, pad_cols):
    theta = angles(np.arange(ker) - HALF, np.arange(pup), ker)
    real, imag = np.cos(theta), -np.sin(theta)
    right = np.zeros((2 * pup, 2 * pad_cols))
    right[:pup, :ker] = real.T
    right[:pup, pad_cols : pad_cols + ker] = imag.T
    right[pup:, :ker] = -imag.T
    right[pup:, pad_cols : pad_cols + ker] = real.T
    left = np.zeros((2 * pad_rows, 2 * pup))
    left[:ker, :pup] = real
    left[:ker, pup:] = -imag
    left[pad_rows : pad_rows + ker, :pup] = imag
    left[pad_rows : pad_rows + ker, pup:] = real
    return left, right


class Joined:
    def __init__(self, left, right):
        self.places, groups = {}, {}
        for name, matrix in right.items():
            high, low = halves(matrix)
            groups.setdefault(matrix.shape[0], []).append((name, np.concatenate([high, high, low], 0)))
        for name, matrix in left.items():
            high, low = halves(matrix)
            held = np.concatenate([high, low], 0) if name in STACKED else np.concatenate([high, low, high], 1)
            groups.setdefault("left", []).append((name, held))
        self.arrays = []
        for kind, members in groups.items():
            at = 0
            for name, block in members:
                rows, cols = block.shape
                start = (at, 0) if kind == "left" else (0, at)
                self.places[name] = (len(self.arrays), *start, rows, cols)
                at += rows if kind == "left" else cols
            blocks = [block for _, block in members]
            if kind == "left":
                width = max(block.shape[1] for block in blocks)
                blocks = [np.pad(block, ((0, 0), (0, width - block.shape[1]))) for block in blocks]
            self.arrays.append(np.concatenate(blocks, 0 if kind == "left" else 1))

    def at(self, *refs):
        return {
            name: refs[which].at[top : top + rows, first : first + cols]
            for name, (which, top, first, rows, cols) in self.places.items()
        }


def dot(left, right):
    return jnp.dot(left, right, preferred_element_type=jnp.float32)


def split(value):
    high = value.astype(jnp.bfloat16)
    low = (value - high.astype(jnp.float32)).astype(jnp.bfloat16)
    return high, low


def left_by(const, value):
    high, low = split(value)
    return dot(const[...], jnp.concatenate([high, high, low], 0))


def left_stacked(const, value):
    high, low = split(value)
    rows = const.shape[0] // 2
    both = dot(const[...], high)
    return both[:rows] + (both[rows:] + dot(const[:rows], low))


def right_by(value, const):
    high, low = split(value)
    return dot(jnp.concatenate([high, low, high], 1), const[...])


def sine_cosine(angle):
    turns = jnp.floor(angle * (2.0 / math.pi) + 0.5)
    rest = angle - turns * 1.5703125
    rest = rest - turns * 4.837512969970703e-4
    rest = rest - turns * 7.54978995489e-8
    square = rest * rest
    sine = rest + rest * square * (
        -1.6666654611e-1 + square * (8.3321608736e-3 + square * -1.9515295891e-4)
    )
    cosine = 1.0 - 0.5 * square + square * square * (
        4.166664568298827e-2 + square * (-1.388731625493765e-3 + square * 2.443315711809948e-5)
    )
    quadrant = turns.astype(jnp.int32) & 3
    swap = (quadrant & 1) == 1
    sine_out = jnp.where(swap, cosine, sine)
    cosine_out = jnp.where(swap, sine, cosine)
    sine_out = jnp.where(quadrant >= 2, -sine_out, sine_out)
    cosine_out = jnp.where((quadrant == 1) | (quadrant == 2), -cosine_out, cosine_out)
    return sine_out, cosine_out


def total(value):
    return jnp.sum(jnp.sum(value, axis=0, keepdims=True), axis=1, keepdims=True)


def weights(amplitude):
    pup = amplitude.shape[0]
    rows = lax.broadcasted_iota(jnp.int32, amplitude.shape, 0).astype(jnp.float32) - (pup - 1) / 2.0
    cols = lax.broadcasted_iota(jnp.int32, amplitude.shape, 1).astype(jnp.float32) - (pup - 1) / 2.0
    return jnp.where(rows * rows + cols * cols <= (pup / 2.0) ** 2, amplitude, 0.0)


def point_spread(phase, amplitude, const, wait_for=lambda name: None):
    weight = weights(amplitude)
    sine, cosine = sine_cosine(phase)
    pupil = jnp.concatenate([weight * cosine, weight * sine], 1)
    wait_for("pupil_right")
    across = right_by(pupil, const["pupil_right"])
    cols = across.shape[1] // 2
    wait_for("pupil_left")
    field = left_by(const["pupil_left"], jnp.concatenate([across[:, :cols], across[:, cols:]], 0))
    rows = field.shape[0] // 2
    intensity = field[:rows] * field[:rows] + field[rows:] * field[rows:]
    norm = 1.0 / total(intensity)
    left = left_by(const["kernel_rows"], intensity)
    freqs = left.shape[0] // 2
    wait_for("kernel_right")
    spectrum = right_by(jnp.concatenate([left[:freqs], left[freqs:]], 1), const["kernel_right"])
    return pupil, field, spectrum * norm, norm


def mixed_halves(strip, level=None):
    half = strip.shape[1] // 2
    first, second = strip[:, :half], strip[:, half:]
    both = first + second if level is None else first + second - 2.0 * level
    return jnp.concatenate([both, first - second], 1)


def columns(mixed, const):
    sums, differences = [], []
    for strip in mixed:
        half, freqs = strip.shape[1] // 2, strip.shape[0] // 2
        sums.append(jnp.concatenate([strip[:freqs, :half], strip[freqs:, :half]], 1))
        differences.append(jnp.concatenate([strip[:freqs, half:], strip[freqs:, half:]], 1))
    even, odd = [], []
    for p in range(0, len(sums), 2):
        even.append(right_by(jnp.concatenate(sums[p : p + 2], 0), const["forward_even"]))
        odd.append(right_by(jnp.concatenate(differences[p : p + 2], 0), const["forward_odd"]))
    return even, odd


def forward(strips, row_matrix, const):
    return columns([left_by(row_matrix, mixed_halves(strip)) for strip in strips], const)


def inverse(even, odd, freqs, const):
    pairs = [
        (right_by(sums, const["inverse_even"]), right_by(differences, const["inverse_odd"]))
        for sums, differences in zip(even, odd)
    ]
    strips = []
    for sums, differences in pairs:
        half = sums.shape[1] // 2
        for top in range(0, sums.shape[0], freqs):
            rows = slice(top, top + freqs)
            stacked = jnp.concatenate(
                [
                    jnp.concatenate([sums[rows, :half], differences[rows, :half]], 1),
                    jnp.concatenate([sums[rows, half:], differences[rows, half:]], 1),
                ],
                0,
            )
            mixed = left_stacked(const["row_inverse"], stacked)
            first, second = mixed[:, :half], mixed[:, half:]
            strips.append(jnp.concatenate([first + second, first - second], 1))
    return strips


def times(spectra, other, conjugate):
    half = other.shape[1] // 2
    products = []
    for spectrum in spectra:
        planes = spectrum.shape[0] // other.shape[0]
        real = jnp.concatenate([other[:, :half]] * planes, 0)
        imag = jnp.concatenate([other[:, half:]] * planes, 0)
        left, right = spectrum[:, :half], spectrum[:, half:]
        if conjugate:
            product = [left * real + right * imag, right * real - left * imag]
        else:
            product = [left * real - right * imag, left * imag + right * real]
        products.append(jnp.concatenate(product, 1))
    return products


def cross(firsts, seconds, freqs):
    summed = None
    for first, second in zip(firsts, seconds):
        half = first.shape[1] // 2
        left, right = first[:, :half], first[:, half:]
        real, imag = second[:, :half], second[:, half:]
        both = jnp.concatenate([left * real + right * imag, right * real - left * imag], 1)
        for top in range(0, both.shape[0], freqs):
            summed = both[top : top + freqs] if summed is None else summed + both[top : top + freqs]
    return summed


def is_even():
    return lax.axis_index("tile") % 2 == 0


def edge_rows(top, bottom):
    even = is_even()
    return [pl.multiple_of(jnp.where(even, *choice), 8) for choice in ((top, bottom), (bottom, top))]


def near_kernel(own, chip_out, sem):
    chip, _ = edge_rows(0, own.shape[1] - HALF)
    copy = pltpu.make_async_copy(own.at[:, pl.ds(chip, HALF), :], chip_out, sem)
    copy.start()
    copy.wait()


def first_kernel(
    phase, amplitude, own, observed, *refs, at, places, arrays,
):
    psf_refs, outs = refs[:arrays], refs[arrays + 1 : arrays + 9]
    pupil_out, field_out, spec_out, chip_out, core_out, early_out, late_out, means_out = outs
    psf_outs, (phase_in, amplitude_in, own_in, sems) = refs[arrays + 9 : -4], refs[-4:]
    planes, rows, cols = own.shape
    early = early_out.shape[0]
    objects_chip, objects_core = edge_rows(HALF, rows - 2 * HALF)
    observed_chip, observed_core = edge_rows(0, rows - HALF)
    pairs = [
        (phase, phase_in),
        (amplitude, amplitude_in),
        *zip(psf_refs, psf_outs),
        (own.at[:early, pl.ds(observed_core, HALF), :], early_out),
        (own.at[early:, pl.ds(observed_core, HALF), :], late_out),
        (own.at[:, pl.ds(objects_chip, HALF), :], chip_out.at[:planes]),
        (observed.at[:, pl.ds(observed_chip, HALF), :], chip_out.at[planes:]),
        (own.at[:, pl.ds(objects_core, HALF), :], core_out.at[:planes]),
        (observed.at[:, pl.ds(observed_core, HALF), :], core_out.at[planes:]),
        (own, own_in),
    ]
    copies = [pltpu.make_async_copy(source, target, sems.at[i]) for i, (source, target) in enumerate(pairs)]
    for i in (0, 1, *(2 + places[name][0] for name in NEEDED_IN_ORDER), *range(2 + arrays, len(copies))):
        copies[i].start()
    for copy in copies[:2]:
        copy.wait()

    def wait_for(name):
        copies[2 + places[name][0]].wait()

    pupil, field, spectrum, norm = point_spread(phase_in[...], amplitude_in[...], at(*psf_outs), wait_for)
    root = jnp.sqrt(norm)
    pupil_out[...] = pupil * root
    field_out[...] = field * root
    spec_out[...] = spectrum
    for copy in copies[2 + arrays :]:
        copy.wait()
    for p in range(planes):
        means_out[p] = jnp.broadcast_to(total(own_in[p]) * (1.0 / (rows * cols)), means_out.shape[1:])


def halo_rows(chip, core):
    even = is_even()
    return jnp.where(even, chip, core), jnp.where(even, core, chip)


def known_kernel(own, means, *refs, at):
    const, known_out = at(*refs[:-1]), refs[-1]
    for p in range(own.shape[0]):
        known_out[p] = left_by(const["row_own"], mixed_halves(own[p], means[p][:1, :1]))


def gradient_kernel(
    from_chip, early_core, late_core, known, observed, spec, pupil, field, means, *refs, at,
):
    planes = known.shape[0]
    cols = known.shape[2]
    const = at(*refs[:-2])
    keep_out, give_out = refs[-2:]
    freqs = spec.shape[0]
    early = early_core.shape[0]
    levels = [means[p][:1, :1] for p in range(planes)]
    mixed = []
    for p in range(planes):
        edges = halo_rows(from_chip[p], early_core[p] if p < early else late_core[p - early])
        edges = mixed_halves(jnp.concatenate(edges, 0), levels[p])
        mixed.append(known[p] + left_by(const["row_edges"], edges))
    even, odd = columns(mixed, const)
    blurred = inverse(times(even, spec[:, :cols], False), times(odd, spec[:, cols:], False), freqs, const)
    misfit = [1.0 - observed[p] / (blurred[p] + (levels[p] + BACKGROUND)) for p in range(planes)]
    weighted = misfit[0] * blurred[0]
    for p in range(1, planes):
        weighted = weighted + misfit[p] * blurred[p]
    mean = total(weighted)
    misfit_even, misfit_odd = forward(misfit, const["row_own"], const)
    shared = jnp.concatenate([cross(misfit_even, even, freqs), cross(misfit_odd, odd, freqs)], 1)
    across = right_by(shared, const["lag_right"])
    pad_cols = across.shape[1] // 2
    psf_grad = left_by(const["lag_left"], jnp.concatenate([across[:, :pad_cols], across[:, pad_cols:]], 0))
    far = field[...]
    pad_rows = far.shape[0] // 2
    real, imag = far[:pad_rows], far[pad_rows:]
    centred = 2.0 * (psf_grad - mean)
    back = left_by(const["adjoint_left"], jnp.concatenate([centred * real, centred * imag], 0))
    pup = back.shape[0] // 2
    back = right_by(jnp.concatenate([back[:pup], back[pup:]], 1), const["adjoint_right"])
    near = pupil[...]
    slope = back[:, pup:] * near[:, :pup] - back[:, :pup] * near[:, pup:]
    even_core = is_even()
    keep_out[...] = jnp.where(even_core, slope[: pup // 2], slope[pup // 2 :])
    give_out[...] = jnp.where(even_core, slope[pup // 2 :], slope[: pup // 2])


def square_sums(value):
    rows = value.shape[0]
    squared = value * value
    summed = squared[:8]
    for top in range(8, rows, 8):
        summed = summed + squared[top : top + 8]
    return summed


def squares_kernel(mine, received, *others):
    joined_out = others[-1]
    half = mine[...] + received[...]
    squares = square_sums(half)
    for first, second in zip(others[:-1:2], others[1:-1:2]):
        squares = squares + square_sums(first[...] + second[...])
    joined_out[: half.shape[0]] = half
    joined_out[half.shape[0] :] = squares


def blocks_kernel(from_chip, early_core, late_core, own, far_chip, far_core, _, *refs, at):
    planes = own.shape[0]
    const = at(*refs[:-2])
    even_out, odd_out = refs[-2:]
    early = early_core.shape[0]
    strips = []
    for p in range(planes):
        above, below = halo_rows(from_chip[p], early_core[p] if p < early else late_core[p - early])
        far_above, far_below = halo_rows(far_chip[p], far_core[p])
        strips.append(jnp.concatenate([far_above, above, own[p]], 0))
        strips.append(jnp.concatenate([own[p], below, far_below], 0))
    even, odd = forward(strips, const["row_forward"], const)
    even_out[...] = jnp.concatenate(even, 0)
    odd_out[...] = jnp.concatenate(odd, 0)


def second_kernel(phase, amplitude, mine, theirs, *refs, at, psf_at, arrays, cells, squares_apart):
    if squares_apart:
        squares, *refs = refs
    even, odd, own, observed, far_chip, far_core, *refs = refs
    planes, rows, cols = own.shape
    const = at(*refs[:arrays])
    psf_const = psf_at(*refs[arrays:-5])
    objects_out, phase_out, objects, new_phase, sems = refs[-5:]
    writes = [pltpu.make_async_copy(new_phase, phase_out, sems.at[planes])]
    half = phase.shape[0] // 2
    first, second = halo_rows(mine[:half], theirs[:half])
    slope = jnp.concatenate([first, second], 0)
    summed = squares[...] if squares_apart else mine[half:] + theirs[half:]
    mean_square = total(summed) * (1.0 / cells)
    updated = phase[...] - STEP_SIZE * slope / jnp.sqrt(mean_square + EPSILON)
    new_phase[...] = updated
    writes[0].start()
    _, _, spec, _ = point_spread(updated, amplitude[...], psf_const)
    spec_even, spec_odd = spec[:, :cols], spec[:, cols:]
    freqs = spec.shape[0]
    pairs = range(0, even.shape[0], 2 * freqs)
    light = inverse(
        times([even[top : top + 2 * freqs] for top in pairs], spec_even, False),
        times([odd[top : top + 2 * freqs] for top in pairs], spec_odd, False),
        freqs, const,
    )
    ratios = []
    for p in range(planes):
        above, below = halo_rows(far_chip[planes + p], far_core[planes + p])
        blurred = jnp.concatenate(light[2 * p : 2 * p + 2], 0) + BACKGROUND
        ratios.append(jnp.concatenate([above, observed[p], below], 0) / blurred)
    ratio_even, ratio_odd = forward(ratios, const["row_forward"], const)
    correction = inverse(times(ratio_even, spec_even, True), times(ratio_odd, spec_odd, True), freqs, const)
    for p in range(planes):
        objects[p] = own[p] * correction[p]
        writes.append(pltpu.make_async_copy(objects.at[p], objects_out.at[p], sems.at[p]))
        writes[-1].start()
    for write in writes:
        write.wait()


def call(kernel, out_shapes, args, flops=10**6, spaces=None, scratch=(), out_space=pltpu.VMEM):
    outs = [
        jax.ShapeDtypeStruct(shape, jnp.float32) if isinstance(shape, tuple) else shape for shape in out_shapes
    ]
    spaces = spaces or {}
    return pl.pallas_call(
        kernel,
        out_shape=outs,
        in_specs=[pl.BlockSpec(memory_space=spaces.get(i, pltpu.VMEM)) for i in range(len(args))],
        out_specs=[pl.BlockSpec(memory_space=out_space)] * len(outs),
        scratch_shapes=scratch,
        compiler_params=pltpu.CompilerParams(vmem_limit_bytes=VMEM_LIMIT),
        cost_estimate=pl.CostEstimate(flops=flops, bytes_accessed=10**5, transcendentals=0),
    )(*args)


def to_next_chip(value):
    count = lax.axis_size("tile")
    return lax.ppermute(value, "tile", [(i, (i + 1 if i % 2 else i - 1) % count) for i in range(count)])


def exchange(value, step):
    return lax.ppermute(value, "tile", [(i, i ^ step) for i in range(lax.axis_size("tile"))])


def across_depth_and_chip(value):
    pairs = [(2 * t + d, 2 * (t ^ 2) + 1 - d) for t in range(lax.axis_size("tile")) for d in range(2)]
    return lax.ppermute(value, ("tile", "depth"), pairs)


def sum_over_depth(value):
    count = lax.axis_size("depth")
    if count & (count - 1):
        return lax.psum(value, "depth")
    for bit in range(count.bit_length() - 1):
        value = value + lax.ppermute(value, "depth", [(i, i ^ (1 << bit)) for i in range(count)])
    return value


def on_device(objects, observed, pupil_phase, pupil_amplitude):
    picture, measured, phase, amplitude = objects[0], observed[0], pupil_phase[0], pupil_amplitude[0]
    planes, rows, cols = picture.shape
    pup = phase.shape[0]
    count = lax.axis_size("tile")
    ker = 2 * HALF + 1
    length = rows + 2 * HALF
    pad_rows, pad_cols = round_up(ker, 16), round_up(ker, 128)
    row_forward, row_inverse = row_constants(rows, length)
    col_forward, col_inverse = col_constants(cols)
    kernel_rows, kernel_right = kernel_constants(length, cols, ker, pad_rows, pad_cols)
    pupil_left, pupil_right = pupil_constants(pup, ker, pad_rows, pad_cols)
    psf_const = Joined(
        {"pupil_left": pupil_left, "kernel_rows": kernel_rows},
        {"pupil_right": pupil_right, "kernel_right": kernel_right},
    )
    block_left = {"row_forward": row_forward, "row_inverse": row_inverse}
    block_right = {
        "forward_even": col_forward[0],
        "forward_odd": col_forward[1],
        "inverse_even": col_inverse[0],
        "inverse_odd": col_inverse[1],
    }
    block_const = Joined(block_left, block_right)
    lag_const = Joined(
        {
            "row_edges": np.concatenate([row_forward[:, :HALF], row_forward[:, HALF + rows :]], 1),
            "lag_left": kernel_rows.T * (2.0 / length),
            "adjoint_left": pupil_left.T,
        },
        {"lag_right": kernel_right.T / cols, "adjoint_right": pupil_right.T},
    )
    own_const = Joined({"row_own": row_forward[:, HALF : HALF + rows]}, {})
    psf_arrays, block_arrays, lag_arrays, own_arrays = (
        [jnp.asarray(array) for array in const.arrays] for const in (psf_const, block_const, lag_const, own_const)
    )

    def gradient_at(*refs):
        held = len(block_arrays)
        end = held + len(lag_arrays)
        return {**block_const.at(*refs[:held]), **lag_const.at(*refs[held:end]), **own_const.at(*refs[end:])}

    in_hbm = [
        pltpu.with_memory_space_constraint(value, pltpu.HBM)
        for value in (phase, amplitude, picture, measured, *psf_arrays)
    ]
    (chip_rows,) = call(
        near_kernel, [(planes, HALF, cols)], in_hbm[2:3], scratch=[pltpu.SemaphoreType.DMA(())], spaces={0: pltpu.HBM}
    )
    from_chip = to_next_chip(chip_rows)
    pupil, field, spec, far_chip, far_core, early_rows, late_rows, means, *psf_arrays = call(
        functools.partial(first_kernel, at=psf_const.at, places=psf_const.places, arrays=len(psf_arrays)),
        [(pup, 2 * pup), (2 * pad_rows, pad_cols), (length // 2, 2 * cols)]
        + [(2 * planes, HALF, cols)] * 2
        + [(planes // 2, HALF, cols), (planes - planes // 2, HALF, cols), (planes, 8, 128)]
        + psf_arrays,
        (*in_hbm, chip_rows),
        flops=3 * 10**9,
        spaces={**dict.fromkeys(range(len(in_hbm)), pltpu.HBM), len(in_hbm): pl.ANY},
        scratch=[pltpu.VMEM(value.shape, jnp.float32) for value in (phase, amplitude, picture)]
        + [pltpu.SemaphoreType.DMA((9 + len(psf_arrays),))],
    )
    early_core, late_core, far_core = (exchange(value, 1) for value in (early_rows, late_rows, far_core))
    (known,) = call(
        functools.partial(known_kernel, at=own_const.at),
        [(planes, length, cols)],
        (picture, means, *own_arrays),
        flops=10**3,
    )
    far_chip, known = lax.optimization_barrier((far_chip, known))
    far_chip = to_next_chip(far_chip)
    keep, give = call(
        functools.partial(gradient_kernel, at=gradient_at),
        [(pup // 2, pup)] * 2,
        (
            from_chip, early_core, late_core, known, measured, spec, pupil, field, means, *block_arrays, *lag_arrays,
            *own_arrays,
        ),
        flops=4 * 10**10,
    )
    half = keep + exchange(give, 1)
    bits = list(range(2, count.bit_length() - 1))
    for low, high in zip(bits[::2], bits[1::2]):
        half = half + ((exchange(half, 1 << low) + exchange(half, 1 << high)) + exchange(half, (1 << low) | (1 << high)))
    if len(bits) % 2:
        half = half + exchange(half, 1 << bits[-1])
    last_round = [exchange(half, 2)]
    two_strata = lax.axis_size("depth") == 2
    if two_strata:
        last_round += [lax.ppermute(half, "depth", [(0, 1), (1, 0)]), across_depth_and_chip(half)]
    even, odd = call(
        functools.partial(blocks_kernel, at=block_const.at),
        [(planes * length, cols)] * 2,
        (from_chip, early_core, late_core, picture, far_chip, far_core, half, *block_arrays),
        spaces={6: pl.ANY},
    )
    even, *last_round = lax.optimization_barrier((even, *last_round))
    (joined,) = call(squares_kernel, [(pup // 2 + 8, pup)], (half, *last_round))
    other = exchange(joined, 1)
    squares = []
    if not two_strata:
        squares = [sum_over_depth(joined[pup // 2 :] + other[pup // 2 :])]
    new_objects, new_phase = call(
        functools.partial(
            second_kernel,
            at=block_const.at,
            psf_at=psf_const.at,
            arrays=len(block_arrays),
            cells=lax.axis_size("depth") * pup * pup,
            squares_apart=bool(squares),
        ),
        [picture.shape, phase.shape],
        (
            phase, amplitude, joined, other, *squares, even, odd, picture, measured,
            far_chip, far_core, *block_arrays, *psf_arrays,
        ),
        scratch=[pltpu.VMEM(value.shape, jnp.float32) for value in (picture, phase)]
        + [pltpu.SemaphoreType.DMA((planes + 1,))],
        out_space=pltpu.HBM,
    )
    return new_objects[None], new_phase[None]


def solution(mesh):
    return jax.shard_map(
        on_device,
        mesh=mesh,
        in_specs=(
            P("depth", None, "tile", None),
            P("depth", None, "tile", None),
            P("depth", None, None),
            P("depth", None, None),
        ),
        out_specs=(P("depth", None, "tile", None), P("depth", None, None)),
        check_vma=False,
    )
```

```python
import functools
import math

import jax
import jax.numpy as jnp
import ml_dtypes
import numpy as np
from jax import lax
from jax.experimental import pallas as pl
from jax.experimental.pallas import tpu as pltpu
from jax.sharding import PartitionSpec as P

HALF = 64
BACKGROUND = 0.1
STEP_SIZE = 0.3
EPSILON = 1e-06
STACKED = ("row_inverse",)
NEEDED_IN_ORDER = ("pupil_right", "pupil_left", "kernel_right")
VMEM_LIMIT = 32 * 1024 * 1024


def round_up(value, step):
    return -(-value // step) * step


def angles(left, right, length):
    return (2.0 * math.pi / length) * np.outer(left, right)


def halves(matrix):
    high = matrix.astype(np.float32).astype(ml_dtypes.bfloat16)
    low = (matrix - high.astype(np.float64)).astype(np.float32).astype(ml_dtypes.bfloat16)
    return high, low


def row_constants(rows, length):
    freqs = np.arange(length // 2) + 0.5
    theta = angles(freqs, np.arange(length), length)
    forward = np.concatenate([np.cos(theta), -np.sin(theta)], 0)
    inner = theta[:, HALF : HALF + rows]
    inverse = np.concatenate([np.cos(inner).T, -np.sin(inner).T], 1) * (2.0 / length)
    return forward, inverse


def col_constants(cols):
    half = cols // 2
    forward, inverse = [], []
    for parity in range(2):
        theta = angles(np.arange(half), 2 * np.arange(half) + parity, cols)
        c, s = np.cos(theta), np.sin(theta)
        forward.append(np.block([[c, -s], [s, c]]))
        inverse.append(np.block([[c.T, s.T], [-s.T, c.T]]) / cols)
    return forward, inverse


def kernel_constants(length, cols, ker, pad_rows, pad_cols):
    lags = np.arange(ker) - HALF
    theta = angles(np.arange(length // 2) + 0.5, lags, length)
    rows = np.zeros((length, pad_rows))
    rows[: length // 2, :ker] = np.cos(theta)
    rows[length // 2 :, :ker] = -np.sin(theta)
    half = cols // 2
    right = np.zeros((2 * pad_cols, 2 * cols))
    for parity in range(2):
        theta = angles(lags, 2 * np.arange(half) + parity, cols)
        c, s = np.cos(theta), np.sin(theta)
        at = parity * cols
        right[:ker, at : at + half] = c
        right[:ker, at + half : at + cols] = -s
        right[pad_cols : pad_cols + ker, at : at + half] = s
        right[pad_cols : pad_cols + ker, at + half : at + cols] = c
    return rows, right


def pupil_constants(pup, ker, pad_rows, pad_cols):
    theta = angles(np.arange(ker) - HALF, np.arange(pup), ker)
    real, imag = np.cos(theta), -np.sin(theta)
    right = np.zeros((2 * pup, 2 * pad_cols))
    right[:pup, :ker] = real.T
    right[:pup, pad_cols : pad_cols + ker] = imag.T
    right[pup:, :ker] = -imag.T
    right[pup:, pad_cols : pad_cols + ker] = real.T
    left = np.zeros((2 * pad_rows, 2 * pup))
    left[:ker, :pup] = real
    left[:ker, pup:] = -imag
    left[pad_rows : pad_rows + ker, :pup] = imag
    left[pad_rows : pad_rows + ker, pup:] = real
    return left, right


class Joined:
    def __init__(self, left, right):
        self.places, groups = {}, {}
        for name, matrix in right.items():
            high, low = halves(matrix)
            groups.setdefault(matrix.shape[0], []).append((name, np.concatenate([high, high, low], 0)))
        for name, matrix in left.items():
            high, low = halves(matrix)
            held = np.concatenate([high, low], 0) if name in STACKED else np.concatenate([high, low, high], 1)
            groups.setdefault("left", []).append((name, held))
        self.arrays = []
        for kind, members in groups.items():
            at = 0
            for name, block in members:
                rows, cols = block.shape
                start = (at, 0) if kind == "left" else (0, at)
                self.places[name] = (len(self.arrays), *start, rows, cols)
                at += rows if kind == "left" else cols
            blocks = [block for _, block in members]
            if kind == "left":
                width = max(block.shape[1] for block in blocks)
                blocks = [np.pad(block, ((0, 0), (0, width - block.shape[1]))) for block in blocks]
            self.arrays.append(np.concatenate(blocks, 0 if kind == "left" else 1))

    def at(self, *refs):
        return {
            name: refs[which].at[top : top + rows, first : first + cols]
            for name, (which, top, first, rows, cols) in self.places.items()
        }


def dot(left, right):
    return jnp.dot(left, right, preferred_element_type=jnp.float32)


def split(value):
    high = value.astype(jnp.bfloat16)
    low = (value - high.astype(jnp.float32)).astype(jnp.bfloat16)
    return high, low


def left_by(const, value):
    high, low = split(value)
    return dot(const[...], jnp.concatenate([high, high, low], 0))


def left_stacked(const, value):
    high, low = split(value)
    rows = const.shape[0] // 2
    both = dot(const[...], high)
    return both[:rows] + (both[rows:] + dot(const[:rows], low))


def right_by(value, const):
    high, low = split(value)
    return dot(jnp.concatenate([high, low, high], 1), const[...])


def sine_cosine(angle):
    turns = jnp.floor(angle * (2.0 / math.pi) + 0.5)
    rest = angle - turns * 1.5703125
    rest = rest - turns * 4.837512969970703e-4
    rest = rest - turns * 7.54978995489e-8
    square = rest * rest
    sine = rest + rest * square * (
        -1.6666654611e-1 + square * (8.3321608736e-3 + square * -1.9515295891e-4)
    )
    cosine = 1.0 - 0.5 * square + square * square * (
        4.166664568298827e-2 + square * (-1.388731625493765e-3 + square * 2.443315711809948e-5)
    )
    quadrant = turns.astype(jnp.int32) & 3
    swap = (quadrant & 1) == 1
    sine_out = jnp.where(swap, cosine, sine)
    cosine_out = jnp.where(swap, sine, cosine)
    sine_out = jnp.where(quadrant >= 2, -sine_out, sine_out)
    cosine_out = jnp.where((quadrant == 1) | (quadrant == 2), -cosine_out, cosine_out)
    return sine_out, cosine_out


def total(value):
    return jnp.sum(jnp.sum(value, axis=0, keepdims=True), axis=1, keepdims=True)


def weights(amplitude):
    pup = amplitude.shape[0]
    rows = lax.broadcasted_iota(jnp.int32, amplitude.shape, 0).astype(jnp.float32) - (pup - 1) / 2.0
    cols = lax.broadcasted_iota(jnp.int32, amplitude.shape, 1).astype(jnp.float32) - (pup - 1) / 2.0
    return jnp.where(rows * rows + cols * cols <= (pup / 2.0) ** 2, amplitude, 0.0)


def point_spread(phase, amplitude, const, wait_for=lambda name: None):
    weight = weights(amplitude)
    sine, cosine = sine_cosine(phase)
    pupil = jnp.concatenate([weight * cosine, weight * sine], 1)
    wait_for("pupil_right")
    across = right_by(pupil, const["pupil_right"])
    cols = across.shape[1] // 2
    wait_for("pupil_left")
    field = left_by(const["pupil_left"], jnp.concatenate([across[:, :cols], across[:, cols:]], 0))
    rows = field.shape[0] // 2
    intensity = field[:rows] * field[:rows] + field[rows:] * field[rows:]
    norm = 1.0 / total(intensity)
    left = left_by(const["kernel_rows"], intensity)
    freqs = left.shape[0] // 2
    wait_for("kernel_right")
    spectrum = right_by(jnp.concatenate([left[:freqs], left[freqs:]], 1), const["kernel_right"])
    return pupil, field, spectrum * norm, norm


def mixed_halves(strip, level=None):
    half = strip.shape[1] // 2
    first, second = strip[:, :half], strip[:, half:]
    both = first + second if level is None else first + second - 2.0 * level
    return jnp.concatenate([both, first - second], 1)


def columns(mixed, const):
    sums, differences = [], []
    for strip in mixed:
        half, freqs = strip.shape[1] // 2, strip.shape[0] // 2
        sums.append(jnp.concatenate([strip[:freqs, :half], strip[freqs:, :half]], 1))
        differences.append(jnp.concatenate([strip[:freqs, half:], strip[freqs:, half:]], 1))
    even = [right_by(jnp.concatenate(sums[p : p + 2], 0), const["forward_even"]) for p in range(0, len(sums), 2)]
    odd = [right_by(jnp.concatenate(differences[p : p + 2], 0), const["forward_odd"]) for p in range(0, len(sums), 2)]
    return even, odd


def forward(strips, row_matrix, const):
    return columns([left_by(row_matrix, mixed_halves(strip)) for strip in strips], const)


def inverse(even, odd, freqs, const):
    even = [right_by(spectrum, const["inverse_even"]) for spectrum in even]
    odd = [right_by(spectrum, const["inverse_odd"]) for spectrum in odd]
    strips = []
    for sums, differences in zip(even, odd):
        half = sums.shape[1] // 2
        for top in range(0, sums.shape[0], freqs):
            rows = slice(top, top + freqs)
            stacked = jnp.concatenate(
                [
                    jnp.concatenate([sums[rows, :half], differences[rows, :half]], 1),
                    jnp.concatenate([sums[rows, half:], differences[rows, half:]], 1),
                ],
                0,
            )
            mixed = left_stacked(const["row_inverse"], stacked)
            first, second = mixed[:, :half], mixed[:, half:]
            strips.append(jnp.concatenate([first + second, first - second], 1))
    return strips


def times(spectra, other, conjugate):
    half = other.shape[1] // 2
    products = []
    for spectrum in spectra:
        planes = spectrum.shape[0] // other.shape[0]
        real = jnp.concatenate([other[:, :half]] * planes, 0)
        imag = jnp.concatenate([other[:, half:]] * planes, 0)
        left, right = spectrum[:, :half], spectrum[:, half:]
        if conjugate:
            product = [left * real + right * imag, right * real - left * imag]
        else:
            product = [left * real - right * imag, left * imag + right * real]
        products.append(jnp.concatenate(product, 1))
    return products


def cross(firsts, seconds, freqs):
    summed = None
    for first, second in zip(firsts, seconds):
        half = first.shape[1] // 2
        left, right = first[:, :half], first[:, half:]
        real, imag = second[:, :half], second[:, half:]
        both = jnp.concatenate([left * real + right * imag, right * real - left * imag], 1)
        for top in range(0, both.shape[0], freqs):
            summed = both[top : top + freqs] if summed is None else summed + both[top : top + freqs]
    return summed


def is_even():
    return lax.axis_index("tile") % 2 == 0


def edge_rows(top, bottom):
    even = is_even()
    return [pl.multiple_of(jnp.where(even, *choice), 8) for choice in ((top, bottom), (bottom, top))]


def near_kernel(own, chip_out, sem):
    chip, _ = edge_rows(0, own.shape[1] - HALF)
    copy = pltpu.make_async_copy(own.at[:, pl.ds(chip, HALF), :], chip_out, sem)
    copy.start()
    copy.wait()


def first_kernel(
    phase, amplitude, own, observed, *refs, at, places, arrays,
):
    psf_refs, outs = refs[:arrays], refs[arrays + 1 : arrays + 8]
    pupil_out, field_out, spec_out, chip_out, core_out, early_out, late_out = outs
    psf_outs, (phase_in, amplitude_in, sems) = refs[arrays + 8 : -3], refs[-3:]
    planes, rows, _ = own.shape
    early = early_out.shape[0]
    objects_chip, objects_core = edge_rows(HALF, rows - 2 * HALF)
    observed_chip, observed_core = edge_rows(0, rows - HALF)
    pairs = [
        (phase, phase_in),
        (amplitude, amplitude_in),
        *zip(psf_refs, psf_outs),
        (own.at[:early, pl.ds(observed_core, HALF), :], early_out),
        (own.at[early:, pl.ds(observed_core, HALF), :], late_out),
        (own.at[:, pl.ds(objects_chip, HALF), :], chip_out.at[:planes]),
        (observed.at[:, pl.ds(observed_chip, HALF), :], chip_out.at[planes:]),
        (own.at[:, pl.ds(objects_core, HALF), :], core_out.at[:planes]),
        (observed.at[:, pl.ds(observed_core, HALF), :], core_out.at[planes:]),
    ]
    copies = [pltpu.make_async_copy(source, target, sems.at[i]) for i, (source, target) in enumerate(pairs)]
    for i in (0, 1, *(2 + places[name][0] for name in NEEDED_IN_ORDER), *range(2 + arrays, len(copies))):
        copies[i].start()
    for copy in copies[:2]:
        copy.wait()

    def wait_for(name):
        copies[2 + places[name][0]].wait()

    pupil, field, spectrum, norm = point_spread(phase_in[...], amplitude_in[...], at(*psf_outs), wait_for)
    root = jnp.sqrt(norm)
    pupil_out[...] = pupil * root
    field_out[...] = field * root
    spec_out[...] = spectrum
    for copy in copies[2 + arrays :]:
        copy.wait()


def halo_rows(chip, core):
    even = is_even()
    return jnp.where(even, chip, core), jnp.where(even, core, chip)


def known_kernel(own, *refs, at):
    const, (known_out, means_out) = at(*refs[:-2]), refs[-2:]
    planes, rows, cols = own.shape
    for p in range(planes):
        mean = total(own[p]) * (1.0 / (rows * cols))
        known_out[p] = left_by(const["row_own"], mixed_halves(own[p], mean))
        means_out[p] = jnp.broadcast_to(mean, means_out.shape[1:])


def gradient_kernel(
    from_chip, early_core, late_core, known, observed, spec, pupil, field, means, *refs, at,
):
    planes = known.shape[0]
    cols = known.shape[2]
    const = at(*refs[:-2])
    keep_out, give_out = refs[-2:]
    freqs = spec.shape[0]
    early = early_core.shape[0]
    levels = [means[p][:1, :1] for p in range(planes)]
    mixed = []
    for p in range(planes):
        edges = halo_rows(from_chip[p], early_core[p] if p < early else late_core[p - early])
        edges = mixed_halves(jnp.concatenate(edges, 0), levels[p])
        mixed.append(known[p] + left_by(const["row_edges"], edges))
    even, odd = columns(mixed, const)
    blurred = inverse(times(even, spec[:, :cols], False), times(odd, spec[:, cols:], False), freqs, const)
    misfit = [1.0 - observed[p] / (blurred[p] + (levels[p] + BACKGROUND)) for p in range(planes)]
    weighted = misfit[0] * blurred[0]
    for p in range(1, planes):
        weighted = weighted + misfit[p] * blurred[p]
    mean = total(weighted)
    misfit_even, misfit_odd = forward(misfit, const["row_own"], const)
    shared = jnp.concatenate([cross(misfit_even, even, freqs), cross(misfit_odd, odd, freqs)], 1)
    across = right_by(shared, const["lag_right"])
    pad_cols = across.shape[1] // 2
    psf_grad = left_by(const["lag_left"], jnp.concatenate([across[:, :pad_cols], across[:, pad_cols:]], 0))
    far = field[...]
    pad_rows = far.shape[0] // 2
    real, imag = far[:pad_rows], far[pad_rows:]
    centred = 2.0 * (psf_grad - mean)
    back = left_by(const["adjoint_left"], jnp.concatenate([centred * real, centred * imag], 0))
    pup = back.shape[0] // 2
    back = right_by(jnp.concatenate([back[:pup], back[pup:]], 1), const["adjoint_right"])
    near = pupil[...]
    slope = back[:, pup:] * near[:, :pup] - back[:, :pup] * near[:, pup:]
    even_core = is_even()
    keep_out[...] = jnp.where(even_core, slope[: pup // 2], slope[pup // 2 :])
    give_out[...] = jnp.where(even_core, slope[pup // 2 :], slope[: pup // 2])


def square_sums(value):
    rows = value.shape[0]
    squared = value * value
    summed = squared[:8]
    for top in range(8, rows, 8):
        summed = summed + squared[top : top + 8]
    return summed


def squares_kernel(mine, received, *others):
    joined_out = others[-1]
    half = mine[...] + received[...]
    squares = square_sums(half)
    for first, second in zip(others[:-1:2], others[1:-1:2]):
        squares = squares + square_sums(first[...] + second[...])
    joined_out[: half.shape[0]] = half
    joined_out[half.shape[0] :] = squares


def blocks_kernel(from_chip, early_core, late_core, own, far_chip, far_core, _, *refs, at):
    planes = own.shape[0]
    const = at(*refs[:-2])
    even_out, odd_out = refs[-2:]
    early = early_core.shape[0]
    strips = []
    for p in range(planes):
        above, below = halo_rows(from_chip[p], early_core[p] if p < early else late_core[p - early])
        far_above, far_below = halo_rows(far_chip[p], far_core[p])
        strips.append(jnp.concatenate([far_above, above, own[p]], 0))
        strips.append(jnp.concatenate([own[p], below, far_below], 0))
    even, odd = forward(strips, const["row_forward"], const)
    even_out[...] = jnp.concatenate(even, 0)
    odd_out[...] = jnp.concatenate(odd, 0)


def second_kernel(phase, amplitude, mine, theirs, *refs, at, psf_at, arrays, cells, squares_apart):
    if squares_apart:
        squares, *refs = refs
    even, odd, own, observed, far_chip, far_core, *refs = refs
    planes, rows, cols = own.shape
    const = at(*refs[:arrays])
    psf_const = psf_at(*refs[arrays:-5])
    objects_out, phase_out, objects, new_phase, sems = refs[-5:]
    writes = [pltpu.make_async_copy(new_phase, phase_out, sems.at[planes])]
    half = phase.shape[0] // 2
    first, second = halo_rows(mine[:half], theirs[:half])
    slope = jnp.concatenate([first, second], 0)
    summed = squares[...] if squares_apart else mine[half:] + theirs[half:]
    mean_square = total(summed) * (1.0 / cells)
    updated = phase[...] - STEP_SIZE * slope / jnp.sqrt(mean_square + EPSILON)
    new_phase[...] = updated
    writes[0].start()
    _, _, spec, _ = point_spread(updated, amplitude[...], psf_const)
    spec_even, spec_odd = spec[:, :cols], spec[:, cols:]
    freqs = spec.shape[0]
    pairs = range(0, even.shape[0], 2 * freqs)
    light = inverse(
        times([even[top : top + 2 * freqs] for top in pairs], spec_even, False),
        times([odd[top : top + 2 * freqs] for top in pairs], spec_odd, False),
        freqs, const,
    )
    ratios = []
    for p in range(planes):
        above, below = halo_rows(far_chip[planes + p], far_core[planes + p])
        blurred = jnp.concatenate(light[2 * p : 2 * p + 2], 0) + BACKGROUND
        ratios.append(jnp.concatenate([above, observed[p], below], 0) / blurred)
    ratio_even, ratio_odd = forward(ratios, const["row_forward"], const)
    correction = inverse(times(ratio_even, spec_even, True), times(ratio_odd, spec_odd, True), freqs, const)
    for p in range(planes):
        objects[p] = own[p] * correction[p]
        writes.append(pltpu.make_async_copy(objects.at[p], objects_out.at[p], sems.at[p]))
        writes[-1].start()
    for write in writes:
        write.wait()


def call(kernel, out_shapes, args, flops=10**6, spaces=None, scratch=(), out_space=pltpu.VMEM):
    outs = [
        jax.ShapeDtypeStruct(shape, jnp.float32) if isinstance(shape, tuple) else shape for shape in out_shapes
    ]
    spaces = spaces or {}
    return pl.pallas_call(
        kernel,
        out_shape=outs,
        in_specs=[pl.BlockSpec(memory_space=spaces.get(i, pltpu.VMEM)) for i in range(len(args))],
        out_specs=[pl.BlockSpec(memory_space=out_space)] * len(outs),
        scratch_shapes=scratch,
        compiler_params=pltpu.CompilerParams(vmem_limit_bytes=VMEM_LIMIT),
        cost_estimate=pl.CostEstimate(flops=flops, bytes_accessed=10**5, transcendentals=0),
    )(*args)


def to_next_chip(value):
    count = lax.axis_size("tile")
    return lax.ppermute(value, "tile", [(i, (i + 1 if i % 2 else i - 1) % count) for i in range(count)])


def exchange(value, step):
    return lax.ppermute(value, "tile", [(i, i ^ step) for i in range(lax.axis_size("tile"))])


def across_depth_and_chip(value):
    pairs = [(2 * t + d, 2 * (t ^ 2) + 1 - d) for t in range(lax.axis_size("tile")) for d in range(2)]
    return lax.ppermute(value, ("tile", "depth"), pairs)


def sum_over_depth(value):
    count = lax.axis_size("depth")
    if count & (count - 1):
        return lax.psum(value, "depth")
    for bit in range(count.bit_length() - 1):
        value = value + lax.ppermute(value, "depth", [(i, i ^ (1 << bit)) for i in range(count)])
    return value


def on_device(objects, observed, pupil_phase, pupil_amplitude):
    picture, measured, phase, amplitude = objects[0], observed[0], pupil_phase[0], pupil_amplitude[0]
    planes, rows, cols = picture.shape
    pup = phase.shape[0]
    count = lax.axis_size("tile")
    ker = 2 * HALF + 1
    length = rows + 2 * HALF
    pad_rows, pad_cols = round_up(ker, 16), round_up(ker, 128)
    row_forward, row_inverse = row_constants(rows, length)
    col_forward, col_inverse = col_constants(cols)
    kernel_rows, kernel_right = kernel_constants(length, cols, ker, pad_rows, pad_cols)
    pupil_left, pupil_right = pupil_constants(pup, ker, pad_rows, pad_cols)
    psf_const = Joined(
        {"pupil_left": pupil_left, "kernel_rows": kernel_rows},
        {"pupil_right": pupil_right, "kernel_right": kernel_right},
    )
    block_left = {"row_forward": row_forward, "row_inverse": row_inverse}
    block_right = {
        "forward_even": col_forward[0],
        "forward_odd": col_forward[1],
        "inverse_even": col_inverse[0],
        "inverse_odd": col_inverse[1],
    }
    block_const = Joined(block_left, block_right)
    lag_const = Joined(
        {
            "row_edges": np.concatenate([row_forward[:, :HALF], row_forward[:, HALF + rows :]], 1),
            "lag_left": kernel_rows.T * (2.0 / length),
            "adjoint_left": pupil_left.T,
        },
        {"lag_right": kernel_right.T / cols, "adjoint_right": pupil_right.T},
    )
    own_const = Joined({"row_own": row_forward[:, HALF : HALF + rows]}, {})
    psf_arrays, block_arrays, lag_arrays, own_arrays = (
        [jnp.asarray(array) for array in const.arrays] for const in (psf_const, block_const, lag_const, own_const)
    )

    def gradient_at(*refs):
        held = len(block_arrays)
        end = held + len(lag_arrays)
        return {**block_const.at(*refs[:held]), **lag_const.at(*refs[held:end]), **own_const.at(*refs[end:])}

    in_hbm = [
        pltpu.with_memory_space_constraint(value, pltpu.HBM)
        for value in (phase, amplitude, picture, measured, *psf_arrays)
    ]
    (chip_rows,) = call(
        near_kernel, [(planes, HALF, cols)], in_hbm[2:3], scratch=[pltpu.SemaphoreType.DMA(())], spaces={0: pltpu.HBM}
    )
    from_chip = to_next_chip(chip_rows)
    pupil, field, spec, far_chip, far_core, early_rows, late_rows, *psf_arrays = call(
        functools.partial(first_kernel, at=psf_const.at, places=psf_const.places, arrays=len(psf_arrays)),
        [(pup, 2 * pup), (2 * pad_rows, pad_cols), (length // 2, 2 * cols)]
        + [(2 * planes, HALF, cols)] * 2
        + [(planes // 2, HALF, cols), (planes - planes // 2, HALF, cols)]
        + psf_arrays,
        (*in_hbm, chip_rows),
        flops=3 * 10**9,
        spaces={**dict.fromkeys(range(len(in_hbm)), pltpu.HBM), len(in_hbm): pl.ANY},
        scratch=[pltpu.VMEM(value.shape, jnp.float32) for value in (phase, amplitude)]
        + [pltpu.SemaphoreType.DMA((8 + len(psf_arrays),))],
    )
    early_core, late_core, far_core = (exchange(value, 1) for value in (early_rows, late_rows, far_core))
    known, means = call(
        functools.partial(known_kernel, at=own_const.at),
        [(planes, length, cols), (planes, 8, 128)],
        (picture, *own_arrays),
        flops=10**3,
    )
    far_chip, known = lax.optimization_barrier((far_chip, known))
    far_chip = to_next_chip(far_chip)
    keep, give = call(
        functools.partial(gradient_kernel, at=gradient_at),
        [(pup // 2, pup)] * 2,
        (
            from_chip, early_core, late_core, known, measured, spec, pupil, field, means, *block_arrays, *lag_arrays,
            *own_arrays,
        ),
        flops=4 * 10**10,
    )
    half = keep + exchange(give, 1)
    bits = list(range(2, count.bit_length() - 1))
    for low, high in zip(bits[::2], bits[1::2]):
        half = half + ((exchange(half, 1 << low) + exchange(half, 1 << high)) + exchange(half, (1 << low) | (1 << high)))
    if len(bits) % 2:
        half = half + exchange(half, 1 << bits[-1])
    last_round = [exchange(half, 2)]
    two_strata = lax.axis_size("depth") == 2
    if two_strata:
        last_round += [lax.ppermute(half, "depth", [(0, 1), (1, 0)]), across_depth_and_chip(half)]
    even, odd = call(
        functools.partial(blocks_kernel, at=block_const.at),
        [(planes * length, cols)] * 2,
        (from_chip, early_core, late_core, picture, far_chip, far_core, half, *block_arrays),
        spaces={6: pl.ANY},
    )
    even, *last_round = lax.optimization_barrier((even, *last_round))
    (joined,) = call(squares_kernel, [(pup // 2 + 8, pup)], (half, *last_round))
    other = exchange(joined, 1)
    squares = []
    if not two_strata:
        squares = [sum_over_depth(joined[pup // 2 :] + other[pup // 2 :])]
    new_objects, new_phase = call(
        functools.partial(
            second_kernel,
            at=block_const.at,
            psf_at=psf_const.at,
            arrays=len(block_arrays),
            cells=lax.axis_size("depth") * pup * pup,
            squares_apart=bool(squares),
        ),
        [picture.shape, phase.shape],
        (
            phase, amplitude, joined, other, *squares, even, odd, picture, measured,
            far_chip, far_core, *block_arrays, *psf_arrays,
        ),
        scratch=[pltpu.VMEM(value.shape, jnp.float32) for value in (picture, phase)]
        + [pltpu.SemaphoreType.DMA((planes + 1,))],
        out_space=pltpu.HBM,
    )
    return new_objects[None], new_phase[None]


def solution(mesh):
    return jax.shard_map(
        on_device,
        mesh=mesh,
        in_specs=(
            P("depth", None, "tile", None),
            P("depth", None, "tile", None),
            P("depth", None, None),
            P("depth", None, None),
        ),
        out_specs=(P("depth", None, "tile", None), P("depth", None, None)),
        check_vma=False,
    )
```
